32 devices in a mesh: dp: 4 (over z), seq: 8 (over y, x, core).
Axes of the slice: x: 2, y: 2, z: 4, core: 2. Of those that a mesh axis runs over, the one named last changes fastest.
Arguments:
- tokens: bfloat16 [4, 8192, 768], P('dp', 'seq'), may hold values from -6 to 6
- cotangent: bfloat16 [4, 8192, 768], P('dp', 'seq'), may hold values from -6 to 6
- first_gain: float32 [768], replicated, may hold values from 0.25 to 1.75
- first_shift: float32 [768], replicated, may hold values from -1.75 to 1.75
- joint_weight: bfloat16 [768, 2304], replicated, may hold values from -0.21875 to 0.21875
- query_bias: float32 [768], replicated, may hold values from -3 to 3
- value_bias: float32 [768], replicated, may hold values from -3 to 3
- score_weight: bfloat16 [768, 12], replicated, may hold values from -0.3125 to 0.3125
- out_weight: bfloat16 [768, 768], replicated, may hold values from -1.75 to 1.75
- out_bias: float32 [768], replicated, may hold values from -3 to 3
- second_gain: float32 [768], replicated, may hold values from 0.25 to 1.75
- second_shift: float32 [768], replicated, may hold values from -1.75 to 1.75
- expand_weight: bfloat16 [768, 3072], replicated, may hold values from -0.21875 to 0.21875
- expand_bias: float32 [3072], replicated, may hold values from -3 to 3
- reduce_weight: bfloat16 [3072, 768], replicated, may hold values from -0.109375 to 0.109375
- reduce_bias: float32 [768], replicated, may hold values from -3 to 3
- picks: int32 [4, 8, 8, 8], P('dp', 'seq'), may hold values from 0 to 1023
- quota: int32 [4, 8, 8], P('dp', 'seq'), may hold values from 0 to 8, as said below
Outputs:
- layer_out: bfloat16 [4, 8192, 768], P('dp', 'seq')
- token_grad: float32 [4, 8192, 768], P('dp', 'seq')
- first_gain_grad: float32 [768], replicated
- first_shift_grad: float32 [768], replicated
- joint_weight_grad: float32 [768, 2304], replicated
- query_bias_grad: float32 [768], replicated
- value_bias_grad: float32 [768], replicated
- score_weight_grad: float32 [768, 12], replicated
- out_weight_grad: float32 [768, 768], replicated
- out_bias_grad: float32 [768], replicated
- second_gain_grad: float32 [768], replicated
- second_shift_grad: float32 [768], replicated
- expand_weight_grad: float32 [768, 3072], replicated
- expand_bias_grad: float32 [3072], replicated
- reduce_weight_grad: float32 [3072, 768], replicated
- reduce_bias_grad: float32 [768], replicated
The draws below stay inside these ranges and needn't reach their ends.
Inputs may be any that keep to these rules, and one draw needn't show every extreme that they name: quota[s, d] is zero where s > d; the last query block takes 8 keys from every block. `picks`: only entries with c < quota[s, d] are read.
All inputs are finite; a program needn't handle non-finite values.
Results may differ from the reference program's by a relative error of at most 0.011.
Values may be sent and summed in bfloat16 or wider, within the bound.
No kernel may reach another device: no remote copies, remote signals or barrier semaphores. Data moves between devices by JAX's collectives and lax.ppermute only.
A program may use at most 192 MiB of HBM per device.

```python
import math
import jax
import jax.numpy as jnp
from jax import lax

D = 768
H = 12
HD = 64
FF = 3072
BLOCK = 1024
WIN = 64
PICK = 8
NBLK = 8
LEN = 8192
SEQS = 4


def draw_quota(key, part):
    source = jnp.arange(NBLK, dtype=jnp.int32)[:, None]
    target = jnp.arange(NBLK, dtype=jnp.int32)[None, :]
    lowered = jax.random.randint(key, (SEQS, NBLK, NBLK), 0, PICK // 4 + 1, dtype=jnp.int32)
    filled = jnp.where(target == NBLK - 1, PICK, PICK - lowered)
    return jnp.where(source <= target, filled, 0).astype(jnp.int32)


def place_ends(values, own_key, smallest, high):
    spot = [jax.random.randint(jax.random.fold_in(own_key, axis), (), 0, length) for axis, length in enumerate(values.shape)]
    widest = values.shape.index(max(values.shape))
    neighbour = spot[:widest] + [(spot[widest] + 1) % values.shape[widest]] + spot[widest + 1:]
    return values.at[tuple(spot)].set(smallest).at[tuple(neighbour)].set(high)


def level_of(key, extent, split, smallest, largest):
    level = 1.0
    for position, shards_of in split:
        heights = jax.random.uniform(jax.random.fold_in(jax.random.fold_in(key, 6), position), (shards_of,), jnp.float32, smallest / len(split), largest / len(split))
        level = level * jnp.repeat(jnp.exp(heights), extent[position] // shards_of).reshape((-1,) + (1,) * (len(extent) - 1 - position))
    return level


def scatter_about(stream_key, extent, scale, reach, pieces=(), kind=jnp.bfloat16):
    level = level_of(stream_key, extent, pieces, -0.22, 0.18) if pieces else 1.0
    values = jax.random.normal(stream_key, extent, jnp.float32) * scale * level
    return jnp.minimum(jnp.maximum(values, -reach), reach).astype(kind)


def setup_inputs(seed: int = 0) -> dict:
    streams_of = jax.random.split(jax.random.key(seed), 19)
    tokens = scatter_about(streams_of[0], (SEQS, LEN, D), 1.0, 6.0, ((0, 4), (1, 8)))
    cotangent = scatter_about(streams_of[1], (SEQS, LEN, D), 1.0, 6.0, ((0, 4), (1, 8)))
    first_gain = jnp.clip(1.0 + 0.15 * jax.random.normal(streams_of[2], (D,), jnp.float32), 0.25, 1.75)
    first_shift = scatter_about(streams_of[3], (D,), 0.3, 1.75, (), jnp.float32)
    joint_weight = scatter_about(streams_of[4], (D, 3 * D), D ** -0.5, 0.21875)
    query_bias = scatter_about(streams_of[5], (D,), 0.5, 3.0, (), jnp.float32)
    value_bias = scatter_about(streams_of[6], (D,), 0.5, 3.0, (), jnp.float32)
    score_weight = scatter_about(streams_of[7], (D, H), (D // 2) ** -0.5, 0.3125)
    out_weight = scatter_about(streams_of[8], (D, D), (D // 64) ** -0.5, 1.75)
    out_bias = scatter_about(streams_of[9], (D,), 0.5, 3.0, (), jnp.float32)
    second_gain = jnp.clip(1.0 + 0.15 * jax.random.normal(streams_of[10], (D,), jnp.float32), 0.25, 1.75)
    second_shift = scatter_about(streams_of[11], (D,), 0.3, 1.75, (), jnp.float32)
    expand_weight = scatter_about(streams_of[12], (D, FF), D ** -0.5, 0.21875)
    expand_bias = scatter_about(streams_of[13], (FF,), 0.5, 3.0, (), jnp.float32)
    reduce_weight = scatter_about(streams_of[14], (FF, D), FF ** -0.5, 0.109375)
    reduce_bias = scatter_about(streams_of[15], (D,), 0.5, 3.0, (), jnp.float32)
    picks = place_ends(jax.random.randint(streams_of[16], (SEQS, NBLK, NBLK, PICK), 0, BLOCK), jax.random.fold_in(streams_of[16], 1), 0, BLOCK - 1).astype(jnp.int32)
    quota = draw_quota(jax.random.fold_in(streams_of[18], 71), 0)
    return dict(tokens=tokens, cotangent=cotangent, first_gain=first_gain, first_shift=first_shift, joint_weight=joint_weight, query_bias=query_bias, value_bias=value_bias, score_weight=score_weight, out_weight=out_weight, out_bias=out_bias, second_gain=second_gain, second_shift=second_shift, expand_weight=expand_weight, expand_bias=expand_bias, reduce_weight=reduce_weight, reduce_bias=reduce_bias, picks=picks, quota=quota)


@jax.custom_vjp
def low(v):
    return lax.optimization_barrier(v.astype(jnp.bfloat16)).astype(jnp.float32)

@jax.custom_vjp
def low_back(v):
    return v

def low_keep(v):
    return (low(v), None)

def low_pass(kept, grad):
    return (grad,)

def back_keep(v):
    return (v, None)

def back_low(kept, grad):
    return (low(grad),)
low.defvjp(low_keep, low_pass)
low_back.defvjp(back_keep, back_low)
highest = lax.Precision.HIGHEST
epsilon = 1e-05
very_low = -1e+30

def matmul(left, right):
    return jnp.dot(left, right, precision=highest)

def layer_norm(values, gain, shift):
    average = lax.optimization_barrier(jnp.mean(values, axis=-1, keepdims=True))
    centred = values - average
    variance = lax.optimization_barrier(jnp.mean(centred * centred, axis=-1, keepdims=True))
    return centred * lax.rsqrt(variance + epsilon) * gain + shift

def gelu_tanh(values):
    return 0.5 * values * (1.0 + jnp.tanh(0.7978845608028654 * (values + 0.044715 * values * values * values)))

def rim_copy(blocked):
    leading = jnp.zeros((1, WIN, blocked.shape[2]), blocked.dtype)
    return low_back(jnp.concatenate([leading, blocked[:-1, BLOCK - WIN:]], axis=0))

def attend_block(inputs):
    query_block, key_ext, value_ext, score_ext, ext_pos, key_far, value_far, score_far, far_pos, query_pos = inputs
    scale = 1.0 / math.sqrt(HD)
    query_heads = query_block.reshape(BLOCK, H, HD)
    near_raw = low_back(jnp.einsum('qhd,khd->hqk', query_heads, key_ext.reshape(-1, H, HD), precision=highest))
    far_raw = low_back(jnp.einsum('qhd,khd->hqk', query_heads, key_far.reshape(-1, H, HD), precision=highest))
    near_logit = near_raw * scale + jnp.transpose(jax.nn.log_sigmoid(score_ext))[:, None, :]
    far_logit = far_raw * scale + jnp.transpose(jax.nn.log_sigmoid(score_far))[:, None, :]
    near_mask = (ext_pos[None, :] <= query_pos[:, None]) & (ext_pos[None, :] > query_pos[:, None] - WIN) & (ext_pos[None, :] >= 0)
    far_mask = far_pos[None, :] <= query_pos[:, None] - WIN
    near_logit = jnp.where(near_mask[None], near_logit, very_low)
    far_logit = jnp.where(far_mask[None], far_logit, very_low)
    top = jnp.maximum(lax.optimization_barrier(jnp.max(near_logit, axis=-1)), lax.optimization_barrier(jnp.max(far_logit, axis=-1)))
    total = lax.optimization_barrier(jnp.sum(jnp.exp(near_logit - top[..., None]), axis=-1)) + lax.optimization_barrier(jnp.sum(jnp.exp(far_logit - top[..., None]), axis=-1))
    log_total = top + jnp.log(total)
    near_prob = low(jnp.exp(near_logit - log_total[..., None]))
    far_prob = low(jnp.exp(far_logit - log_total[..., None]))
    mixed = jnp.einsum('hqk,khd->qhd', near_prob, value_ext.reshape(-1, H, HD), precision=highest)
    mixed = mixed + jnp.einsum('hqk,khd->qhd', far_prob, value_far.reshape(-1, H, HD), precision=highest)
    return mixed.reshape(BLOCK, D)

def forward(tokens, params, picks, quota):
    first_gain, first_shift, joint_weight, query_bias, value_bias, score_weight, out_weight, out_bias, second_gain, second_shift, expand_weight, expand_bias, reduce_weight, reduce_bias = params
    normed = low(layer_norm(tokens, first_gain, first_shift))
    joint = matmul(normed, joint_weight)
    query = low_back(low(joint[:, :D] + query_bias))
    keys = low_back(low(joint[:, D:2 * D]))
    values = low_back(low(joint[:, 2 * D:] + value_bias))
    score = low_back(low(matmul(normed, score_weight)))
    key_blocks = keys.reshape(NBLK, BLOCK, D)
    value_blocks = values.reshape(NBLK, BLOCK, D)
    score_blocks = score.reshape(NBLK, BLOCK, H)
    key_ext = jnp.concatenate([rim_copy(key_blocks), key_blocks], axis=1)
    value_ext = jnp.concatenate([rim_copy(value_blocks), value_blocks], axis=1)
    score_ext = jnp.concatenate([rim_copy(score_blocks), score_blocks], axis=1)
    block_ids = jnp.arange(NBLK, dtype=jnp.int32)
    ext_pos = block_ids[:, None] * BLOCK - WIN + jnp.arange(WIN + BLOCK, dtype=jnp.int32)[None, :]
    query_pos = block_ids[:, None] * BLOCK + jnp.arange(BLOCK, dtype=jnp.int32)[None, :]
    source_rows = (block_ids[:, None, None] * BLOCK + picks).astype(jnp.int32)
    live = jnp.arange(PICK, dtype=jnp.int32)[None, None, :] < quota[:, :, None]
    far_rows = jnp.transpose(source_rows, (1, 0, 2)).reshape(NBLK, NBLK * PICK)
    far_pos = jnp.transpose(jnp.where(live, source_rows, 2 * LEN), (1, 0, 2)).reshape(NBLK, NBLK * PICK).astype(jnp.int32)
    key_far = low_back(keys[far_rows])
    value_far = low_back(values[far_rows])
    score_far = low_back(score[far_rows])
    mixed = lax.map(jax.checkpoint(attend_block), (query.reshape(NBLK, BLOCK, D), key_ext, value_ext, score_ext, ext_pos, key_far, value_far, score_far, far_pos, query_pos))
    mixed = low_back(low(mixed.reshape(LEN, D)))
    attn = matmul(mixed, out_weight) + out_bias
    resid = tokens + low_back(attn)
    normed_two = low(layer_norm(resid, second_gain, second_shift))
    pre = low_back(matmul(normed_two, expand_weight) + expand_bias)
    hidden = low(gelu_tanh(pre))
    return resid + matmul(hidden, reduce_weight) + reduce_bias

def reference(tokens, cotangent, first_gain, first_shift, joint_weight, query_bias, value_bias, score_weight, out_weight, out_bias, second_gain, second_shift, expand_weight, expand_bias, reduce_weight, reduce_bias, picks, quota):
    params = tuple((array.astype(jnp.float32) for array in (first_gain, first_shift, joint_weight, query_bias, value_bias, score_weight, out_weight, out_bias, second_gain, second_shift, expand_weight, expand_bias, reduce_weight, reduce_bias)))

    def one_sequence(totals, inputs):
        seq_tokens, seq_cotangent, seq_picks, seq_quota = inputs

        def apply(token_rows, weights):
            return forward(token_rows, weights, seq_picks, seq_quota)
        result, pullback = jax.vjp(apply, seq_tokens.astype(jnp.float32), params)
        token_part, weight_parts = pullback(seq_cotangent.astype(jnp.float32))
        totals = jax.tree.map(lambda left, right: left + right, totals, weight_parts)
        return (totals, (result.astype(jnp.bfloat16), token_part))
    zeros = jax.tree.map(jnp.zeros_like, params)
    totals, (outputs, token_grads) = lax.scan(one_sequence, zeros, (tokens, cotangent, picks, quota))
    return (outputs, token_grads, totals[0], totals[1], totals[2], totals[3], totals[4], totals[5], totals[6], totals[7], totals[8], totals[9], totals[10], totals[11], totals[12], totals[13])
```

```python
import functools
import math

import jax
import jax.numpy as jnp
from jax import lax
from jax.experimental import pallas as pl
from jax.experimental.pallas import tpu as pltpu
from jax.sharding import PartitionSpec as P

WIN = 64
PICK = 8
LANES = 128
PACK = 4
DIGIT = 32
TOKEN = (8, 128)
epsilon = 1e-05
very_low = -1e30
bf16 = jnp.bfloat16
f32 = jnp.float32


def nt(left, right):
    return lax.dot_general(left, right, (((1,), (1,)), ((), ())), preferred_element_type=f32)


def tn(left, right):
    return lax.dot_general(left, right, (((0,), (0,)), ((), ())), preferred_element_type=f32)


def nn(left, right):
    return jnp.dot(left, right, preferred_element_type=f32)


def three_parts(value):
    high = value.astype(bf16)
    rest = value - high.astype(f32)
    middle = rest.astype(bf16)
    low = (rest - middle.astype(f32)).astype(bf16)
    return high, middle, low


def head_spread(group, head_size, width):
    row = lax.broadcasted_iota(jnp.int32, (LANES, width), 0)
    lane = lax.broadcasted_iota(jnp.int32, (LANES, width), 1)
    return jnp.where(row == group * PACK + lane // WIN, 1.0, 0.0).astype(bf16)


def stack_heads(tile, head_size, factor):
    width = tile.shape[1]
    lane = lax.broadcasted_iota(jnp.int32, tile.shape, 1) // head_size
    scaled = tile * jnp.asarray(factor, tile.dtype)
    zero = jnp.zeros_like(scaled)
    return jnp.concatenate([jnp.where(lane == h, scaled, zero) for h in range(PACK)], axis=0)


def pick_heads(full, head_size):
    lane = lax.broadcasted_iota(jnp.int32, (WIN, full.shape[1]), 1) // head_size
    out = full[0:WIN]
    for h in range(1, PACK):
        out = jnp.where(lane == h, full[h * WIN : (h + 1) * WIN], out)
    return out


def gates_into(gate_ref, group, place, score_ref, rim_score_ref, far_score_ref, head_size, rows, slots):
    width = PACK * WIN
    spread = head_spread(group, head_size, width)

    def expand(score):
        gate = jax.nn.log_sigmoid(score.astype(f32))
        return sum(nn(part, spread) for part in three_parts(gate))

    gate_ref[0:WIN, :] = jnp.where(place == 0, very_low, expand(rim_score_ref[...]))
    gate_ref[WIN : WIN + rows, :] = expand(score_ref[...])
    gate_ref[WIN + rows :, :] = expand(far_score_ref[...])


def near_bias(width):
    key = lax.broadcasted_iota(jnp.int32, (2 * WIN, width), 0)
    query = lax.broadcasted_iota(jnp.int32, (2 * WIN, width), 1) % WIN
    return (key <= query + WIN) & (key > query)


def tile_logits(i, keys_cat, query_stack, gate_ref, far_pos, place, rows, near_ok):
    width = PACK * WIN
    raw = nt(keys_cat, query_stack)
    gate_near = gate_ref[pl.ds(pl.multiple_of(i * WIN, WIN), 2 * WIN), :]
    gate_far = gate_ref[WIN + rows :, :]
    slots = gate_far.shape[0]
    near = jnp.where(near_ok, raw[: 2 * WIN] + gate_near, very_low)
    lane = lax.broadcasted_iota(jnp.int32, (slots, LANES), 1) % WIN
    far_ok = far_pos <= lane + (place * rows + i * WIN - WIN)
    far_raw = raw[2 * WIN :] + gate_far
    far = jnp.concatenate(
        [
            jnp.where(far_ok, far_raw[:, c * LANES : (c + 1) * LANES], very_low)
            for c in range(width // LANES)
        ],
        axis=1,
    )
    return jnp.concatenate([near, far], axis=0)


def launch(kernel, name, work, grid, in_specs, out_specs, out_shape, scratch, limit, operands, after=(), prefetch=(),
           free=()):
    count, extra = len(operands), len(after)

    def body(*refs):
        lead = len(prefetch)
        rest = refs[lead + count + extra :]
        rest[len(shapes)][...] = jnp.zeros(TOKEN, f32)
        kernel(*refs[: lead + count], *rest[: len(shapes)], *rest[len(shapes) + 1 :])

    def place(at, value, spec):
        if spec.memory_space == pltpu.SMEM or at in free:
            return value
        return pltpu.with_memory_space_constraint(value, pltpu.HBM)

    operands = [place(at, value, spec) for at, (value, spec) in enumerate(zip(operands, in_specs))]
    after = [pltpu.with_memory_space_constraint(value, pltpu.HBM) for value in after]
    shapes, kept = out_shape, len(free) > 0 and name == "advance"
    out = pl.pallas_call(
        body,
        grid_spec=pltpu.PrefetchScalarGridSpec(
            num_scalar_prefetch=len(prefetch),
            grid=grid,
            in_specs=list(in_specs) + [pl.BlockSpec(memory_space=pl.ANY)] * extra,
            out_specs=list(out_specs) + [same(*TOKEN)],
            scratch_shapes=scratch,
        ),
        out_shape=[shape if kept else pltpu.HBM(shape.shape, shape.dtype) for shape in shapes] + [pltpu.HBM(TOKEN, f32)],
        compiler_params=pltpu.CompilerParams(vmem_limit_bytes=limit * 2**20),
        cost_estimate=pl.CostEstimate(flops=int(work * 1.15e9), bytes_accessed=2**20, transcendentals=0),
        name=name,
    )(*prefetch, *operands, *after)
    return list(out)


def passed_along(value, axis, steps):
    count = lax.axis_size(axis)
    leading, last = (max(0, -steps), min(count, count - steps))
    return lax.ppermute(value, axis, [(source, source + steps) for source in range(leading, last)])


def normalise(values):
    average = jnp.mean(values, axis=-1, keepdims=True)
    centred = values - average
    variance = jnp.mean(centred * centred, axis=-1, keepdims=True)
    inverse = lax.rsqrt(variance + epsilon)
    return (centred * inverse, inverse)


def normalise_back(grad_out, unit, inverse, gain):
    grad_unit = grad_out * gain
    mean_grad = jnp.mean(grad_unit, axis=-1, keepdims=True)
    mean_cross = jnp.mean(grad_unit * unit, axis=-1, keepdims=True)
    return (grad_unit - mean_grad - unit * mean_cross) * inverse


def row(ref):
    return ref[...].reshape(1, -1)


def column_sums(values):
    return jnp.sum(values, axis=0, keepdims=True)


def accumulate(ref, update):
    step = pl.program_id(0)

    @pl.when(step == 0)
    def _():
        ref[...] = update

    @pl.when(step > 0)
    def _():
        ref[...] += update


def project_kernel(
    steps, tokens_ref, picks_ref, live_ref, gain_ref, shift_ref, joint_ref, query_bias_ref, value_bias_ref,
    score_weight_ref, normed_ref, q_ref, k_ref, v_ref, score_ref, rim_ref, sent_ref, gathered,
):
    step = pl.program_id(0)
    tile, width = tokens_ref.shape
    unit, _ = normalise(tokens_ref[...].astype(f32))
    normed = (unit * row(gain_ref) + row(shift_ref)).astype(bf16)
    normed_ref[...] = normed
    q_ref[...] = (nn(normed, joint_ref[:, :width]) + row(query_bias_ref)).astype(bf16)
    keys = nn(normed, joint_ref[:, width : 2 * width]).astype(bf16)
    values = (nn(normed, joint_ref[:, 2 * width :]) + row(value_bias_ref)).astype(bf16)
    score = nn(normed, score_weight_ref[...]).astype(bf16)
    heads = score.shape[1]
    k_ref[...] = keys
    v_ref[...] = values
    score_ref[...] = jnp.zeros_like(score_ref)
    score_ref[:, :heads] = score
    picks = picks_ref[...]
    slots = picks.shape[0]
    chosen = picks - step * tile == lax.broadcasted_iota(jnp.int32, (slots, tile), 1)
    chosen = jnp.where(chosen, 1.0, 0.0).astype(bf16)
    parts = ((0, keys), (width, values), (2 * width, score_ref[...]))

    @pl.when(step == 0)
    def _():
        gathered[...] = jnp.zeros_like(gathered)

    for start, part in parts:
        gathered[:, start : start + part.shape[1]] += nn(chosen, part)

    @pl.when(step == steps - 1)
    def _():
        for start, part in parts:
            rim_ref[:, start : start + part.shape[1]] = part[tile - WIN :]
        sent_ref[...] = gathered[...].astype(bf16)
        lane = lax.broadcasted_iota(jnp.int32, (slots, LANES), 1)
        coded = jnp.where(lane == heads, picks // DIGIT, jnp.where(lane == heads + 1, picks % DIGIT, live_ref[...]))
        last = gathered[:, 2 * width :]
        sent_ref[:, 2 * width :] = jnp.where(
            (lane >= heads) & (lane < heads + 3), coded.astype(f32), last
        ).astype(bf16)


def same(*shape):
    return pl.BlockSpec(shape, lambda *_: (0,) * len(shape))


def tiled(*shape):
    return pl.BlockSpec(shape, lambda r, *_: (r,) + (0,) * (len(shape) - 1))


def project(tokens, picks, live, gain, shift, joint, query_bias, value_bias, score_weight, tile=256):
    rows, width = tokens.shape
    slots = picks.shape[0]
    channels = 2 * width + LANES
    steps = rows // tile
    S = jax.ShapeDtypeStruct
    return launch(
        functools.partial(project_kernel, steps),
        "project", 8, (steps,),
        [
            tiled(tile, width), same(slots, 1), same(slots, 1), same(width), same(width), same(*joint.shape), same(width),
            same(width), same(*score_weight.shape),
        ],
        [tiled(tile, width)] * 4 + [tiled(tile, LANES), same(WIN, channels), same(slots, channels)],
        [S((rows, width), bf16)] * 4 + [S((rows, LANES), bf16), S((WIN, channels), bf16), S((slots, channels), bf16)],
        [pltpu.VMEM((slots, channels), f32)], 24,
        (tokens, picks, live, gain, shift, joint, query_bias, value_bias, score_weight),
    )


def far_positions(far_score, heads, place_rows, blocks):
    wide = far_score.astype(f32)
    slot = lax.broadcasted_iota(jnp.int32, (far_score.shape[0], 1), 0)
    at = (wide[:, heads : heads + 1] * DIGIT + wide[:, heads + 1 : heads + 2]).astype(jnp.int32)
    return jnp.where(
        wide[:, heads + 2 : heads + 3] > 0.5, (slot // PICK) * place_rows + at, 2 * place_rows * blocks
    )


def load_block(group, place_ref, k_ref, v_ref, score_ref, rim_refs, far_refs, keys, values, gate_ref, head_size):
    rows, width = k_ref.shape
    rim_k_ref, rim_v_ref, rim_score_ref = rim_refs
    far_score_ref = far_refs[2]
    slots = far_score_ref.shape[0]
    keys[0:WIN, :] = rim_k_ref[...]
    keys[WIN:, :] = k_ref[...]
    values[0:WIN, :] = rim_v_ref[...]
    values[WIN:, :] = v_ref[...]
    gates_into(gate_ref, group, place_ref[0], score_ref, rim_score_ref, far_score_ref, head_size, rows, slots)


def attend_kernel(
    heads, head_size, unroll, place_ref, q_ref, k_ref, v_ref, score_ref,
    rim_k_ref, rim_v_ref, rim_score_ref, far_k_ref, far_v_ref, far_score_ref,
    mixed_ref, total_ref, keys, values, gate_ref,
):
    group = pl.program_id(0)
    place = place_ref[0]
    rows, width = q_ref.shape
    slots = far_k_ref.shape[0]
    load_block(
        group, place_ref, k_ref, v_ref, score_ref, (rim_k_ref, rim_v_ref, rim_score_ref),
        (far_k_ref, far_v_ref, far_score_ref), keys, values, gate_ref, head_size,
    )
    near_ok = near_bias(width)
    far_pos = jnp.broadcast_to(far_positions(far_score_ref[...], heads, rows, slots // PICK), (slots, LANES))

    @pl.loop(0, rows // WIN, unroll=unroll)
    def _(i):
        at = pl.ds(pl.multiple_of(i * WIN, WIN), WIN)
        span = pl.ds(pl.multiple_of(i * WIN, WIN), 2 * WIN)
        keys_cat = jnp.concatenate([keys[span, :], far_k_ref[...]], axis=0)
        values_cat = jnp.concatenate([values[span, :], far_v_ref[...]], axis=0)
        stack = stack_heads(q_ref[at, :], head_size, 1.0 / math.sqrt(head_size))
        logit = tile_logits(i, keys_cat, stack, gate_ref, far_pos, place, rows, near_ok)
        top = jnp.max(logit, axis=0, keepdims=True)
        power = jnp.exp(logit - top)
        total = jnp.sum(power, axis=0, keepdims=True)
        prob = (power * (1.0 / total)).astype(bf16)
        total_ref[0, pl.ds(i, 1), :] = top + jnp.log(total)
        mixed_ref[at, :] = pick_heads(tn(prob, values_cat), head_size).astype(bf16)


def far_specs(slots, width, groups, offset=0):
    return [
        pl.BlockSpec((slots, width), lambda g: (0, g + offset)),
        pl.BlockSpec((slots, width), lambda g: (0, groups + g + offset)),
        pl.BlockSpec((slots, LANES), lambda g: (0, 2 * groups * width // LANES)),
    ]


def attend(place, q, k, v, score, rim, far, heads, unroll=8):
    rows, model = q.shape
    slots = far.shape[0]
    width = PACK * WIN
    groups = model // width
    cols = pl.BlockSpec((rows, width), lambda g: (0, g))
    return launch(
        functools.partial(attend_kernel, heads, WIN, unroll),
        "attend", 12, (groups,),
        [pl.BlockSpec(memory_space=pltpu.SMEM), cols, cols, cols, pl.BlockSpec((rows, LANES), lambda g: (0, 0))]
        + far_specs(WIN, width, groups) + far_specs(slots, width, groups),
        [cols, pl.BlockSpec((1, rows // WIN, width), lambda g: (g, 0, 0))],
        [
            jax.ShapeDtypeStruct((rows, model), bf16),
            jax.ShapeDtypeStruct((groups, rows // WIN, width), f32),
        ],
        [
            pltpu.VMEM((WIN + rows, width), bf16),
            pltpu.VMEM((WIN + rows, width), bf16),
            pltpu.VMEM((WIN + rows + slots, width), f32),
        ],
        32, (place, q, k, v, score, rim, rim, rim, far, far, far),
    )


def attend_back_kernel(
    heads, head_size, unroll, place_ref, q_ref, k_ref, v_ref, grad_ref, total_ref, score_ref,
    rim_k_ref, rim_v_ref, rim_score_ref, far_k_ref, far_v_ref, far_score_ref,
    dq_ref, dk_ref, dv_ref, ds_ref, rim_out, far_out,
    keys, values, gate_ref, dkeys, dvalues, dscore, rim_ds, far_ds,
):
    group = pl.program_id(0)
    model = (rim_out.shape[1] - LANES) // 2
    place = place_ref[0]
    rows, width = q_ref.shape
    slots = far_k_ref.shape[0]
    load_block(
        group, place_ref, k_ref, v_ref, score_ref, (rim_k_ref, rim_v_ref, rim_score_ref),
        (far_k_ref, far_v_ref, far_score_ref), keys, values, gate_ref, head_size,
    )
    near_ok = near_bias(width)
    far_pos = jnp.broadcast_to(far_positions(far_score_ref[...], heads, rows, slots // PICK), (slots, LANES))
    for ref in (dkeys, dvalues, dscore):
        ref[...] = jnp.zeros_like(ref)

    @pl.loop(0, rows // WIN, unroll=unroll)
    def _(i):
        at = pl.ds(pl.multiple_of(i * WIN, WIN), WIN)
        span = pl.ds(pl.multiple_of(i * WIN, WIN), 2 * WIN)
        keys_cat = jnp.concatenate([keys[span, :], far_k_ref[...]], axis=0)
        values_cat = jnp.concatenate([values[span, :], far_v_ref[...]], axis=0)
        stack = stack_heads(q_ref[at, :], head_size, 1.0 / math.sqrt(head_size))
        grad_stack = stack_heads(grad_ref[at, :], head_size, 1.0)
        logit = tile_logits(i, keys_cat, stack, gate_ref, far_pos, place, rows, near_ok)
        prob = jnp.exp(logit - total_ref[0, pl.ds(i, 1), :])
        grad_prob = nt(values_cat, grad_stack)
        delta = jnp.sum(prob * grad_prob, axis=0, keepdims=True)
        grad_logit = prob * (grad_prob - delta)
        low = grad_logit.astype(bf16)
        dq_ref[at, :] = (pick_heads(tn(low, keys_cat), head_size) * (1.0 / math.sqrt(head_size))).astype(bf16)
        for ref, update in (
            (dkeys, nn(low, stack)),
            (dvalues, nn(prob.astype(bf16), grad_stack)),
            (dscore, grad_logit),
        ):
            ref[span, :] += update[: 2 * WIN]
            ref[WIN + rows :, :] += update[2 * WIN :]

    dk_ref[...] = dkeys[WIN : WIN + rows, :]
    dv_ref[...] = dvalues[WIN : WIN + rows, :]
    for out, start, count in ((rim_out, 0, WIN), (far_out, WIN + rows, slots)):
        for base, ref in ((0, dkeys), (model, dvalues)):
            at = pl.ds(pl.multiple_of(base + group * width, LANES), width)
            out[:, at] = ref[start : start + count, :].astype(bf16)
    gather = head_spread(group, head_size, width)
    for out_ref, score, start, count in (
        (rim_ds, rim_score_ref, 0, WIN),
        (ds_ref, score_ref, WIN, rows),
        (far_ds, far_score_ref, WIN + rows, slots),
    ):
        sums = dscore[start : start + count, :]
        high = sums.astype(bf16)
        rest = (sums - high.astype(f32)).astype(bf16)
        update = (nt(high, gather) + nt(rest, gather)) * jax.nn.sigmoid(-score[...].astype(f32))
        accumulate(out_ref, update)
    rim_out[:, 2 * model :] = rim_ds[...].astype(bf16)
    far_out[:, 2 * model :] = far_ds[...].astype(bf16)


def attend_back(place, q, k, v, grad, total, score, rim, far, heads, after=(), unroll=4):
    rows, model = q.shape
    slots, channels = far.shape
    width = PACK * WIN
    groups = model // width
    cols = pl.BlockSpec((rows, width), lambda g: (0, g))
    S = jax.ShapeDtypeStruct
    return launch(
        functools.partial(attend_back_kernel, heads, WIN, unroll),
        "attend_back", 28, (groups,),
        [
            pl.BlockSpec(memory_space=pltpu.SMEM),
            cols, cols, cols, cols,
            pl.BlockSpec((1, rows // WIN, width), lambda g: (g, 0, 0)),
            same(rows, LANES),
        ] + far_specs(WIN, width, groups) + far_specs(slots, width, groups),
        [cols, cols, cols, same(rows, LANES), same(WIN, channels), same(slots, channels)],
        [
            S((rows, model), bf16), S((rows, model), f32), S((rows, model), f32), S((rows, LANES), f32),
            S((WIN, channels), bf16), S((slots, channels), bf16),
        ],
        [
            pltpu.VMEM((WIN + rows, width), bf16),
            pltpu.VMEM((WIN + rows, width), bf16),
        ] + [pltpu.VMEM((WIN + rows + slots, width), f32)] * 4
        + [pltpu.VMEM((WIN, LANES), f32), pltpu.VMEM((slots, LANES), f32)],
        44, (place, q, k, v, grad, total, score, rim, rim, rim, far, far, far), after,
    )


cubic = 0.044715
root = 0.7978845608028654


def feed_kernel(
    tile, pieces, blocks_one, blocks_two, mine_ref, mixed_ref, tokens_ref, cot_ref, out_weight_ref, out_bias_ref, gain_ref,
    shift_ref, expand_bias_ref, expand_hbm, reduce_hbm,
    resid_ref, hidden_ref, grad_pre_ref, sums_ref, send_one, keep_one, send_two, keep_two,
    expand, reduce, normed, hidden, grad_pre, arrived,
):
    step = pl.program_id(0)
    rows, width = cot_ref.shape
    inner = expand.shape[1]
    span = inner // pieces
    steps = rows // tile
    mine = mine_ref[0]

    def fetches():
        result = []
        for piece in range(pieces):
            at = pl.ds(piece * span, span)
            result.append(pltpu.make_async_copy(expand_hbm.at[:, at], expand.at[:, at], arrived.at[2 * piece]))
            result.append(pltpu.make_async_copy(reduce_hbm.at[at, :], reduce.at[at, :], arrived.at[2 * piece + 1]))
        return result

    @pl.when(step == 0)
    def _():
        for fetch in fetches():
            fetch.start()

    def feed_tile(first):
        here = pl.ds(pl.multiple_of(step * tile, tile), tile)
        cot = cot_ref[here, :]
        resid = tokens_ref[...].astype(f32) + nn(mixed_ref[...], out_weight_ref[...]) + row(out_bias_ref)
        resid_ref[...] = resid
        unit, _ = normalise(resid)
        low = (unit * row(gain_ref) + row(shift_ref)).astype(bf16)
        normed[here, :] = low
        sums = []
        for piece in range(pieces):
            at = slice(piece * span, (piece + 1) * span)
            if first:
                for fetch in fetches()[2 * piece : 2 * piece + 2]:
                    fetch.wait()
            pre = nn(low, expand[:, at]) + row(expand_bias_ref)[:, at]
            back = nt(cot, reduce[at, :])
            squared = pre * pre
            half = 0.5 + 0.5 * jnp.tanh(pre * (root + root * cubic * squared))
            active = pre * half
            slope = half + (active - active * half) * (2.0 * root + 6.0 * root * cubic * squared)
            active = active.astype(bf16)
            hidden[here, at] = active
            hidden_ref[:, at] = active
            grad = (back * slope).astype(bf16)
            grad_pre[here, at] = grad
            grad_pre_ref[:, at] = grad
            sums.append(column_sums(grad.astype(f32)))
        accumulate(sums_ref, jnp.concatenate(sums, axis=1))

    @pl.when(step == 0)
    def _():
        feed_tile(True)

    @pl.when((step > 0) & (step < steps))
    def _():
        feed_tile(False)

    def block(at, half):
        return jnp.where(at < half, at + (1 - mine) * half, at - half + mine * half)

    def outers(start, half, left, right, send, keep):
        size = send.shape[0]
        at = step - start

        @pl.when((at >= 0) & (at < 2 * half))
        def _():
            lanes = pl.ds(pl.multiple_of(block(at, half) * size, LANES), size)
            update = tn(left[:, lanes], right[...]).astype(bf16)

            @pl.when(at < half)
            def _():
                send[...] = update

            @pl.when(at >= half)
            def _():
                keep[...] = update

    outers(steps, blocks_one, hidden, cot_ref, send_one, keep_one)
    outers(steps + 2 * blocks_one, blocks_two, normed, grad_pre, send_two, keep_two)


def feed(
    mine, mixed, tokens, cot, out_weight, out_bias, gain, shift, expand, expand_bias, reduce,
    tile=256, pieces=4, blocks_one=3, blocks_two=1,
):
    rows, width = tokens.shape
    inner = expand.shape[1]
    steps = rows // tile
    size_one, size_two = inner // (2 * blocks_one), width // (2 * blocks_two)
    S = jax.ShapeDtypeStruct

    def early(*shape):
        return pl.BlockSpec(shape, lambda r, *_: (jnp.minimum(r, steps - 1), 0))

    def late(start, count, *shape):
        return pl.BlockSpec(shape, lambda r, *_: (jnp.clip(r - start, 0, count - 1), 0))

    middle = steps + 2 * blocks_one
    return launch(
        functools.partial(feed_kernel, tile, pieces, blocks_one, blocks_two),
        "feed", 28, (middle + 2 * blocks_two,),
        [early(tile, width)] * 2 + [
            same(rows, width), same(width, width), same(width), same(width), same(width), same(inner),
            pl.BlockSpec(memory_space=pl.ANY), pl.BlockSpec(memory_space=pl.ANY),
        ],
        [
            early(tile, width), early(tile, inner), early(tile, inner), same(1, inner),
            late(steps, blocks_one, size_one, width), late(steps + blocks_one, blocks_one, size_one, width),
            late(middle, blocks_two, size_two, inner), late(middle + blocks_two, blocks_two, size_two, inner),
        ],
        [
            S((rows, width), f32), S((rows, inner), bf16), S((rows, inner), bf16), S((1, inner), f32),
            S((inner // 2, width), bf16), S((inner // 2, width), bf16),
            S((width // 2, inner), bf16), S((width // 2, inner), bf16),
        ],
        [
            pltpu.VMEM((width, inner), bf16), pltpu.VMEM((inner, width), bf16), pltpu.VMEM((rows, width), bf16),
            pltpu.VMEM((rows, inner), bf16), pltpu.VMEM((rows, inner), bf16), pltpu.SemaphoreType.DMA((2 * pieces,)),
        ],
        60, (mixed, tokens, cot, out_weight, out_bias, gain, shift, expand_bias, expand, reduce), (), (mine,),
    )


def feed_back_kernel(
    resid_ref, cot_ref, grad_pre_ref, out_weight_ref, gain_ref, expand_ref,
    grad_resid_ref, grad_attn_ref, grad_mixed_ref, sums_ref,
):
    cot = cot_ref[...].astype(f32)
    unit, inverse = normalise(resid_ref[...])
    grad_normed = nt(grad_pre_ref[...], expand_ref[...])
    grad_resid = cot + normalise_back(grad_normed, unit, inverse, row(gain_ref))
    grad_resid_ref[...] = grad_resid
    grad_attn = grad_resid.astype(bf16)
    grad_attn_ref[...] = grad_attn
    grad_mixed_ref[...] = nt(grad_attn, out_weight_ref[...]).astype(bf16)
    accumulate(
        sums_ref,
        jnp.concatenate(
            [
                column_sums(grad_attn.astype(f32)),
                column_sums(grad_normed * unit),
                column_sums(grad_normed),
                column_sums(cot),
            ],
            axis=0,
        ),
    )


def feed_back(resid, cot, grad_pre, out_weight, gain, expand, after=(), tile=256):
    rows, width = resid.shape
    inner = expand.shape[1]
    S = jax.ShapeDtypeStruct
    return launch(
        feed_back_kernel, "feed_back", 11, (rows // tile,),
        [tiled(tile, width)] * 2 + [tiled(tile, inner), same(width, width), same(width), same(width, inner)],
        [tiled(tile, width)] * 3 + [same(4, width)],
        [S((rows, width), f32), S((rows, width), bf16), S((rows, width), bf16), S((4, width), f32)],
        [], 40, (resid, cot, grad_pre, out_weight, gain, expand), after,
    )


def finish_kernel(resid_ref, hidden_ref, reduce_ref, bias_ref, out_ref):
    out_ref[...] = (resid_ref[...] + nn(hidden_ref[...], reduce_ref[...]) + row(bias_ref)).astype(bf16)


def finish(resid, hidden, reduce, bias, after=(), tile=256):
    rows, width = resid.shape
    inner = reduce.shape[0]
    return launch(
        finish_kernel, "finish", 7, (rows // tile,),
        [tiled(tile, width), tiled(tile, inner), same(inner, width), same(width)],
        [tiled(tile, width)], [jax.ShapeDtypeStruct((rows, width), bf16)],
        [], 40, (resid, hidden, reduce, bias), after,
    )


def pair_outer_kernel(mine_ref, a_ref, b_ref, c_ref, *refs):
    d_ref, send_ref, keep_ref = refs
    one = tn(a_ref[...], b_ref[...]).astype(bf16)
    two = tn(c_ref[...], d_ref[...]).astype(bf16)
    mine = mine_ref[0]
    send_ref[...] = jnp.where(mine == 0, two, one)
    keep_ref[...] = jnp.where(mine == 0, one, two)


def pair_outer(mine, a, b, c, d, name, work, after=()):
    rows, m = a.shape
    S = jax.ShapeDtypeStruct
    return launch(
        pair_outer_kernel, name, work, (1,),
        [same(rows, m)] * 4, [same(m, m)] * 2, [S((m, m), bf16)] * 2,
        [], 40, (a, b, c, d), after, (mine,),
    )


def join_keys_kernel(
    tile, mine_ref, dk_ref, dv_ref, ds_ref, rim_ref, far_ref, picks_ref, normed_ref,
    dk_out, dv_out, ds_out, send_ref, keep_ref, both,
):
    step = pl.program_id(0)
    rows, width = normed_ref.shape
    steps = rows // tile
    slots = far_ref.shape[0]
    mine = mine_ref[0]

    @pl.when(step < steps)
    def _():
        chosen = picks_ref[...] - step * tile == lax.broadcasted_iota(jnp.int32, (tile, slots), 0)
        chosen = jnp.where(chosen, 1.0, 0.0).astype(bf16)
        at_end = jnp.where(step == steps - 1, 1.0, 0.0)
        here = pl.ds(pl.multiple_of(step * tile, tile), tile)

        def whole(own, start):
            span = own.shape[1]
            total = own + nn(chosen, far_ref[:, start : start + span])
            rim = rim_ref[:, start : start + span].astype(f32) * at_end
            return jnp.concatenate([total[: tile - WIN], total[tile - WIN :] + rim], axis=0).astype(bf16)

        dk = whole(dk_ref[...], 0)
        dv = whole(dv_ref[...], width)
        dk_out[...] = dk
        dv_out[...] = dv
        ds_out[...] = whole(ds_ref[...], 2 * width)
        both[here, :width] = dk
        both[here, width:] = dv

    half = width // 2
    for turn, ref in ((0, send_ref), (1, keep_ref)):
        @pl.when(step == steps + turn)
        def _():
            at = (1 - mine) if turn == 0 else mine
            ref[...] = tn(normed_ref[:, pl.ds(pl.multiple_of(at * half, LANES), half)], both[...]).astype(bf16)


def join_keys(mine, dk, dv, ds, rim, far, picks, normed, after=(), tile=256):
    rows, width = dk.shape
    slots, channels = far.shape
    S = jax.ShapeDtypeStruct
    steps = rows // tile

    def early(*shape):
        return pl.BlockSpec(shape, lambda r, *_: (jnp.minimum(r, steps - 1), 0))

    return launch(
        functools.partial(join_keys_kernel, tile),
        "join_keys", 8, (steps + 2,),
        [
            early(tile, width), early(tile, width), early(tile, LANES),
            same(WIN, channels), same(slots, channels), same(1, slots), same(rows, width),
        ],
        [early(tile, width), early(tile, width), early(tile, LANES)] + [same(width // 2, 2 * width)] * 2,
        [S((rows, width), bf16), S((rows, width), bf16), S((rows, LANES), bf16)]
        + [S((width // 2, 2 * width), bf16)] * 2,
        [pltpu.VMEM((rows, 2 * width), bf16)], 40, (dk, dv, ds, rim, far, picks, normed), after, (mine,),
    )


def join_tokens_kernel(
    tokens_ref, resid_ref, dq_ref, dk_ref, dv_ref, ds_ref, gain_ref, shift_ref, joint_ref, score_weight_ref,
    token_ref, sums_ref, score_grad_ref,
):
    width = tokens_ref.shape[1]
    heads = score_weight_ref.shape[1]
    unit, inverse = normalise(tokens_ref[...].astype(f32))
    gain = row(gain_ref)
    normed = (unit * gain + row(shift_ref)).astype(bf16)
    dq, dk, dv, ds = dq_ref[...], dk_ref[...], dv_ref[...], ds_ref[...]
    grad_normed = (
        nt(dq, joint_ref[:, :width])
        + nt(dk, joint_ref[:, width : 2 * width])
        + nt(dv, joint_ref[:, 2 * width :])
        + nt(ds[:, :heads], score_weight_ref[...])
    )
    token_ref[...] = resid_ref[...] + normalise_back(grad_normed, unit, inverse, gain)
    accumulate(
        sums_ref,
        jnp.concatenate(
            [
                column_sums(grad_normed * unit),
                column_sums(grad_normed),
                column_sums(dq.astype(f32)),
                column_sums(dv.astype(f32)),
            ],
            axis=0,
        ),
    )
    accumulate(score_grad_ref, tn(ds, normed)[: score_grad_ref.shape[0]])


def join_tokens(tokens, resid, dq, dk, dv, ds, gain, shift, joint, score_weight, after=(), tile=256):
    rows, width = tokens.shape
    heads = score_weight.shape[1]
    S = jax.ShapeDtypeStruct
    return launch(
        join_tokens_kernel, "join_tokens", 9, (rows // tile,),
        [tiled(tile, width)] * 5 + [
            tiled(tile, LANES), same(width), same(width), same(*joint.shape), same(*score_weight.shape),
        ],
        [tiled(tile, width), same(4, width), same(heads, width)],
        [S((rows, width), f32), S((4, width), f32), S((heads, width), f32)],
        [], 40, (tokens, resid, dq, dk, dv, ds, gain, shift, joint, score_weight), after,
    )


def swap(value, axis, bit):
    count = lax.axis_size(axis)
    return lax.ppermute(value, axis, [(i, i ^ bit) for i in range(count)])


def side(axis, bit):
    return (lax.axis_index(axis) // bit) % 2


def axis_bits(axis):
    count, bits, bit = lax.axis_size(axis), [], 1
    while bit < count:
        bits.append((axis, bit))
        bit *= 2
    return bits


def woven(*lists):
    result = []
    for step in range(max(map(len, lists))):
        for items in lists:
            result += items[step : step + 1]
    return result


def orders():
    near, far = axis_bits("seq"), axis_bits("dp")
    first, rest = near[:1], near[1:]
    return (
        first + rest + far,
        first + woven(rest[::-1], far),
    )


def cut(value, pieces):
    return value.reshape(pieces, value.shape[0] // pieces, value.shape[1])


class Chain:
    def __init__(self, send, keep, order):
        self.order, self.level, self.down = order, 0, True
        half = 2 ** (len(order) - 1)
        self.send, self.keep = cut(send, half), cut(keep, half)
        self.mine = [side(*where).astype(jnp.int32) for where in order]

    def got(self):
        return swap(self.send, *self.order[self.level])


def added(one, two):
    return (one[...].astype(f32) + two[...].astype(f32)).astype(bf16)


class Total:
    def __init__(self, value, order):
        self.send, self.order, self.level = value, order, 0

    def got(self):
        return swap(self.send, *self.order[self.level])


def advance_kernel(plan, bits_ref, *refs):
    refs = list(refs)
    outs = refs[sum(4 if kind == "split" else 2 for kind in plan) :]
    for kind in plan:
        if kind == "split":
            for _ in range(2):
                outs.pop(0)[...] = added(refs.pop(0), refs.pop(0))
        elif kind == "sum":
            outs.pop(0)[...] = refs.pop(0)[...] + refs.pop(0)[...]
        elif kind == "close":
            outs.pop(0)[...] = added(refs.pop(0), refs.pop(0))
        else:
            out = outs.pop(0)
            for which in range(2):
                out[which] = refs.pop(0)[...]


def advance(chains, after=()):
    plan, operands, in_specs, out_specs, shapes, bits, free = [], [], [], [], [], [], []
    depth = len(chains[0].order)
    for chain in chains:
        if isinstance(chain, Total):
            plan.append("sum")
            continue
        last = chain.down and chain.level == depth - 1
        plan.append("close" if last else "split" if chain.down else "stack")
    sizes = [chain.send.shape[0] // (2 if kind == "split" else 1) for chain, kind in zip(chains, plan)]
    steps = min([4] + [size for size, kind in zip(sizes, plan) if kind != "sum"])
    S = jax.ShapeDtypeStruct

    def half_of(which, other, block, tail):
        def index(g, bits_ref):
            mine = bits_ref[which]
            return ((1 - mine if other else mine) * steps + g, 0, 0)

        return pl.BlockSpec((block,) + tail, index)

    for chain, kind, size in zip(chains, plan, sizes):
        got, tail = chain.got(), chain.send.shape[1:]
        block = size // steps
        if kind == "sum":
            free += [len(operands), len(operands) + 1]
            operands += [chain.send, got]
            in_specs += [same(*chain.send.shape)] * 2
            out_specs += [same(*chain.send.shape)]
            shapes += [S(chain.send.shape, f32)]
        elif kind == "split":
            which = len(bits)
            bits.append(chain.mine[chain.level + 1])
            places = len(operands)
            free += [places + 1, places + 3] if chain.level == 0 else range(places, places + 4)
            for other in (True, False):
                operands += [chain.keep, got]
                in_specs += [half_of(which, other, block, tail)] * 2
            out_specs += [tiled(block, *tail)] * 2
            shapes += [S((size,) + tail, bf16)] * 2
        elif kind == "close":
            free += [len(operands), len(operands) + 1]
            operands += [chain.keep, got]
            in_specs += [tiled(block, *tail)] * 2
            out_specs += [tiled(block, *tail)]
            shapes += [S((size,) + tail, bf16)]
        else:
            free += [len(operands), len(operands) + 1]
            operands += [chain.send, got]
            in_specs += [tiled(block, *tail)] * 2
            out_specs += [pl.BlockSpec((2, block) + tail, lambda g, *_: (0, g, 0, 0))]
            shapes += [S((2, size) + tail, bf16)]
    bits = jnp.stack(bits) if bits else jnp.zeros((1,), jnp.int32)
    outs = launch(
        functools.partial(advance_kernel, plan), "advance", 2, (steps,), in_specs, out_specs, shapes, [], 40, operands,
        after, (bits,), free,
    )
    for chain, kind in zip(chains, plan):
        if kind == "split":
            chain.send, chain.keep = outs[:2]
            chain.level += 1
            outs = outs[2:]
        elif kind == "sum":
            chain.send = outs[0]
            chain.level += 1
            outs = outs[1:]
        else:
            chain.send = outs[0].reshape((-1,) + chain.send.shape[1:])
            outs = outs[1:]
            if kind == "close":
                chain.down = False
            else:
                chain.level -= 1
    return outs[0]


def ends(chain):
    return chain.send, chain.got()


def own_place(order):
    place = 0
    for axis, bit in order:
        place = place * 2 + side(axis, bit)
    return place.astype(jnp.int32).reshape(1)


def piece_of(own, p, count, value_ref, other_ref):
    half = count // 2
    at = jnp.bitwise_xor(own & (half - 1), p & (half - 1))
    far_side = jnp.bitwise_xor(own, p) >= half
    return jnp.where(far_side, other_ref[at], value_ref[at]).astype(f32)


def widen_kernel(group, count, own_ref, value_ref, other_ref, out_ref):
    own, first = own_ref[0], pl.program_id(0) * group
    for i in range(group):
        out_ref[i] = piece_of(own, first + i, count, value_ref, other_ref)


def widen(own, value, other, name, after=(), group=4):
    half, size, n = value.shape
    count = 2 * half
    out, token = launch(
        functools.partial(widen_kernel, group, count), name, 5, (count // group,),
        [same(half, size, n)] * 2, [tiled(group, size, n)], [jax.ShapeDtypeStruct((count, size, n), f32)],
        [], 40, (value, other), after, (own,), (0, 1),
    )
    return out.reshape(count * size, n), token


def widen_pair_kernel(group, count, own_one_ref, own_two_ref, v_one, o_one, v_two, o_two, first_ref, joint_ref):
    own_one, own_two = own_one_ref[0], own_two_ref[0]
    half, base = count // 2, pl.program_id(0) * group
    width, size = v_one.shape[2], v_two.shape[1]
    for i in range(group):
        p = base + i
        first_ref[i] = piece_of(own_one, p, count, v_one, o_one)
        piece = piece_of(own_one, half + p, count, v_one, o_one)
        for j in range(2):
            joint_ref[2 * i + j, :, :width] = piece[j * size : (j + 1) * size]
            joint_ref[2 * i + j, :, width:] = piece_of(own_two, 2 * p + j, count, v_two, o_two)


def widen_pair(own_one, own_two, v_one, o_one, v_two, o_two, group=4):
    half, size, width = v_one.shape
    count = 2 * half
    small, rest = v_two.shape[1:]
    S = jax.ShapeDtypeStruct
    first, joint, _ = launch(
        functools.partial(widen_pair_kernel, group, count), "widen_joint", 5, (half // group,),
        [same(*v_one.shape)] * 2 + [same(*v_two.shape)] * 2,
        [tiled(group, size, width), tiled(2 * group, small, width + rest)],
        [S((half, size, width), f32), S((count, small, width + rest), f32)],
        [], 40, (v_one, o_one, v_two, o_two), (), (own_one, own_two), (0, 1, 2, 3),
    )
    return first.reshape(half * size, width), joint.reshape(count * small, width + rest)


def per_device(
    tokens, cotangent, first_gain, first_shift, joint_weight, query_bias, value_bias, score_weight, out_weight, out_bias,
    second_gain, second_shift, expand_weight, expand_bias, reduce_weight, reduce_bias, picks, quota,
):
    rows, width = tokens.shape[1:]
    heads = score_weight.shape[1]
    inner = expand_weight.shape[1]
    blocks = lax.axis_size("seq")
    slots = blocks * PICK
    here = lax.axis_index("seq").astype(jnp.int32).reshape(1)
    first, second = orders()
    mine = side(*first[0]).astype(jnp.int32).reshape(1)
    inputs, grad_out = tokens[0], cotangent[0]
    live = (jnp.arange(PICK, dtype=jnp.int32)[None, :] < quota[0, 0][:, None]).astype(jnp.int32)
    flat = picks[0, 0].reshape(-1)
    normed, q, k, v, score, rim_sent, sent, _ = project(
        inputs, flat[:, None], live.reshape(-1, 1), first_gain, first_shift, joint_weight, query_bias, value_bias,
        score_weight,
    )
    channels = sent.shape[1]
    rim = passed_along(rim_sent, "seq", 1)
    far = lax.all_to_all(
        sent.reshape(blocks, PICK, channels), "seq", split_axis=0, concat_axis=0, tiled=True
    ).reshape(slots, channels)
    mixed, total, _ = attend(here, q, k, v, score, rim, far, heads)
    resid, hidden, grad_pre, expand_sums, *halves, _ = feed(
        mine, mixed, inputs, grad_out, out_weight, out_bias, second_gain, second_shift, expand_weight, expand_bias,
        reduce_weight,
    )
    reduced, expanded = Chain(*halves[:2], first), Chain(*halves[2:], second)
    one = [reduced, expanded]
    grad_resid, grad_attn, grad_mixed, sums_two, stage = feed_back(
        resid, grad_out, grad_pre, out_weight, second_gain, expand_weight
    )
    stage = advance(one, (stage,))
    dq, dk_own, dv_own, ds_own, rim_grad, far_grad, stage = attend_back(
        here, q, k, v, grad_mixed, total, score, rim, far, heads, (stage,)
    )
    stage = advance(one, (stage,))
    rim_back = passed_along(rim_grad, "seq", -1)
    far_back = lax.all_to_all(
        far_grad.reshape(blocks, PICK, channels), "seq", split_axis=0, concat_axis=0, tiled=True
    ).reshape(slots, channels)
    *halves, stage = pair_outer(mine, mixed, grad_attn, normed, dq, "pair_outer", 6, (stage,))
    paired = Chain(*halves, first)
    stage = advance(one, (stage,))
    dk, dv, ds, *halves, stage = join_keys(mine, dk_own, dv_own, ds_own, rim_back, far_back, flat[None, :], normed, (stage,))
    keyed = Chain(*halves, second)
    two = [paired, keyed]
    stage = advance(one + two, (stage,))
    token_grad, sums_one, score_grad, stage = join_tokens(
        inputs, grad_resid, dq, dk, dv, ds, first_gain, first_shift, joint_weight, score_weight, (stage,)
    )
    small = Total(
        jnp.concatenate([sums_one, sums_two, expand_sums.reshape(inner // width, width), score_grad], axis=0), first
    )
    stage = advance(one + two, (stage,))
    layer_out, stage = finish(resid, hidden, reduce_weight, reduce_bias, (stage,))

    def with_small(chains):
        return chains + ([small] if small.level < len(first) else [])

    while one[0].level > 0 or one[0].down:
        stage = advance(with_small(one + two), (stage,))
    reduce_weight_grad, stage = widen(own_place(first), *ends(reduced), "widen_reduce", (stage,))
    while two[0].level > 1 or two[0].down:
        stage = advance(with_small(two), (stage,))
    expand_weight_grad, stage = widen(own_place(second), *ends(expanded), "widen_expand", (stage,))
    while two[0].level > 0 or two[0].down:
        stage = advance(with_small(two), (stage,))
    out_weight_grad, joint_weight_grad = widen_pair(own_place(first), own_place(second), *ends(paired), *ends(keyed))
    small = small.send
    gain_one, shift_one, query_sum, value_sum, out_sum, gain_two, shift_two, reduce_sum = (small[i] for i in range(8))
    past = 8 + inner // width
    return (
        layer_out[None],
        token_grad[None],
        gain_one,
        shift_one,
        joint_weight_grad,
        query_sum,
        value_sum,
        small[past : past + heads].T,
        out_weight_grad,
        out_sum,
        gain_two,
        shift_two,
        expand_weight_grad,
        small[8:past].reshape(inner),
        reduce_weight_grad,
        reduce_sum,
    )


def solution(mesh):
    placed = (
        P("dp", "seq", None),
        P("dp", "seq", None),
        P(),
        P(),
        P(),
        P(),
        P(),
        P(),
        P(),
        P(),
        P(),
        P(),
        P(),
        P(),
        P(),
        P(),
        P("dp", "seq", None, None),
        P("dp", "seq", None),
    )
    return jax.shard_map(
        per_device,
        mesh=mesh,
        in_specs=placed,
        out_specs=(
            P("dp", "seq", None),
            P("dp", "seq", None),
            P(),
            P(),
            P(),
            P(),
            P(),
            P(),
            P(),
            P(),
            P(),
            P(),
            P(),
            P(),
            P(),
            P(),
        ),
        check_vma=False,
    )
```

```python
import functools
import math

import jax
import jax.numpy as jnp
from jax import lax
from jax.experimental import pallas as pl
from jax.experimental.pallas import tpu as pltpu
from jax.sharding import PartitionSpec as P

WIN = 64
PICK = 8
LANES = 128
PACK = 4
DIGIT = 32
TOKEN = (8, 128)
epsilon = 1e-05
very_low = -1e30
bf16 = jnp.bfloat16
f32 = jnp.float32


def nt(left, right):
    return lax.dot_general(left, right, (((1,), (1,)), ((), ())), preferred_element_type=f32)


def tn(left, right):
    return lax.dot_general(left, right, (((0,), (0,)), ((), ())), preferred_element_type=f32)


def nn(left, right):
    return jnp.dot(left, right, preferred_element_type=f32)


def three_parts(value):
    high = value.astype(bf16)
    rest = value - high.astype(f32)
    middle = rest.astype(bf16)
    low = (rest - middle.astype(f32)).astype(bf16)
    return high, middle, low


def head_spread(group, head_size, width):
    row = lax.broadcasted_iota(jnp.int32, (LANES, width), 0)
    lane = lax.broadcasted_iota(jnp.int32, (LANES, width), 1)
    return jnp.where(row == group * PACK + lane // WIN, 1.0, 0.0).astype(bf16)


def stack_heads(tile, head_size, factor):
    width = tile.shape[1]
    lane = lax.broadcasted_iota(jnp.int32, tile.shape, 1) // head_size
    scaled = tile * jnp.asarray(factor, tile.dtype)
    zero = jnp.zeros_like(scaled)
    return jnp.concatenate([jnp.where(lane == h, scaled, zero) for h in range(PACK)], axis=0)


def pick_heads(full, head_size):
    lane = lax.broadcasted_iota(jnp.int32, (WIN, full.shape[1]), 1) // head_size
    out = full[0:WIN]
    for h in range(1, PACK):
        out = jnp.where(lane == h, full[h * WIN : (h + 1) * WIN], out)
    return out


def gates_into(gate_ref, group, place, score_ref, rim_score_ref, far_score_ref, head_size, rows, slots):
    width = PACK * WIN
    spread = head_spread(group, head_size, width)

    def expand(score):
        gate = jax.nn.log_sigmoid(score.astype(f32))
        return sum(nn(part, spread) for part in three_parts(gate))

    gate_ref[0:WIN, :] = jnp.where(place == 0, very_low, expand(rim_score_ref[...]))
    gate_ref[WIN : WIN + rows, :] = expand(score_ref[...])
    gate_ref[WIN + rows :, :] = expand(far_score_ref[...])


def near_bias(width):
    key = lax.broadcasted_iota(jnp.int32, (2 * WIN, width), 0)
    query = lax.broadcasted_iota(jnp.int32, (2 * WIN, width), 1) % WIN
    return (key <= query + WIN) & (key > query)


def tile_logits(i, keys_cat, query_stack, gate_ref, far_pos, place, rows, near_ok):
    width = PACK * WIN
    raw = nt(keys_cat, query_stack)
    gate_near = gate_ref[pl.ds(pl.multiple_of(i * WIN, WIN), 2 * WIN), :]
    gate_far = gate_ref[WIN + rows :, :]
    slots = gate_far.shape[0]
    near = jnp.where(near_ok, raw[: 2 * WIN] + gate_near, very_low)
    lane = lax.broadcasted_iota(jnp.int32, (slots, LANES), 1) % WIN
    far_ok = far_pos <= lane + (place * rows + i * WIN - WIN)
    far_raw = raw[2 * WIN :] + gate_far
    far = jnp.concatenate(
        [
            jnp.where(far_ok, far_raw[:, c * LANES : (c + 1) * LANES], very_low)
            for c in range(width // LANES)
        ],
        axis=1,
    )
    return jnp.concatenate([near, far], axis=0)


def launch(kernel, name, work, grid, in_specs, out_specs, out_shape, scratch, limit, operands, after=(), prefetch=(),
           free=(), aliases=None):
    count, extra = len(operands), len(after)

    def body(*refs):
        lead = len(prefetch)
        rest = refs[lead + count + extra :]
        rest[len(shapes)][...] = jnp.zeros(TOKEN, f32)
        kernel(*refs[: lead + count], *rest[: len(shapes)], *rest[len(shapes) + 1 :])

    def place(at, value, spec):
        if spec.memory_space == pltpu.SMEM or at in free:
            return value
        return pltpu.with_memory_space_constraint(value, pltpu.HBM)

    operands = [place(at, value, spec) for at, (value, spec) in enumerate(zip(operands, in_specs))]
    after = [pltpu.with_memory_space_constraint(value, pltpu.HBM) for value in after]
    shapes, kept = out_shape, len(free) > 0 and name == "advance"
    out = pl.pallas_call(
        body,
        grid_spec=pltpu.PrefetchScalarGridSpec(
            num_scalar_prefetch=len(prefetch),
            grid=grid,
            in_specs=list(in_specs) + [pl.BlockSpec(memory_space=pl.ANY)] * extra,
            out_specs=list(out_specs) + [same(*TOKEN)],
            scratch_shapes=scratch,
        ),
        out_shape=[shape if kept else pltpu.HBM(shape.shape, shape.dtype) for shape in shapes] + [pltpu.HBM(TOKEN, f32)],
        compiler_params=pltpu.CompilerParams(vmem_limit_bytes=limit * 2**20),
        cost_estimate=pl.CostEstimate(flops=int(work * 5e9), bytes_accessed=2**20, transcendentals=0),
        input_output_aliases=aliases or {},
        name=name,
    )(*prefetch, *operands, *after)
    return list(out)


def passed_along(value, axis, steps):
    count = lax.axis_size(axis)
    leading, last = (max(0, -steps), min(count, count - steps))
    return lax.ppermute(value, axis, [(source, source + steps) for source in range(leading, last)])


def normalise(values):
    average = jnp.mean(values, axis=-1, keepdims=True)
    centred = values - average
    variance = jnp.mean(centred * centred, axis=-1, keepdims=True)
    inverse = lax.rsqrt(variance + epsilon)
    return (centred * inverse, inverse)


def normalise_back(grad_out, unit, inverse, gain):
    grad_unit = grad_out * gain
    mean_grad = jnp.mean(grad_unit, axis=-1, keepdims=True)
    mean_cross = jnp.mean(grad_unit * unit, axis=-1, keepdims=True)
    return (grad_unit - mean_grad - unit * mean_cross) * inverse


def row(ref):
    return ref[...].reshape(1, -1)


def column_sums(values):
    return jnp.sum(values, axis=0, keepdims=True)


def accumulate(ref, update):
    step = pl.program_id(0)

    @pl.when(step == 0)
    def _():
        ref[...] = update

    @pl.when(step > 0)
    def _():
        ref[...] += update


def same(*shape):
    return pl.BlockSpec(shape, lambda *_: (0,) * len(shape))


class Moves:
    def __init__(self, sems):
        self.sems, self.made = sems, []

    def add(self, source, target):
        self.made.append((source, target, self.sems.at[len(self.made)]))
        return len(self.made) - 1

    def start(self, *which):
        for at in which:
            pltpu.make_async_copy(*self.made[at]).start()

    def wait(self, *which):
        for at in which:
            pltpu.make_async_copy(*self.made[at]).wait()


def rows_at(index, size):
    return pl.ds(pl.multiple_of(index * size, size), size)


def vmem():
    return pl.BlockSpec(memory_space=pltpu.VMEM)


def anywhere():
    return pl.BlockSpec(memory_space=pl.ANY)


def spread_slots(grid):
    blocks = grid.shape[0]
    slots = blocks * PICK
    wide = jnp.concatenate([jnp.broadcast_to(grid[s : s + 1, :], (PICK, grid.shape[1])) for s in range(blocks)], axis=0)
    lane = lax.broadcasted_iota(jnp.int32, wide.shape, 1)
    turn = lax.broadcasted_iota(jnp.int32, wide.shape, 0) % PICK
    return jnp.sum(jnp.where(lane == turn, wide, 0.0), axis=1, keepdims=True)


def project_kernel(
    steps, tokens_ref, picks_ref, quota_ref, gain_ref, shift_ref, joint_ref, query_bias_ref, value_bias_ref,
    score_weight_ref, normed_ref, q_ref, k_ref, v_ref, score_ref, rim_ref, sent_ref, gathered,
):
    step = pl.program_id(0)
    tile, width = tokens_ref.shape
    unit, _ = normalise(tokens_ref[...].astype(f32))
    normed = (unit * row(gain_ref) + row(shift_ref)).astype(bf16)
    normed_ref[...] = normed
    q_ref[...] = (nn(normed, joint_ref[:, :width]) + row(query_bias_ref)).astype(bf16)
    keys = nn(normed, joint_ref[:, width : 2 * width]).astype(bf16)
    values = (nn(normed, joint_ref[:, 2 * width :]) + row(value_bias_ref)).astype(bf16)
    score = nt(normed, score_weight_ref[...]).astype(bf16)
    heads = score.shape[1]
    k_ref[...] = keys
    v_ref[...] = values
    score_ref[...] = jnp.zeros_like(score_ref)
    score_ref[:, :heads] = score
    picks = spread_slots(picks_ref[...].astype(f32))
    slots = picks.shape[0]
    row_of = lax.broadcasted_iota(jnp.int32, (slots, tile), 1) + step * tile
    chosen = jnp.where(picks == row_of.astype(f32), 1.0, 0.0).astype(bf16)
    parts = ((0, keys), (width, values), (2 * width, normed), (3 * width, score_ref[...]))

    @pl.when(step == 0)
    def _():
        gathered[...] = jnp.zeros_like(gathered)

    for start, part in parts:
        gathered[:, start : start + part.shape[1]] += nn(chosen, part)

    @pl.when(step == steps - 1)
    def _():
        for start, part in parts:
            rim_ref[:, start : start + part.shape[1]] = part[tile - WIN :]
        sent_ref[...] = gathered[...].astype(bf16)
        lane = lax.broadcasted_iota(jnp.int32, (slots, LANES), 1)
        blocks = slots // PICK
        quota = jnp.broadcast_to(quota_ref[...].astype(f32), (slots, blocks))
        block_of = lax.broadcasted_iota(jnp.int32, (slots, blocks), 0) // PICK
        taken = jnp.where(lax.broadcasted_iota(jnp.int32, (slots, blocks), 1) == block_of, quota, 0.0)
        taken = jnp.sum(taken, axis=1, keepdims=True)
        turn = (lax.broadcasted_iota(jnp.int32, (slots, 1), 0) % PICK).astype(f32)
        live = jnp.where(turn < taken, 1.0, 0.0)
        high = jnp.floor(picks * (1.0 / DIGIT))
        coded = jnp.where(lane == heads, high, jnp.where(lane == heads + 1, picks - high * DIGIT, live))
        sent_ref[:, 3 * width :] = jnp.where(
            (lane >= heads) & (lane < heads + 3), coded, gathered[:, 3 * width :]
        ).astype(bf16)


def tiled(*shape):
    return pl.BlockSpec(shape, lambda r, *_: (r,) + (0,) * (len(shape) - 1))


def project(tokens, picks, quota, gain, shift, joint, query_bias, value_bias, score_weight, tile=256):
    rows, width = tokens.shape
    slots = picks.shape[0] * picks.shape[1]
    channels = 3 * width + LANES
    steps = rows // tile
    S = jax.ShapeDtypeStruct
    return launch(
        functools.partial(project_kernel, steps),
        "project", 10, (steps,),
        [
            tiled(tile, width), same(*picks.shape), same(*quota.shape), same(width), same(width), same(*joint.shape),
            same(width), same(width), same(*score_weight.shape),
        ],
        [tiled(tile, width)] * 4 + [tiled(tile, LANES), same(WIN, channels), same(slots, channels)],
        [S((rows, width), bf16)] * 4 + [S((rows, LANES), bf16), S((WIN, channels), bf16), S((slots, channels), bf16)],
        [pltpu.VMEM((slots, channels), f32)], 24,
        (tokens, picks, quota, gain, shift, joint, query_bias, value_bias, score_weight),
    )


def far_positions(far_score, heads, place_rows, blocks):
    wide = far_score.astype(f32)
    slot = lax.broadcasted_iota(jnp.int32, (far_score.shape[0], 1), 0)
    at = (wide[:, heads : heads + 1] * DIGIT + wide[:, heads + 1 : heads + 2]).astype(jnp.int32)
    return jnp.where(
        wide[:, heads + 2 : heads + 3] > 0.5, (slot // PICK) * place_rows + at, 2 * place_rows * blocks
    )


def load_block(group, place_ref, k_ref, v_ref, score_ref, rim_refs, far_refs, keys, values, gate_ref, head_size):
    rows, width = k_ref.shape
    rim_k_ref, rim_v_ref, rim_score_ref = rim_refs
    far_score_ref = far_refs[2]
    slots = far_score_ref.shape[0]
    keys[0:WIN, :] = rim_k_ref[...]
    keys[WIN:, :] = k_ref[...]
    values[0:WIN, :] = rim_v_ref[...]
    values[WIN:, :] = v_ref[...]
    gates_into(gate_ref, group, place_ref[0], score_ref, rim_score_ref, far_score_ref, head_size, rows, slots)


def attend_kernel(
    heads, head_size, unroll, place_ref, q_ref, k_ref, v_ref, score_ref,
    rim_k_ref, rim_v_ref, rim_score_ref, far_k_ref, far_v_ref, far_score_ref,
    mixed_ref, total_ref, keys, values, gate_ref,
):
    group = pl.program_id(0)
    place = place_ref[0]
    rows, width = q_ref.shape
    slots = far_k_ref.shape[0]
    load_block(
        group, place_ref, k_ref, v_ref, score_ref, (rim_k_ref, rim_v_ref, rim_score_ref),
        (far_k_ref, far_v_ref, far_score_ref), keys, values, gate_ref, head_size,
    )
    near_ok = near_bias(width)
    far_pos = jnp.broadcast_to(far_positions(far_score_ref[...], heads, rows, slots // PICK), (slots, LANES))

    @pl.loop(0, rows // WIN, unroll=unroll)
    def _(i):
        at = pl.ds(pl.multiple_of(i * WIN, WIN), WIN)
        span = pl.ds(pl.multiple_of(i * WIN, WIN), 2 * WIN)
        keys_cat = jnp.concatenate([keys[span, :], far_k_ref[...]], axis=0)
        values_cat = jnp.concatenate([values[span, :], far_v_ref[...]], axis=0)
        stack = stack_heads(q_ref[at, :], head_size, 1.0 / math.sqrt(head_size))
        logit = tile_logits(i, keys_cat, stack, gate_ref, far_pos, place, rows, near_ok)
        top = jnp.max(logit, axis=0, keepdims=True)
        power = jnp.exp(logit - top)
        total = jnp.sum(power, axis=0, keepdims=True)
        prob = (power * (1.0 / total)).astype(bf16)
        total_ref[0, pl.ds(i, 1), :] = top + jnp.log(total)
        mixed_ref[at, :] = pick_heads(tn(prob, values_cat), head_size).astype(bf16)


def far_specs(slots, width, groups):
    return [
        pl.BlockSpec((slots, width), lambda g: (0, g)),
        pl.BlockSpec((slots, width), lambda g: (0, groups + g)),
        pl.BlockSpec((slots, LANES), lambda g: (0, 3 * groups * width // LANES)),
    ]


def attend(place, q, k, v, score, rim, far, heads, unroll=8):
    rows, model = q.shape
    slots = far.shape[0]
    width = PACK * WIN
    groups = model // width
    cols = pl.BlockSpec((rows, width), lambda g: (0, g))
    return launch(
        functools.partial(attend_kernel, heads, WIN, unroll),
        "attend", 12, (groups,),
        [pl.BlockSpec(memory_space=pltpu.SMEM), cols, cols, cols, pl.BlockSpec((rows, LANES), lambda g: (0, 0))]
        + far_specs(WIN, width, groups) + far_specs(slots, width, groups),
        [cols, pl.BlockSpec((1, rows // WIN, width), lambda g: (g, 0, 0))],
        [
            jax.ShapeDtypeStruct((rows, model), bf16),
            jax.ShapeDtypeStruct((groups, rows // WIN, width), f32),
        ],
        [
            pltpu.VMEM((WIN + rows, width), bf16),
            pltpu.VMEM((WIN + rows, width), bf16),
            pltpu.VMEM((WIN + rows + slots, width), f32),
        ],
        32, (place, q, k, v, score, rim, rim, rim, far, far, far),
    )


def attend_back_kernel(
    heads, head_size, unroll, group, last, place_ref, q_h, k_h, v_h, grad_h, total_ref, score_h, rim_h, far_h, normed_h,
    *refs,
):
    refs = list(refs)
    earlier = [refs.pop(0) for _ in range(5)] if group else []
    beside_refs = [refs.pop(0) for _ in range(2)] if group else []
    dq_h, dk_h, dv_h, ds_ref, rim_out, far_out, rim_ds, far_ds, send, keep = refs[:10]
    q_ref, grad_ref, score_ref, dq_ref, keys, values, gate_ref, dkeys, dvalues, dscore, normed, loaded, stored = refs[10:]
    model = normed.shape[1]
    place = place_ref[0]
    rows, width = q_ref.shape
    slots = far_h.shape[0]
    cols, value_cols = pl.ds(group * width, width), pl.ds(model + group * width, width)
    scores, normed_cols = pl.ds(3 * model, LANES), pl.ds(2 * model, model)
    near, own, far = pl.ds(0, WIN), pl.ds(WIN, rows), pl.ds(WIN + rows, slots)
    loads = Moves(loaded)
    first = [
        loads.add(source, target)
        for source, target in (
            (score_h, score_ref.at[own, :]), (rim_h.at[:, scores], score_ref.at[near, :]),
            (far_h.at[:, scores], score_ref.at[far, :]),
        )
    ]
    second = [
        loads.add(source, target)
        for source, target in (
            (q_h.at[:, cols], q_ref), (grad_h.at[:, cols], grad_ref), (k_h.at[:, cols], keys.at[own, :]),
            (rim_h.at[:, cols], keys.at[near, :]), (far_h.at[:, cols], keys.at[far, :]),
            (v_h.at[:, cols], values.at[own, :]), (rim_h.at[:, value_cols], values.at[near, :]),
            (far_h.at[:, value_cols], values.at[far, :]),
        )
    ]
    third = [
        loads.add(source, target)
        for source, target in (
            (normed_h, normed.at[own, :]), (rim_h.at[:, normed_cols], normed.at[near, :]),
            (far_h.at[:, normed_cols], normed.at[far, :]),
        )
    ]
    loads.start(*first, *second, *third)
    for ref in (dkeys, dvalues, dscore):
        ref[...] = jnp.zeros_like(ref)
    loads.wait(*first)
    gather = head_spread(group, head_size, width)
    gate = jax.nn.log_sigmoid(score_ref[...].astype(f32))
    gate_ref[...] = sum(nn(part, gather) for part in three_parts(gate))
    gate_ref[0:WIN, :] = jnp.where(place == 0, very_low, gate_ref[0:WIN, :])
    near_ok = near_bias(width)
    far_pos = jnp.broadcast_to(far_positions(score_ref[far, :], heads, rows, slots // PICK), (slots, LANES))
    loads.wait(*second)

    @pl.loop(0, rows // WIN, unroll=unroll)
    def _(i):
        at = pl.ds(pl.multiple_of(i * WIN, WIN), WIN)
        after = pl.ds(pl.multiple_of(i * WIN + WIN, WIN), WIN)
        span = pl.ds(pl.multiple_of(i * WIN, WIN), 2 * WIN)
        keys_cat = jnp.concatenate([keys[span, :], keys[far, :]], axis=0)
        values_cat = jnp.concatenate([values[span, :], values[far, :]], axis=0)
        stack = stack_heads(q_ref[at, :], head_size, 1.0 / math.sqrt(head_size))
        grad_stack = stack_heads(grad_ref[at, :], head_size, 1.0)
        logit = tile_logits(i, keys_cat, stack, gate_ref, far_pos, place, rows, near_ok)
        prob = jnp.exp(logit - total_ref[group, pl.ds(i, 1), :])
        grad_prob = nt(values_cat, grad_stack)
        delta = jnp.sum(prob * grad_prob, axis=0, keepdims=True)
        grad_logit = prob * (grad_prob - delta)
        low = grad_logit.astype(bf16)
        dq_ref[at, :] = (pick_heads(tn(low, keys_cat), head_size) * (1.0 / math.sqrt(head_size))).astype(bf16)
        for ref, update in (
            (dkeys, nn(low, stack)),
            (dvalues, nn(prob.astype(bf16), grad_stack)),
            (dscore, grad_logit),
        ):
            ref[at, :] += update[:WIN]
            ref[after, :] = update[WIN : 2 * WIN]
            ref[far, :] += update[2 * WIN :]

    stores = Moves(stored)
    for source, target in ((dq_ref, dq_h), (dkeys.at[own, :], dk_h), (dvalues.at[own, :], dv_h)):
        stores.start(stores.add(source, target))
    loads.wait(*third)
    mine = place % 2
    half = model // 2
    joint = jnp.concatenate(
        [tn(normed[own, :], dq_ref[...])]
        + [tn(normed[...], ref[...].astype(bf16)) for ref in (dkeys, dvalues)],
        axis=1,
    ).astype(bf16)
    top, low = joint[:half], joint[half:]
    start = 0
    if group:
        start = beside_refs[0].shape[1]
        send[:, :start] = beside_refs[0][...]
        keep[:, :start] = beside_refs[1][...]
    send[:, start:] = jnp.where(mine == 0, low, top)
    keep[:, start:] = jnp.where(mine == 0, top, low)
    if group:
        for out, old in zip((rim_out, far_out), earlier[:2]):
            out[...] = old[...]
    for out, part in ((rim_out, near), (far_out, far)):
        for base, ref in ((0, dkeys), (model, dvalues)):
            out[:, base + group * width : base + (group + 1) * width] = ref[part, :].astype(bf16)
    for number, (out_ref, part) in enumerate(((rim_ds, near), (far_ds, far), (ds_ref, own))):
        sums = dscore[part, :]
        high = sums.astype(bf16)
        rest = (sums - high.astype(f32)).astype(bf16)
        update = (nt(high, gather) + nt(rest, gather)) * jax.nn.sigmoid(-score_ref[part, :].astype(f32))
        out_ref[...] = update + earlier[2 + number][...] if group else update
    if last:
        rim_out[:, 2 * model :] = rim_ds[...].astype(bf16)
        far_out[:, 2 * model :] = far_ds[...].astype(bf16)
    stores.wait(*range(len(stores.made)))


def attend_back(place, q, k, v, grad, total, score, rim, far, normed, heads, group, earlier, joined, after=(), unroll=4):
    rows, model = q.shape
    slots = far.shape[0]
    width = PACK * WIN
    groups = model // width
    channels = 2 * model + LANES
    S = jax.ShapeDtypeStruct
    half = (model // 2, 3 * width + (joined[0].shape[1] if joined else 0))
    ext = WIN + rows + slots
    V = pltpu.VMEM
    out = launch(
        functools.partial(attend_back_kernel, heads, WIN, unroll, group, group == groups - 1),
        "attend_back", 13, (),
        [pl.BlockSpec(memory_space=pltpu.SMEM)] + [anywhere()] * 4 + [vmem()] + [anywhere()] * 4
        + [vmem()] * (len(earlier) + len(joined)),
        [anywhere()] * 3 + [vmem()] * 7,
        [
            S((rows, width), bf16), S((rows, width), f32), S((rows, width), f32), S((rows, LANES), f32),
            S((WIN, channels), bf16), S((slots, channels), bf16), S((WIN, LANES), f32), S((slots, LANES), f32),
        ] + [S(half, bf16)] * 2,
        [
            V((rows, width), bf16), V((rows, width), bf16), V((ext, LANES), bf16), V((rows, width), bf16),
            V((ext, width), bf16), V((ext, width), bf16),
        ] + [V((ext, width), f32)] * 4
        + [V((ext, model), bf16), pltpu.SemaphoreType.DMA((14,)), pltpu.SemaphoreType.DMA((3,))],
        30, (place, q, k, v, grad, total, score, rim, far, normed, *earlier, *joined), after,
    )
    dq, dk, dv, ds, rim_out, far_out, rim_ds, far_ds, send, keep, token = out
    return (dq, dk, dv), (rim_out, far_out, rim_ds, far_ds, ds), (send, keep), token


cubic = 0.044715
root = 0.7978845608028654


def feed_kernel(
    tile, pieces, block, mine_ref, mixed_h, tokens_h, cot_h, out_weight_h, expand_h, reduce_h, out_bias_ref, gain_ref,
    shift_ref, expand_bias_ref,
    resid_h, hidden_h, grad_pre_h, sums_ref, send_one, keep_one, send_two, keep_two,
    mixed, tokens, cot, out_weight, expand, reduce, resids, normed, hidden, grad_pre, one, two, loaded, stored,
):
    rows, width = cot.shape
    inner = expand.shape[1]
    span = inner // pieces
    steps = rows // tile
    mine = mine_ref[0]
    loads = Moves(loaded)
    first = [loads.add(*pair) for pair in ((mixed_h, mixed), (out_weight_h, out_weight), (tokens_h, tokens))]
    second = loads.add(cot_h, cot)
    parts = []
    for piece in range(pieces):
        at = pl.ds(piece * span, span)
        parts.append(
            (loads.add(expand_h.at[:, at], expand.at[:, at]), loads.add(reduce_h.at[at, :], reduce.at[at, :]))
        )
    loads.start(*range(len(loads.made)))

    def store(number, source, target):
        return pltpu.make_async_copy(source, target, stored.at[number])

    def tile_stores(step):
        here = rows_at(step, tile)
        return [
            store(3 * step + at, source.at[here, :], target.at[here, :])
            for at, (source, target) in enumerate(((resids, resid_h), (hidden, hidden_h), (grad_pre, grad_pre_h)))
        ]

    def feed_tile(step, leading):
        here = rows_at(step, tile)
        if leading:
            loads.wait(*first)
        resid = tokens[here, :].astype(f32) + nn(mixed[here, :], out_weight[...]) + row(out_bias_ref)
        resids[here, :] = resid
        unit, _ = normalise(resid)
        low = (unit * row(gain_ref) + row(shift_ref)).astype(bf16)
        normed[here, :] = low
        if leading:
            loads.wait(second)
        sums = []
        for piece in range(pieces):
            at = slice(piece * span, (piece + 1) * span)
            if leading:
                loads.wait(*parts[piece])
            pre = nn(low, expand[:, at]) + row(expand_bias_ref)[:, at]
            back = nt(cot[here, :], reduce[at, :])
            squared = pre * pre
            half = 0.5 + 0.5 * jnp.tanh(pre * (root + root * cubic * squared))
            active = pre * half
            slope = half + (active - active * half) * (2.0 * root + 6.0 * root * cubic * squared)
            hidden[here, at] = active.astype(bf16)
            grad = (back * slope).astype(bf16)
            grad_pre[here, at] = grad
            sums.append(column_sums(grad.astype(f32)))
        total = jnp.concatenate(sums, axis=1)
        if leading:
            sums_ref[...] = total
        else:
            sums_ref[...] += total
        for copy in tile_stores(step):
            copy.start()

    feed_tile(0, True)

    @pl.loop(1, steps)
    def _(step):
        feed_tile(step, False)

    base = 3 * steps
    count = inner // 2 // block
    half = width // 2

    def one_store(turn, j):
        here = rows_at(j, block)
        target = (send_one, keep_one)[turn]
        return store(base + turn * count + j, one.at[turn, here, :], target.at[here, :])

    def two_store(turn):
        return store(base + 2 * count + turn, two.at[turn], (send_two, keep_two)[turn])

    for turn in range(2):
        side_of = (1 - mine) if turn == 0 else mine

        @pl.loop(0, count)
        def _(j):
            one[turn, rows_at(j, block), :] = tn(hidden[:, rows_at(side_of * count + j, block)], cot[...]).astype(bf16)
            one_store(turn, j).start()

    for turn in range(2):
        side_of = (1 - mine) if turn == 0 else mine
        two[turn] = tn(normed[:, rows_at(side_of, half)], grad_pre[...]).astype(bf16)
        two_store(turn).start()

    @pl.loop(0, steps)
    def _(step):
        for copy in tile_stores(step):
            copy.wait()

    for turn in range(2):
        @pl.loop(0, count)
        def _(j):
            one_store(turn, j).wait()

        two_store(turn).wait()


def feed(
    mine, mixed, tokens, cot, out_weight, out_bias, gain, shift, expand, expand_bias, reduce, tile=512, pieces=4, block=512,
):
    rows, width = tokens.shape
    inner = expand.shape[1]
    steps = rows // tile
    S = jax.ShapeDtypeStruct
    B = pltpu.VMEM
    return launch(
        functools.partial(feed_kernel, tile, pieces, block),
        "feed", 33, (),
        [anywhere()] * 6 + [vmem()] * 4,
        [anywhere()] * 3 + [vmem()] + [anywhere()] * 4,
        [
            S((rows, width), f32), S((rows, inner), bf16), S((rows, inner), bf16), S((1, inner), f32),
            S((inner // 2, width), bf16), S((inner // 2, width), bf16),
            S((width // 2, inner), bf16), S((width // 2, inner), bf16),
        ],
        [
            B((rows, width), bf16), B((rows, width), bf16), B((rows, width), bf16), B((width, width), bf16),
            B((width, inner), bf16), B((inner, width), bf16), B((rows, width), f32), B((rows, width), bf16),
            B((rows, inner), bf16), B((rows, inner), bf16), B((2, inner // 2, width), bf16), B((2, width // 2, inner), bf16),
            pltpu.SemaphoreType.DMA((4 + 2 * pieces,)),
            pltpu.SemaphoreType.DMA((3 * steps + inner // block + 2,)),
        ],
        60, (mixed, tokens, cot, out_weight, expand, reduce, out_bias, gain, shift, expand_bias), (), (mine,),
    )


def feed_back_kernel(
    tile, pieces, mine_ref, grad_pre_h, resid_h, cot_h, mixed_h, expand_h, out_weight_h, gain_ref,
    grad_resid_h, grad_mixed_h, sums_ref, send_h, keep_h,
    grad_pre, resid, cot, mixed, expand, out_weight, grad_attn, grad_mixed, three, loaded, stored,
):
    rows, width = cot.shape
    inner = expand.shape[1]
    span = inner // pieces
    steps = rows // tile
    half = width // 2
    mine = mine_ref[0]
    loads = Moves(loaded)

    def tile_load(step):
        return [
            loads.add(source.at[rows_at(step, tile), :], target.at[rows_at(step, tile), :])
            for source, target in ((grad_pre_h, grad_pre), (resid_h, resid), (cot_h, cot))
        ]

    tiles = [tile_load(0)]
    weights = [
        loads.add(expand_h.at[:, pl.ds(piece * span, span)], expand.at[:, pl.ds(piece * span, span)])
        for piece in range(pieces)
    ]
    late = loads.add(out_weight_h, out_weight)
    tiles += [tile_load(step) for step in range(1, steps)]
    last = loads.add(mixed_h, mixed)
    loads.start(*range(len(loads.made)))
    stores = Moves(stored)
    sums = []

    def first_part(step):
        here = rows_at(step, tile)
        grad_normed = jnp.zeros((tile, width), f32)
        for piece in range(pieces):
            at = slice(piece * span, (piece + 1) * span)
            if step == 0:
                loads.wait(weights[piece])
            grad_normed = grad_normed + nt(grad_pre[here, at], expand[:, at])
        return grad_normed

    def second_part(step, grad_normed):
        here = rows_at(step, tile)
        wide = cot[here, :].astype(f32)
        unit, inverse = normalise(resid[here, :])
        grad_resid = wide + normalise_back(grad_normed, unit, inverse, row(gain_ref))
        resid[here, :] = grad_resid
        low = grad_resid.astype(bf16)
        grad_attn[here, :] = low
        grad_mixed[here, :] = nt(low, out_weight[...]).astype(bf16)
        sums.append(
            jnp.concatenate(
                [
                    column_sums(low.astype(f32)),
                    column_sums(grad_normed * unit),
                    column_sums(grad_normed),
                    column_sums(wide),
                ],
                axis=0,
            )
        )

    loads.wait(*tiles[0])
    before = first_part(0)
    loads.wait(late, *tiles[1])
    ahead = first_part(1)
    second_part(0, before)
    loads.wait(last, *[at for tile_loads in tiles[2:] for at in tile_loads])
    for step in range(2, steps + 1):
        before, ahead = ahead, first_part(step) if step < steps else None
        second_part(step - 1, before)
    sums_ref[...] = sum(sums)
    for step in range(steps):
        here = rows_at(step, tile)
        stores.start(
            stores.add(resid.at[here, :], grad_resid_h.at[here, :]),
            stores.add(grad_mixed.at[here, :], grad_mixed_h.at[here, :]),
        )
    for turn in range(2):
        side_of = (1 - mine) if turn == 0 else mine
        three[turn] = tn(mixed[:, rows_at(side_of, half)], grad_attn[...]).astype(bf16)
        stores.start(stores.add(three.at[turn], (send_h, keep_h)[turn]))
    stores.wait(*range(len(stores.made)))


def feed_back(mine, grad_pre, resid, cot, mixed, expand, out_weight, gain, tile=256, pieces=4):
    rows, width = resid.shape
    inner = expand.shape[1]
    steps = rows // tile
    S = jax.ShapeDtypeStruct
    B = pltpu.VMEM
    return launch(
        functools.partial(feed_back_kernel, tile, pieces), "feed_back", 12, (),
        [anywhere()] * 6 + [vmem()],
        [anywhere()] * 2 + [vmem()] + [anywhere()] * 2,
        [
            S((rows, width), f32), S((rows, width), bf16), S((4, width), f32),
            S((width // 2, width), bf16), S((width // 2, width), bf16),
        ],
        [
            B((rows, inner), bf16), B((rows, width), f32), B((rows, width), bf16), B((rows, width), bf16),
            B((width, inner), bf16), B((width, width), bf16), B((rows, width), bf16), B((rows, width), bf16),
            B((2, width // 2, width), bf16),
            pltpu.SemaphoreType.DMA((3 * steps + pieces + 2,)),
            pltpu.SemaphoreType.DMA((2 * steps + 2,)),
        ],
        44, (grad_pre, resid, cot, mixed, expand, out_weight, gain), (), (mine,),
    )


def finish_kernel(resid_ref, hidden_ref, reduce_ref, bias_ref, out_ref):
    out_ref[...] = (resid_ref[...] + nn(hidden_ref[...], reduce_ref[...]) + row(bias_ref)).astype(bf16)


def finish(resid, hidden, reduce, bias, after=(), tile=256):
    rows, width = resid.shape
    inner = reduce.shape[0]
    return launch(
        finish_kernel, "finish", 7, (rows // tile,),
        [tiled(tile, width), tiled(tile, inner), same(inner, width), same(width)],
        [tiled(tile, width)], [jax.ShapeDtypeStruct((rows, width), bf16)],
        [], 26, (resid, hidden, reduce, bias), after,
    )


def beside(refs):
    return jnp.concatenate([ref[...] for ref in refs], axis=1)


def join_kernel(
    steps, groups, tokens_ref, resid_ref, ds_ref, rim_ref, far_ref, picks_ref, gain_ref, shift_ref,
    joint_ref, score_weight_ref, *refs,
):
    dq_refs, dk_refs, dv_refs = (refs[at * groups : (at + 1) * groups] for at in range(3))
    token_ref, sums_ref, score_grad_ref = refs[3 * groups :]
    step = pl.program_id(0)
    tile, width = tokens_ref.shape
    heads = score_weight_ref.shape[0]
    unit, inverse = normalise(tokens_ref[...].astype(f32))
    gain = row(gain_ref)
    normed = (unit * gain + row(shift_ref)).astype(bf16)
    picks = spread_slots(picks_ref[...].astype(f32))
    row_of = lax.broadcasted_iota(jnp.int32, (picks.shape[0], tile), 1) + step * tile
    chosen = jnp.where(picks == row_of.astype(f32), 1.0, 0.0).astype(bf16)
    at_end = jnp.where(step == steps - 1, 1.0, 0.0)

    def whole(own, start):
        span = own.shape[1]
        total = own + tn(chosen, far_ref[:, start : start + span])
        rim = rim_ref[:, start : start + span].astype(f32) * at_end
        return jnp.concatenate([total[: tile - WIN], total[tile - WIN :] + rim], axis=0).astype(bf16)

    dq = beside(dq_refs)
    dk = whole(beside(dk_refs), 0)
    dv = whole(beside(dv_refs), width)
    ds = whole(ds_ref[...], 2 * width)
    grad_normed = (
        nt(dq, joint_ref[:, :width])
        + nt(dk, joint_ref[:, width : 2 * width])
        + nt(dv, joint_ref[:, 2 * width :])
        + nn(ds[:, :heads], score_weight_ref[...])
    )
    token_ref[...] = resid_ref[...] + normalise_back(grad_normed, unit, inverse, gain)
    accumulate(
        sums_ref,
        jnp.concatenate(
            [
                column_sums(grad_normed * unit),
                column_sums(grad_normed),
                column_sums(dq.astype(f32)),
                column_sums(dv.astype(f32)),
            ],
            axis=0,
        ),
    )
    accumulate(score_grad_ref, tn(ds, normed)[: score_grad_ref.shape[0]])


def join(tokens, resid, dqs, dks, dvs, ds, rim, far, picks, gain, shift, joint, score_weight, after=(), tile=256):
    rows, width = tokens.shape
    heads = score_weight.shape[0]
    S = jax.ShapeDtypeStruct
    return launch(
        functools.partial(join_kernel, rows // tile, len(dqs)), "join", 14, (rows // tile,),
        [tiled(tile, width)] * 2 + [
            tiled(tile, LANES), same(*rim.shape), same(*far.shape), same(*picks.shape), same(width), same(width),
            same(*joint.shape), same(*score_weight.shape),
        ] + [tiled(tile, part.shape[1]) for part in (*dqs, *dks, *dvs)],
        [tiled(tile, width), same(4, width), same(heads, width)],
        [S((rows, width), f32), S((4, width), f32), S((heads, width), f32)],
        [], 28, (tokens, resid, ds, rim, far, picks, gain, shift, joint, score_weight, *dqs, *dks, *dvs), after,
    )


def swap(value, axis, bit):
    count = lax.axis_size(axis)
    return lax.ppermute(value, axis, [(i, i ^ bit) for i in range(count)])


def side(axis, bit):
    return (lax.axis_index(axis) // bit) % 2


def axis_bits(axis):
    count, bits, bit = lax.axis_size(axis), [], 1
    while bit < count:
        bits.append((axis, bit))
        bit *= 2
    return bits


def woven(*lists):
    result = []
    for step in range(max(map(len, lists))):
        for items in lists:
            result += items[step : step + 1]
    return result


def orders():
    near, far = axis_bits("seq"), axis_bits("dp")
    first, rest = near[:1], near[1:]
    return (
        first + rest + far,
        first + woven(rest[::-1], far),
        first + woven(far, rest),
    )


def cut(value, pieces):
    return value.reshape(pieces, value.shape[0] // pieces, value.shape[1])


class Chain:
    def __init__(self, send, keep, order):
        self.order, self.level, self.down = order, 0, True
        half = 2 ** (len(order) - 1)
        self.send, self.keep = cut(send, half), cut(keep, half)
        self.mine = [side(*where).astype(jnp.int32) for where in order]

    def got(self):
        return swap(self.send, *self.order[self.level])


def added(one, two):
    return (one[...].astype(f32) + two[...].astype(f32)).astype(bf16)


class Total:
    def __init__(self, value, order):
        self.send, self.order, self.level = value, order, 0

    def got(self):
        return swap(self.send, *self.order[self.level])


def advance_kernel(plan, bits_ref, *refs):
    refs = list(refs)
    outs = refs[sum(4 if kind == "split" else 2 for kind in plan) :]
    for kind in plan:
        if kind == "split":
            for _ in range(2):
                outs.pop(0)[...] = added(refs.pop(0), refs.pop(0))
        elif kind == "sum":
            outs.pop(0)[...] = refs.pop(0)[...] + refs.pop(0)[...]
        elif kind == "close":
            outs.pop(0)[...] = added(refs.pop(0), refs.pop(0))
        else:
            out = outs.pop(0)
            for which in range(2):
                out[which] = refs.pop(0)[...]


def advance(chains, after=()):
    plan, operands, in_specs, out_specs, shapes, bits, free = [], [], [], [], [], [], []
    depth = len(chains[0].order)
    for chain in chains:
        if isinstance(chain, Total):
            plan.append("sum")
            continue
        last = chain.down and chain.level == depth - 1
        plan.append("close" if last else "split" if chain.down else "stack")
    sizes = [chain.send.shape[0] // (2 if kind == "split" else 1) for chain, kind in zip(chains, plan)]
    steps = min([4] + [size for size, kind in zip(sizes, plan) if kind != "sum"])
    S = jax.ShapeDtypeStruct

    def half_of(which, other, block, tail):
        def index(g, bits_ref):
            mine = bits_ref[which]
            return ((1 - mine if other else mine) * steps + g, 0, 0)

        return pl.BlockSpec((block,) + tail, index)

    for chain, kind, size in zip(chains, plan, sizes):
        got, tail = chain.got(), chain.send.shape[1:]
        block = size // steps
        if kind == "sum":
            free += [len(operands), len(operands) + 1]
            operands += [chain.send, got]
            in_specs += [same(*chain.send.shape)] * 2
            out_specs += [same(*chain.send.shape)]
            shapes += [S(chain.send.shape, f32)]
        elif kind == "split":
            which = len(bits)
            bits.append(chain.mine[chain.level + 1])
            places = len(operands)
            free += [places + 1, places + 3] if chain.level == 0 else range(places, places + 4)
            for other in (True, False):
                operands += [chain.keep, got]
                in_specs += [half_of(which, other, block, tail)] * 2
            out_specs += [tiled(block, *tail)] * 2
            shapes += [S((size,) + tail, bf16)] * 2
        elif kind == "close":
            free += [len(operands), len(operands) + 1]
            operands += [chain.keep, got]
            in_specs += [tiled(block, *tail)] * 2
            out_specs += [tiled(block, *tail)]
            shapes += [S((size,) + tail, bf16)]
        else:
            free += [len(operands), len(operands) + 1]
            operands += [chain.send, got]
            in_specs += [tiled(block, *tail)] * 2
            out_specs += [pl.BlockSpec((2, block) + tail, lambda g, *_: (0, g, 0, 0))]
            shapes += [S((2, size) + tail, bf16)]
    bits = jnp.stack(bits) if bits else jnp.zeros((1,), jnp.int32)
    outs = launch(
        functools.partial(advance_kernel, plan), "advance", 2, (steps,), in_specs, out_specs, shapes, [], 20, operands,
        after, (bits,), free,
    )
    for chain, kind in zip(chains, plan):
        if kind == "split":
            chain.send, chain.keep = outs[:2]
            chain.level += 1
            outs = outs[2:]
        elif kind == "sum":
            chain.send = outs[0]
            chain.level += 1
            outs = outs[1:]
        else:
            chain.send = outs[0].reshape((-1,) + chain.send.shape[1:])
            outs = outs[1:]
            if kind == "close":
                chain.down = False
            else:
                chain.level -= 1
    return outs[0]


def finished(chain):
    if isinstance(chain, Total):
        return chain.level == len(chain.order)
    return not chain.down and chain.level == 0


def ends(chain):
    return chain.send, chain.got()


def own_place(order):
    place = 0
    for axis, bit in order:
        place = place * 2 + side(axis, bit)
    return place.astype(jnp.int32).reshape(1)


def widen_half(own, chain, half_of, into=(), after=()):
    value, other = half_of
    half, size, n = value.shape
    count, group = 2 * half, 4

    def side_of(own_ref):
        mine = own_ref[0] // half
        return 1 - mine if other else mine

    def kernel(own_ref, value_ref, *refs):
        out_ref = refs[-1]
        for i in range(group):
            out_ref[i] = value_ref[jnp.bitwise_xor(own_ref[0] % group, i)].astype(f32)

    out, token = launch(
        kernel, "widen", 4, (half // group,),
        [pl.BlockSpec((group, size, n), lambda s, own_ref: (jnp.bitwise_xor(own_ref[0] % half // group, s), 0, 0))]
        + [anywhere()] * len(into),
        [pl.BlockSpec((group, size, n), lambda s, own_ref: (side_of(own_ref) * (half // group) + s, 0, 0))],
        [jax.ShapeDtypeStruct((count, size, n), f32)],
        [], 24, (value, *into), after, (own,), (0,), {2: 0} if into else None,
    )
    return out, token


def widen_joint_half(owns, values, other, into=(), after=()):
    half, size, n = values[0].shape
    count, group, model, width = 2 * half, 4, n // 2, PACK * WIN

    def side_of(own_ref):
        mine = own_ref[0] // half
        return 1 - mine if other else mine

    def kernel(own_one_ref, own_two_ref, one_ref, two_ref, *refs):
        joint_ref, first_ref = refs[-2:]
        for i in range(group):
            one = one_ref[jnp.bitwise_xor(own_one_ref[0] % group, i)].astype(f32)
            two = two_ref[jnp.bitwise_xor(own_two_ref[0] % group, i)].astype(f32)
            first_ref[i] = two[:, :model]
            for piece, start, g in ((one, 0, 0), (one, 3 * width, 1), (two, model, 2)):
                for kind in range(3):
                    to = kind * model + g * width
                    joint_ref[i, :, to : to + width] = piece[:, start + kind * width : start + (kind + 1) * width]

    def read(which):
        def index(s, *own_refs):
            return (jnp.bitwise_xor(own_refs[which][0] % half // group, s), 0, 0)

        return pl.BlockSpec((group, size, n), index)

    def write(columns):
        return pl.BlockSpec((group, size, columns), lambda s, own_ref, _: (side_of(own_ref) * (half // group) + s, 0, 0))

    S = jax.ShapeDtypeStruct
    joint, first, token = launch(
        kernel, "widen_joint", 4, (half // group,),
        [read(0), read(1)] + [anywhere()] * len(into), [write(3 * model), write(model)],
        [S((count, size, 3 * model), f32), S((count, size, model), f32)],
        [], 24, (*values, *into), after, tuple(owns), (0, 1), {4: 0, 5: 1} if into else None,
    )
    return (joint, first), token


def per_device(
    tokens, cotangent, first_gain, first_shift, joint_weight, query_bias, value_bias, score_weight, out_weight, out_bias,
    second_gain, second_shift, expand_weight, expand_bias, reduce_weight, reduce_bias, picks, quota,
):
    rows, width = tokens.shape[1:]
    heads = score_weight.shape[1]
    inner = expand_weight.shape[1]
    blocks = lax.axis_size("seq")
    slots = blocks * PICK
    here = lax.axis_index("seq").astype(jnp.int32).reshape(1)
    first, second, _ = orders()
    mine = side(*first[0]).astype(jnp.int32).reshape(1)
    inputs, grad_out = tokens[0], cotangent[0]
    chosen, turned = picks[0, 0], score_weight.T
    normed, q, k, v, score, rim_sent, sent, _ = project(
        inputs, chosen, quota[0], first_gain, first_shift, joint_weight, query_bias, value_bias, turned
    )
    rim = passed_along(rim_sent, "seq", 1)
    far = lax.all_to_all(
        sent.reshape(blocks, PICK, -1), "seq", split_axis=0, concat_axis=0, tiled=True
    ).reshape(slots, -1)
    mixed, total, _ = attend(here, q, k, v, score, rim, far, heads)
    resid, hidden, grad_pre, expand_sums, *halves, _ = feed(
        mine, mixed, inputs, grad_out, out_weight, out_bias, second_gain, second_shift, expand_weight, expand_bias,
        reduce_weight,
    )
    reduced, expanded = Chain(*halves[:2], first), Chain(*halves[2:], second)
    grad_resid, grad_mixed, sums_two, *out_halves, stage = feed_back(
        mine, grad_pre, resid, grad_out, mixed, expand_weight, out_weight, second_gain
    )
    big = [reduced, expanded]
    back = functools.partial(attend_back, here, q, k, v, grad_mixed, total, score, rim, far, normed, heads)
    stage = advance(big, (stage,))
    grads_zero, carried, joined, stage = back(0, (), (), (stage,))
    grads_one, carried, joined, stage = back(1, carried, joined, (stage,))
    one = Chain(*joined, first)
    stage = advance(big, (stage,))
    grads_two, carried, joined, stage = back(2, carried, tuple(out_halves), (stage,))
    two = Chain(*joined, second)
    rim_grad, far_grad, _, _, ds = carried
    rim_back = passed_along(rim_grad, "seq", -1)
    far_back = lax.all_to_all(
        far_grad.reshape(blocks, PICK, -1), "seq", split_axis=0, concat_axis=0, tiled=True
    ).reshape(slots, -1)
    dqs, dks, dvs = zip(grads_zero, grads_one, grads_two)
    stage = advance(big + [one], (stage,))
    stage = advance(big + [two], (stage,))
    token_grad, sums_one, score_grad, stage = join(
        inputs, grad_resid, dqs, dks, dvs, ds, rim_back, far_back, chosen, first_gain, first_shift, joint_weight, turned,
        (stage,),
    )
    small = Total(
        jnp.concatenate([sums_one, sums_two, expand_sums.reshape(inner // width, width), score_grad], axis=0), first
    )
    late = [one, two]
    stage = advance(big + late, (stage,))
    layer_out, stage = finish(resid, hidden, reduce_weight, reduce_bias, (stage,))
    for chains in (
        big + late + [small], late, big + late + [small], late + [small], big + late + [small],
    ):
        stage = advance([chain for chain in chains if not finished(chain)], (stage,))
    while not finished(reduced):
        stage = advance([chain for chain in big + late if not finished(chain)], (stage,))
    own_first, own_second = own_place(first), own_place(second)
    halves_one, halves_two = ends(reduced), ends(expanded)
    reduce_weight_grad, stage = widen_half(own_first, reduced, (halves_one[0], False), (), (stage,))
    expand_weight_grad, stage = widen_half(own_second, expanded, (halves_two[0], False), (), (stage,))
    reduce_weight_grad, stage = widen_half(own_first, reduced, (halves_one[1], True), (reduce_weight_grad,), (stage,))
    expand_weight_grad, stage = widen_half(own_second, expanded, (halves_two[1], True), (expand_weight_grad,), (stage,))
    while not (finished(one) and finished(two)):
        stage = advance([chain for chain in late if not finished(chain)], (stage,))
    while not finished(small):
        stage = advance([small], (stage,))
    halves_one, halves_two = ends(one), ends(two)
    owns = (own_first, own_second)
    both, stage = widen_joint_half(owns, (halves_one[0], halves_two[0]), False, (), (stage,))
    both, stage = widen_joint_half(owns, (halves_one[1], halves_two[1]), True, both, (stage,))
    reduce_weight_grad = reduce_weight_grad.reshape(inner, width)
    expand_weight_grad = expand_weight_grad.reshape(width, inner)
    joint_weight_grad, out_weight_grad = both[0].reshape(width, 3 * width), both[1].reshape(width, width)
    small = small.send
    gain_one, shift_one, query_sum, value_sum, out_sum, gain_two, shift_two, reduce_sum = (small[i] for i in range(8))
    past = 8 + inner // width
    return (
        layer_out[None],
        token_grad[None],
        gain_one,
        shift_one,
        joint_weight_grad,
        query_sum,
        value_sum,
        small[past : past + heads].T,
        out_weight_grad,
        out_sum,
        gain_two,
        shift_two,
        expand_weight_grad,
        small[8:past].reshape(inner),
        reduce_weight_grad,
        reduce_sum,
    )


def solution(mesh):
    placed = (
        P("dp", "seq", None),
        P("dp", "seq", None),
        P(),
        P(),
        P(),
        P(),
        P(),
        P(),
        P(),
        P(),
        P(),
        P(),
        P(),
        P(),
        P(),
        P(),
        P("dp", "seq", None, None),
        P("dp", "seq", None),
    )
    return jax.shard_map(
        per_device,
        mesh=mesh,
        in_specs=placed,
        out_specs=(
            P("dp", "seq", None),
            P("dp", "seq", None),
            P(),
            P(),
            P(),
            P(),
            P(),
            P(),
            P(),
            P(),
            P(),
            P(),
            P(),
            P(),
            P(),
            P(),
        ),
        check_vma=False,
    )
```

```python
import functools
import math

import jax
import jax.numpy as jnp
from jax import lax
from jax.experimental import pallas as pl
from jax.experimental.pallas import tpu as pltpu
from jax.sharding import PartitionSpec as P

WIN = 64
PICK = 8
LANES = 128
PACK = 4
DIGIT = 32
TOKEN = (8, 128)
epsilon = 1e-05
very_low = -1e30
bf16 = jnp.bfloat16
f32 = jnp.float32


def nt(left, right):
    return lax.dot_general(left, right, (((1,), (1,)), ((), ())), preferred_element_type=f32)


def tn(left, right):
    return lax.dot_general(left, right, (((0,), (0,)), ((), ())), preferred_element_type=f32)


def nn(left, right):
    return jnp.dot(left, right, preferred_element_type=f32)


def three_parts(value):
    high = value.astype(bf16)
    rest = value - high.astype(f32)
    middle = rest.astype(bf16)
    low = (rest - middle.astype(f32)).astype(bf16)
    return high, middle, low


def head_spread(group, head_size, width):
    row = lax.broadcasted_iota(jnp.int32, (LANES, width), 0)
    lane = lax.broadcasted_iota(jnp.int32, (LANES, width), 1)
    return jnp.where(row == group * PACK + lane // WIN, 1.0, 0.0).astype(bf16)


def stack_heads(tile, head_size, factor):
    width = tile.shape[1]
    lane = lax.broadcasted_iota(jnp.int32, tile.shape, 1) // head_size
    scaled = tile * jnp.asarray(factor, tile.dtype)
    zero = jnp.zeros_like(scaled)
    return jnp.concatenate([jnp.where(lane == h, scaled, zero) for h in range(PACK)], axis=0)


def pick_heads(full, head_size):
    lane = lax.broadcasted_iota(jnp.int32, (WIN, full.shape[1]), 1) // head_size
    out = full[0:WIN]
    for h in range(1, PACK):
        out = jnp.where(lane == h, full[h * WIN : (h + 1) * WIN], out)
    return out


def gates_into(gate_ref, group, place, score_ref, rim_score_ref, far_score_ref, head_size, rows, slots):
    width = PACK * WIN
    spread = head_spread(group, head_size, width)

    def expand(score):
        gate = jax.nn.log_sigmoid(score.astype(f32))
        return sum(nn(part, spread) for part in three_parts(gate))

    gate_ref[0:WIN, :] = jnp.where(place == 0, very_low, expand(rim_score_ref[...]))
    gate_ref[WIN : WIN + rows, :] = expand(score_ref[...])
    gate_ref[WIN + rows :, :] = expand(far_score_ref[...])


def near_bias(width):
    key = lax.broadcasted_iota(jnp.int32, (2 * WIN, width), 0)
    query = lax.broadcasted_iota(jnp.int32, (2 * WIN, width), 1) % WIN
    return (key <= query + WIN) & (key > query)


def tile_logits(i, keys_cat, query_stack, gate_ref, far_pos, place, rows, near_ok):
    width = PACK * WIN
    raw = nt(keys_cat, query_stack)
    gate_near = gate_ref[pl.ds(pl.multiple_of(i * WIN, WIN), 2 * WIN), :]
    gate_far = gate_ref[WIN + rows :, :]
    slots = gate_far.shape[0]
    near = jnp.where(near_ok, raw[: 2 * WIN] + gate_near, very_low)
    lane = lax.broadcasted_iota(jnp.int32, (slots, LANES), 1) % WIN
    far_ok = far_pos <= lane + (place * rows + i * WIN - WIN)
    far_raw = raw[2 * WIN :] + gate_far
    far = jnp.concatenate(
        [
            jnp.where(far_ok, far_raw[:, c * LANES : (c + 1) * LANES], very_low)
            for c in range(width // LANES)
        ],
        axis=1,
    )
    return jnp.concatenate([near, far], axis=0)


def launch(kernel, name, work, grid, in_specs, out_specs, out_shape, scratch, limit, operands, after=(), prefetch=(),
           free=(), aliases=None, held=()):
    count, extra = len(operands), len(after)

    def body(*refs):
        lead = len(prefetch)
        rest = refs[lead + count + extra :]
        rest[len(shapes)][...] = jnp.zeros(TOKEN, f32)
        kernel(*refs[: lead + count], *rest[: len(shapes)], *rest[len(shapes) + 1 :])

    def place(at, value, spec):
        if spec.memory_space == pltpu.SMEM or at in free:
            return value
        return pltpu.with_memory_space_constraint(value, pltpu.HBM)

    operands = [place(at, value, spec) for at, (value, spec) in enumerate(zip(operands, in_specs))]
    after = [pltpu.with_memory_space_constraint(value, pltpu.HBM) for value in after]
    shapes, kept = out_shape, len(free) > 0 and name == "advance"
    out = pl.pallas_call(
        body,
        grid_spec=pltpu.PrefetchScalarGridSpec(
            num_scalar_prefetch=len(prefetch),
            grid=grid,
            in_specs=list(in_specs) + [pl.BlockSpec(memory_space=pl.ANY)] * extra,
            out_specs=list(out_specs) + [same(*TOKEN)],
            scratch_shapes=scratch,
        ),
        out_shape=[
            shape if kept and at not in held else pltpu.HBM(shape.shape, shape.dtype) for at, shape in enumerate(shapes)
        ] + [pltpu.HBM(TOKEN, f32)],
        compiler_params=pltpu.CompilerParams(vmem_limit_bytes=limit * 2**20),
        cost_estimate=pl.CostEstimate(flops=int(work * 5e9), bytes_accessed=2**20, transcendentals=0),
        input_output_aliases=aliases or {},
        name=name,
    )(*prefetch, *operands, *after)
    return list(out)


def passed_along(value, axis, steps):
    count = lax.axis_size(axis)
    leading, last = (max(0, -steps), min(count, count - steps))
    return lax.ppermute(value, axis, [(source, source + steps) for source in range(leading, last)])


def normalise(values):
    average = jnp.mean(values, axis=-1, keepdims=True)
    centred = values - average
    variance = jnp.mean(centred * centred, axis=-1, keepdims=True)
    inverse = lax.rsqrt(variance + epsilon)
    return (centred * inverse, inverse)


def normalise_back(grad_out, unit, inverse, gain):
    grad_unit = grad_out * gain
    mean_grad = jnp.mean(grad_unit, axis=-1, keepdims=True)
    mean_cross = jnp.mean(grad_unit * unit, axis=-1, keepdims=True)
    return (grad_unit - mean_grad - unit * mean_cross) * inverse


def row(ref):
    return ref[...].reshape(1, -1)


def column_sums(values):
    return jnp.sum(values, axis=0, keepdims=True)


def accumulate(ref, update):
    step = pl.program_id(0)

    @pl.when(step == 0)
    def _():
        ref[...] = update

    @pl.when(step > 0)
    def _():
        ref[...] += update


def same(*shape):
    return pl.BlockSpec(shape, lambda *_: (0,) * len(shape))


class Moves:
    def __init__(self, sems):
        self.sems, self.made = sems, []

    def add(self, source, target):
        self.made.append((source, target, self.sems.at[len(self.made)]))
        return len(self.made) - 1

    def start(self, *which):
        for at in which:
            pltpu.make_async_copy(*self.made[at]).start()

    def wait(self, *which):
        for at in which:
            pltpu.make_async_copy(*self.made[at]).wait()


def rows_at(index, size):
    return pl.ds(pl.multiple_of(index * size, size), size)


def vmem():
    return pl.BlockSpec(memory_space=pltpu.VMEM)


def anywhere():
    return pl.BlockSpec(memory_space=pl.ANY)


def spread_slots(grid):
    blocks = grid.shape[0]
    slots = blocks * PICK
    wide = jnp.concatenate([jnp.broadcast_to(grid[s : s + 1, :], (PICK, grid.shape[1])) for s in range(blocks)], axis=0)
    lane = lax.broadcasted_iota(jnp.int32, wide.shape, 1)
    turn = lax.broadcasted_iota(jnp.int32, wide.shape, 0) % PICK
    return jnp.sum(jnp.where(lane == turn, wide, 0.0), axis=1, keepdims=True)


def project_kernel(
    steps, tokens_ref, picks_ref, quota_ref, gain_ref, shift_ref, joint_ref, query_bias_ref, value_bias_ref,
    score_weight_ref, normed_ref, q_ref, k_ref, v_ref, score_ref, rim_ref, sent_ref, gathered,
):
    step = pl.program_id(0)
    tile, width = tokens_ref.shape
    unit, _ = normalise(tokens_ref[...].astype(f32))
    normed = (unit * row(gain_ref) + row(shift_ref)).astype(bf16)
    normed_ref[...] = normed
    q_ref[...] = (nn(normed, joint_ref[:, :width]) + row(query_bias_ref)).astype(bf16)
    keys = nn(normed, joint_ref[:, width : 2 * width]).astype(bf16)
    values = (nn(normed, joint_ref[:, 2 * width :]) + row(value_bias_ref)).astype(bf16)
    score = nt(normed, score_weight_ref[...]).astype(bf16)
    heads = score.shape[1]
    k_ref[...] = keys
    v_ref[...] = values
    score_ref[...] = jnp.zeros_like(score_ref)
    score_ref[:, :heads] = score
    picks = spread_slots(picks_ref[...].astype(f32))
    slots = picks.shape[0]
    row_of = lax.broadcasted_iota(jnp.int32, (slots, tile), 1) + step * tile
    chosen = jnp.where(picks == row_of.astype(f32), 1.0, 0.0).astype(bf16)
    parts = ((0, keys), (width, values), (2 * width, normed), (3 * width, score_ref[...]))

    @pl.when(step == 0)
    def _():
        gathered[...] = jnp.zeros_like(gathered)

    for start, part in parts:
        gathered[:, start : start + part.shape[1]] += nn(chosen, part)

    @pl.when(step == steps - 1)
    def _():
        for start, part in parts:
            rim_ref[:, start : start + part.shape[1]] = part[tile - WIN :]
        sent_ref[...] = gathered[...].astype(bf16)
        lane = lax.broadcasted_iota(jnp.int32, (slots, LANES), 1)
        blocks = slots // PICK
        quota = jnp.broadcast_to(quota_ref[...].astype(f32), (slots, blocks))
        block_of = lax.broadcasted_iota(jnp.int32, (slots, blocks), 0) // PICK
        taken = jnp.where(lax.broadcasted_iota(jnp.int32, (slots, blocks), 1) == block_of, quota, 0.0)
        taken = jnp.sum(taken, axis=1, keepdims=True)
        turn = (lax.broadcasted_iota(jnp.int32, (slots, 1), 0) % PICK).astype(f32)
        live = jnp.where(turn < taken, 1.0, 0.0)
        high = jnp.floor(picks * (1.0 / DIGIT))
        coded = jnp.where(lane == heads, high, jnp.where(lane == heads + 1, picks - high * DIGIT, live))
        sent_ref[:, 3 * width :] = jnp.where(
            (lane >= heads) & (lane < heads + 3), coded, gathered[:, 3 * width :]
        ).astype(bf16)


def tiled(*shape):
    return pl.BlockSpec(shape, lambda r, *_: (r,) + (0,) * (len(shape) - 1))


def project(tokens, picks, quota, gain, shift, joint, query_bias, value_bias, score_weight, tile=256):
    rows, width = tokens.shape
    slots = picks.shape[0] * picks.shape[1]
    channels = 3 * width + LANES
    steps = rows // tile
    S = jax.ShapeDtypeStruct
    return launch(
        functools.partial(project_kernel, steps),
        "project", 10, (steps,),
        [
            tiled(tile, width), same(*picks.shape), same(*quota.shape), same(width), same(width), same(*joint.shape),
            same(width), same(width), same(*score_weight.shape),
        ],
        [tiled(tile, width)] * 4 + [tiled(tile, LANES), same(WIN, channels), same(slots, channels)],
        [S((rows, width), bf16)] * 4 + [S((rows, LANES), bf16), S((WIN, channels), bf16), S((slots, channels), bf16)],
        [pltpu.VMEM((slots, channels), f32)], 24,
        (tokens, picks, quota, gain, shift, joint, query_bias, value_bias, score_weight),
    )


def far_positions(far_score, heads, place_rows, blocks):
    wide = far_score.astype(f32)
    slot = lax.broadcasted_iota(jnp.int32, (far_score.shape[0], 1), 0)
    at = (wide[:, heads : heads + 1] * DIGIT + wide[:, heads + 1 : heads + 2]).astype(jnp.int32)
    return jnp.where(
        wide[:, heads + 2 : heads + 3] > 0.5, (slot // PICK) * place_rows + at, 2 * place_rows * blocks
    )


def load_block(group, place_ref, k_ref, v_ref, score_ref, rim_refs, far_refs, keys, values, gate_ref, head_size):
    rows, width = k_ref.shape
    rim_k_ref, rim_v_ref, rim_score_ref = rim_refs
    far_score_ref = far_refs[2]
    slots = far_score_ref.shape[0]
    keys[0:WIN, :] = rim_k_ref[...]
    keys[WIN:, :] = k_ref[...]
    values[0:WIN, :] = rim_v_ref[...]
    values[WIN:, :] = v_ref[...]
    gates_into(gate_ref, group, place_ref[0], score_ref, rim_score_ref, far_score_ref, head_size, rows, slots)


def attend_kernel(
    heads, head_size, unroll, place_ref, q_ref, k_ref, v_ref, score_ref,
    rim_k_ref, rim_v_ref, rim_score_ref, far_k_ref, far_v_ref, far_score_ref,
    mixed_ref, total_ref, keys, values, gate_ref,
):
    group = pl.program_id(0)
    place = place_ref[0]
    rows, width = q_ref.shape
    slots = far_k_ref.shape[0]
    load_block(
        group, place_ref, k_ref, v_ref, score_ref, (rim_k_ref, rim_v_ref, rim_score_ref),
        (far_k_ref, far_v_ref, far_score_ref), keys, values, gate_ref, head_size,
    )
    near_ok = near_bias(width)
    far_pos = jnp.broadcast_to(far_positions(far_score_ref[...], heads, rows, slots // PICK), (slots, LANES))

    @pl.loop(0, rows // WIN, unroll=unroll)
    def _(i):
        at = pl.ds(pl.multiple_of(i * WIN, WIN), WIN)
        span = pl.ds(pl.multiple_of(i * WIN, WIN), 2 * WIN)
        keys_cat = jnp.concatenate([keys[span, :], far_k_ref[...]], axis=0)
        values_cat = jnp.concatenate([values[span, :], far_v_ref[...]], axis=0)
        stack = stack_heads(q_ref[at, :], head_size, 1.0 / math.sqrt(head_size))
        logit = tile_logits(i, keys_cat, stack, gate_ref, far_pos, place, rows, near_ok)
        top = jnp.max(logit, axis=0, keepdims=True)
        power = jnp.exp(logit - top)
        total = jnp.sum(power, axis=0, keepdims=True)
        prob = (power * (1.0 / total)).astype(bf16)
        total_ref[0, pl.ds(i, 1), :] = top + jnp.log(total)
        mixed_ref[at, :] = pick_heads(tn(prob, values_cat), head_size).astype(bf16)


def far_specs(slots, width, groups):
    return [
        pl.BlockSpec((slots, width), lambda g: (0, g)),
        pl.BlockSpec((slots, width), lambda g: (0, groups + g)),
        pl.BlockSpec((slots, LANES), lambda g: (0, 3 * groups * width // LANES)),
    ]


def attend(place, q, k, v, score, rim, far, heads, unroll=8):
    rows, model = q.shape
    slots = far.shape[0]
    width = PACK * WIN
    groups = model // width
    cols = pl.BlockSpec((rows, width), lambda g: (0, g))
    return launch(
        functools.partial(attend_kernel, heads, WIN, unroll),
        "attend", 12, (groups,),
        [pl.BlockSpec(memory_space=pltpu.SMEM), cols, cols, cols, pl.BlockSpec((rows, LANES), lambda g: (0, 0))]
        + far_specs(WIN, width, groups) + far_specs(slots, width, groups),
        [cols, pl.BlockSpec((1, rows // WIN, width), lambda g: (g, 0, 0))],
        [
            jax.ShapeDtypeStruct((rows, model), bf16),
            jax.ShapeDtypeStruct((groups, rows // WIN, width), f32),
        ],
        [
            pltpu.VMEM((WIN + rows, width), bf16),
            pltpu.VMEM((WIN + rows, width), bf16),
            pltpu.VMEM((WIN + rows + slots, width), f32),
        ],
        32, (place, q, k, v, score, rim, rim, rim, far, far, far),
    )


class Block:
    def __init__(self, groups, loaded, k_h, v_h, score_h, rim_h, far_h, score_ref, keys, values, model, rows):
        self.loads = loads = Moves(loaded)
        slots, width = far_h.shape[0], keys.shape[2]
        self.near, self.own, self.far = pl.ds(0, WIN), pl.ds(WIN, rows), pl.ds(WIN + rows, slots)
        scores = pl.ds(3 * model, LANES)
        self.first = [
            loads.add(source, target)
            for source, target in (
                (score_h, score_ref.at[self.own, :]), (rim_h.at[:, scores], score_ref.at[self.near, :]),
                (far_h.at[:, scores], score_ref.at[self.far, :]),
            )
        ]
        self.second = []
        for at, group in enumerate(groups):
            cols, value_cols = pl.ds(group * width, width), pl.ds(model + group * width, width)
            self.second.append(
                [
                    loads.add(source, target)
                    for source, target in (
                        (k_h.at[:, cols], keys.at[at, self.own, :]), (rim_h.at[:, cols], keys.at[at, self.near, :]),
                        (far_h.at[:, cols], keys.at[at, self.far, :]), (v_h.at[:, cols], values.at[at, self.own, :]),
                        (rim_h.at[:, value_cols], values.at[at, self.near, :]),
                        (far_h.at[:, value_cols], values.at[at, self.far, :]),
                    )
                ]
            )

    def add(self, at, source, target):
        self.second[at].append(self.loads.add(source, target))


def gates_of(gate, spread, place, gate_ref):
    gate_ref[...] = sum(nn(part, spread) for part in three_parts(gate))
    gate_ref[0:WIN, :] = jnp.where(place == 0, very_low, gate_ref[0:WIN, :])


def attend_back_kernel(
    heads, head_size, unroll, groups, last, place_ref, q_h, k_h, v_h, grad_h, total_ref, score_h, rim_h, far_h, normed_h,
    *refs,
):
    refs = list(refs)
    earlier = [refs.pop(0) for _ in range(5)] if groups[0] else []
    beside_refs = [refs.pop(0) for _ in range(2)] if groups[0] else []
    dq_h, dk_h, dv_h, ds_ref, rim_out, far_out, rim_ds, far_ds, send, keep = refs[:10]
    q_ref, grad_ref, score_ref, dq_ref, keys, values, gate_refs, all_dkeys, all_dvalues, all_dscore, normed = refs[10:21]
    loaded, stored = refs[21:]
    model = normed.shape[1]
    place = place_ref[0]
    _, rows, width = q_ref.shape
    slots = far_h.shape[0]
    block = Block(groups, loaded, k_h, v_h, score_h, rim_h, far_h, score_ref, keys, values, model, rows)
    near, own, far, loads = block.near, block.own, block.far, block.loads
    for g, group in enumerate(groups):
        cols = pl.ds(group * width, width)
        block.add(g, q_h.at[:, cols], q_ref.at[g])
        block.add(g, grad_h.at[:, cols], grad_ref.at[g])
    normed_cols = pl.ds(2 * model, model)
    third = [
        loads.add(source, target)
        for source, target in (
            (normed_h, normed.at[own, :]), (rim_h.at[:, normed_cols], normed.at[near, :]),
            (far_h.at[:, normed_cols], normed.at[far, :]),
        )
    ]
    loads.start(*range(len(loads.made)))
    for ref in (all_dkeys, all_dvalues, all_dscore):
        ref[...] = jnp.zeros_like(ref)
    loads.wait(*block.first)
    gate = jax.nn.log_sigmoid(score_ref[...].astype(f32))
    near_ok = near_bias(width)
    far_pos = jnp.broadcast_to(far_positions(score_ref[far, :], heads, rows, slots // PICK), (slots, LANES))
    stores = Moves(stored)
    mine = place % 2
    half = model // 2
    start = 0
    if beside_refs:
        start = beside_refs[0].shape[1]
        send[:, :start] = beside_refs[0][...]
        keep[:, :start] = beside_refs[1][...]
        for out, old in zip((rim_out, far_out), earlier[:2]):
            out[...] = old[...]
    for g, group in enumerate(groups):
        gate_ref, dkeys, dvalues, dscore = (ref.at[g] for ref in (gate_refs, all_dkeys, all_dvalues, all_dscore))
        gather = head_spread(group, head_size, width)
        gates_of(gate, gather, place, gate_ref)
        loads.wait(*block.second[g])

        @pl.loop(0, rows // WIN, unroll=unroll)
        def _(i):
            at = pl.ds(pl.multiple_of(i * WIN, WIN), WIN)
            after = pl.ds(pl.multiple_of(i * WIN + WIN, WIN), WIN)
            span = pl.ds(pl.multiple_of(i * WIN, WIN), 2 * WIN)
            keys_cat = jnp.concatenate([keys[g, span, :], keys[g, far, :]], axis=0)
            values_cat = jnp.concatenate([values[g, span, :], values[g, far, :]], axis=0)
            stack = stack_heads(q_ref[g, at, :], head_size, 1.0 / math.sqrt(head_size))
            grad_stack = stack_heads(grad_ref[g, at, :], head_size, 1.0)
            logit = tile_logits(i, keys_cat, stack, gate_ref, far_pos, place, rows, near_ok)
            prob = jnp.exp(logit - total_ref[group, pl.ds(i, 1), :])
            grad_prob = nt(values_cat, grad_stack)
            delta = jnp.sum(prob * grad_prob, axis=0, keepdims=True)
            grad_logit = prob * (grad_prob - delta)
            low = grad_logit.astype(bf16)
            dq = pick_heads(tn(low, keys_cat), head_size) * (1.0 / math.sqrt(head_size))
            dq_ref[g, at, :] = dq.astype(bf16)
            for ref, update in (
                (dkeys, nn(low, stack)),
                (dvalues, nn(prob.astype(bf16), grad_stack)),
                (dscore, grad_logit),
            ):
                ref[at, :] += update[:WIN]
                ref[after, :] = update[WIN : 2 * WIN]
                ref[far, :] += update[2 * WIN :]

        to = pl.ds(g * width, width)
        for source, target in ((dq_ref.at[g], dq_h), (dkeys.at[own, :], dk_h), (dvalues.at[own, :], dv_h)):
            stores.start(stores.add(source, target.at[:, to]))
        if g == 0:
            loads.wait(*third)
        joint = jnp.concatenate(
            [tn(normed[own, :], dq_ref[g])]
            + [tn(normed[...], ref[...].astype(bf16)) for ref in (dkeys, dvalues)],
            axis=1,
        ).astype(bf16)
        top, low = joint[:half], joint[half:]
        span = slice(start + 3 * width * g, start + 3 * width * (g + 1))
        send[:, span] = jnp.where(mine == 0, low, top)
        keep[:, span] = jnp.where(mine == 0, top, low)
        for out, part in ((rim_out, near), (far_out, far)):
            for base, ref in ((0, dkeys), (model, dvalues)):
                out[:, base + group * width : base + (group + 1) * width] = ref[part, :].astype(bf16)
        for number, (out_ref, part) in enumerate(((rim_ds, near), (far_ds, far), (ds_ref, own))):
            sums = dscore[part, :]
            high = sums.astype(bf16)
            rest = (sums - high.astype(f32)).astype(bf16)
            update = (nt(high, gather) + nt(rest, gather)) * jax.nn.sigmoid(-score_ref[part, :].astype(f32))
            if g:
                out_ref[...] += update
            else:
                out_ref[...] = update + earlier[2 + number][...] if earlier else update
    if last:
        rim_out[:, 2 * model :] = rim_ds[...].astype(bf16)
        far_out[:, 2 * model :] = far_ds[...].astype(bf16)
    stores.wait(*range(len(stores.made)))


def attend_back(place, q, k, v, grad, total, score, rim, far, normed, heads, groups, earlier, joined, after=(), unroll=4):
    rows, model = q.shape
    slots = far.shape[0]
    width = PACK * WIN
    count = len(groups)
    channels = 2 * model + LANES
    S = jax.ShapeDtypeStruct
    half = (model // 2, 3 * width * count + (joined[0].shape[1] if joined else 0))
    ext = WIN + rows + slots
    V = pltpu.VMEM
    out = launch(
        functools.partial(attend_back_kernel, heads, WIN, unroll, groups, groups[-1] == model // width - 1),
        "attend_back", 13 * count, (),
        [pl.BlockSpec(memory_space=pltpu.SMEM)] + [anywhere()] * 4 + [vmem()] + [anywhere()] * 4
        + [vmem()] * (len(earlier) + len(joined)),
        [anywhere()] * 3 + [vmem()] * 7,
        [
            S((rows, count * width), bf16), S((rows, count * width), f32), S((rows, count * width), f32),
            S((rows, LANES), f32), S((WIN, channels), bf16), S((slots, channels), bf16), S((WIN, LANES), f32),
            S((slots, LANES), f32),
        ] + [S(half, bf16)] * 2,
        [
            V((count, rows, width), bf16), V((count, rows, width), bf16), V((ext, LANES), bf16),
            V((count, rows, width), bf16), V((count, ext, width), bf16), V((count, ext, width), bf16),
        ] + [V((count, ext, width), f32)] * 4
        + [
            V((ext, model), bf16), pltpu.SemaphoreType.DMA((6 + 8 * count,)), pltpu.SemaphoreType.DMA((3 * count,)),
        ],
        32 if count == 1 else 44,
        (place, q, k, v, grad, total, score, rim, far, normed, *earlier, *joined), after,
    )
    dq, dk, dv, ds, rim_out, far_out, rim_ds, far_ds, send, keep, token = out
    return (dq, dk, dv), (rim_out, far_out, rim_ds, far_ds, ds), (send, keep), token


cubic = 0.044715
root = 0.7978845608028654


def feed_kernel(
    tile, pieces, block, mine_ref, mixed_h, tokens_h, cot_h, out_weight_h, expand_h, reduce_h, out_bias_ref, gain_ref,
    shift_ref, expand_bias_ref,
    resid_h, hidden_h, grad_pre_h, sums_ref, send_one, keep_one, send_two, keep_two,
    mixed, tokens, cot, out_weight, expand, reduce, resids, normed, hidden, grad_pre, one, two, loaded, stored,
):
    rows, width = cot.shape
    inner = expand.shape[1]
    span = inner // pieces
    steps = rows // tile
    mine = mine_ref[0]
    loads = Moves(loaded)
    first = [loads.add(*pair) for pair in ((mixed_h, mixed), (out_weight_h, out_weight), (tokens_h, tokens))]
    second = loads.add(cot_h, cot)
    parts = []
    for piece in range(pieces):
        at = pl.ds(piece * span, span)
        parts.append(
            (loads.add(expand_h.at[:, at], expand.at[:, at]), loads.add(reduce_h.at[at, :], reduce.at[at, :]))
        )
    loads.start(*range(len(loads.made)))

    def store(number, source, target):
        return pltpu.make_async_copy(source, target, stored.at[number])

    def tile_stores(step):
        here = rows_at(step, tile)
        return [
            store(3 * step + at, source.at[here, :], target.at[here, :])
            for at, (source, target) in enumerate(((resids, resid_h), (hidden, hidden_h), (grad_pre, grad_pre_h)))
        ]

    def feed_tile(step, leading):
        here = rows_at(step, tile)
        if leading:
            loads.wait(*first)
        resid = tokens[here, :].astype(f32) + nn(mixed[here, :], out_weight[...]) + row(out_bias_ref)
        resids[here, :] = resid
        unit, _ = normalise(resid)
        low = (unit * row(gain_ref) + row(shift_ref)).astype(bf16)
        normed[here, :] = low
        if leading:
            loads.wait(second)
        sums = []
        for piece in range(pieces):
            at = slice(piece * span, (piece + 1) * span)
            if leading:
                loads.wait(*parts[piece])
            pre = nn(low, expand[:, at]) + row(expand_bias_ref)[:, at]
            back = nt(cot[here, :], reduce[at, :])
            squared = pre * pre
            half = 0.5 + 0.5 * jnp.tanh(pre * (root + root * cubic * squared))
            active = pre * half
            slope = half + (active - active * half) * (2.0 * root + 6.0 * root * cubic * squared)
            hidden[here, at] = active.astype(bf16)
            grad = (back * slope).astype(bf16)
            grad_pre[here, at] = grad
            sums.append(column_sums(grad.astype(f32)))
        total = jnp.concatenate(sums, axis=0)
        if leading:
            sums_ref[...] = total
        else:
            sums_ref[...] += total
        for copy in tile_stores(step):
            copy.start()

    feed_tile(0, True)

    @pl.loop(1, steps)
    def _(step):
        feed_tile(step, False)

    base = 3 * steps
    count = inner // 2 // block
    half = width // 2

    def one_store(turn, j):
        here = rows_at(j, block)
        target = (send_one, keep_one)[turn]
        return store(base + turn * count + j, one.at[turn, here, :], target.at[here, :])

    def two_store(turn):
        return store(base + 2 * count + turn, two.at[turn], (send_two, keep_two)[turn])

    for turn in range(2):
        side_of = (1 - mine) if turn == 0 else mine

        @pl.loop(0, count)
        def _(j):
            one[turn, rows_at(j, block), :] = tn(hidden[:, rows_at(side_of * count + j, block)], cot[...]).astype(bf16)
            one_store(turn, j).start()

    for turn in range(2):
        side_of = (1 - mine) if turn == 0 else mine
        two[turn] = tn(normed[:, rows_at(side_of, half)], grad_pre[...]).astype(bf16)
        two_store(turn).start()

    @pl.loop(0, steps)
    def _(step):
        for copy in tile_stores(step):
            copy.wait()

    for turn in range(2):
        @pl.loop(0, count)
        def _(j):
            one_store(turn, j).wait()

        two_store(turn).wait()


def feed(
    mine, mixed, tokens, cot, out_weight, out_bias, gain, shift, expand, expand_bias, reduce, tile=512, block=512,
):
    rows, width = tokens.shape
    inner = expand.shape[1]
    steps, pieces = rows // tile, inner // width
    S = jax.ShapeDtypeStruct
    B = pltpu.VMEM
    return launch(
        functools.partial(feed_kernel, tile, pieces, block),
        "feed", 33, (),
        [anywhere()] * 6 + [vmem()] * 4,
        [anywhere()] * 3 + [vmem()] + [anywhere()] * 4,
        [
            S((rows, width), f32), S((rows, inner), bf16), S((rows, inner), bf16), S((pieces, inner // pieces), f32),
            S((inner // 2, width), bf16), S((inner // 2, width), bf16),
            S((width // 2, inner), bf16), S((width // 2, inner), bf16),
        ],
        [
            B((rows, width), bf16), B((rows, width), bf16), B((rows, width), bf16), B((width, width), bf16),
            B((width, inner), bf16), B((inner, width), bf16), B((rows, width), f32), B((rows, width), bf16),
            B((rows, inner), bf16), B((rows, inner), bf16), B((2, inner // 2, width), bf16), B((2, width // 2, inner), bf16),
            pltpu.SemaphoreType.DMA((4 + 2 * pieces,)),
            pltpu.SemaphoreType.DMA((3 * steps + inner // block + 2,)),
        ],
        60, (mixed, tokens, cot, out_weight, expand, reduce, out_bias, gain, shift, expand_bias), (), (mine,),
    )


def feed_back_kernel(
    tile, pieces, mine_ref, grad_pre_h, resid_h, cot_h, mixed_h, expand_h, out_weight_h, gain_ref,
    grad_resid_h, grad_mixed_h, sums_ref, send_h, keep_h,
    grad_pre, resid, cot, mixed, expand, out_weight, grad_attn, grad_mixed, three, loaded, stored,
):
    rows, width = cot.shape
    inner = expand.shape[1]
    span = inner // pieces
    steps = rows // tile
    half = width // 2
    mine = mine_ref[0]
    loads = Moves(loaded)

    def tile_load(step):
        return [
            loads.add(source.at[rows_at(step, tile), :], target.at[rows_at(step, tile), :])
            for source, target in ((grad_pre_h, grad_pre), (resid_h, resid), (cot_h, cot))
        ]

    tiles = [tile_load(0)]
    weights = [
        loads.add(expand_h.at[:, pl.ds(piece * span, span)], expand.at[:, pl.ds(piece * span, span)])
        for piece in range(pieces)
    ]
    late = loads.add(out_weight_h, out_weight)
    tiles += [tile_load(step) for step in range(1, steps)]
    last = loads.add(mixed_h, mixed)
    loads.start(*range(len(loads.made)))
    stores = Moves(stored)
    sums = []

    def first_part(step):
        here = rows_at(step, tile)
        grad_normed = jnp.zeros((tile, width), f32)
        for piece in range(pieces):
            at = slice(piece * span, (piece + 1) * span)
            if step == 0:
                loads.wait(weights[piece])
            grad_normed = grad_normed + nt(grad_pre[here, at], expand[:, at])
        return grad_normed

    def second_part(step, grad_normed):
        here = rows_at(step, tile)
        wide = cot[here, :].astype(f32)
        unit, inverse = normalise(resid[here, :])
        grad_resid = wide + normalise_back(grad_normed, unit, inverse, row(gain_ref))
        resid[here, :] = grad_resid
        low = grad_resid.astype(bf16)
        grad_attn[here, :] = low
        grad_mixed[here, :] = nt(low, out_weight[...]).astype(bf16)
        sums.append(
            jnp.concatenate(
                [
                    column_sums(low.astype(f32)),
                    column_sums(grad_normed * unit),
                    column_sums(grad_normed),
                    column_sums(wide),
                ],
                axis=0,
            )
        )

    loads.wait(*tiles[0])
    before = first_part(0)
    loads.wait(late, *tiles[1])
    ahead = first_part(1)
    second_part(0, before)
    loads.wait(last, *[at for tile_loads in tiles[2:] for at in tile_loads])
    for step in range(2, steps + 1):
        before, ahead = ahead, first_part(step) if step < steps else None
        second_part(step - 1, before)
    sums_ref[...] = sum(sums)
    for step in range(steps):
        here = rows_at(step, tile)
        stores.start(
            stores.add(resid.at[here, :], grad_resid_h.at[here, :]),
            stores.add(grad_mixed.at[here, :], grad_mixed_h.at[here, :]),
        )
    for turn in range(2):
        side_of = (1 - mine) if turn == 0 else mine
        three[turn] = tn(mixed[:, rows_at(side_of, half)], grad_attn[...]).astype(bf16)
        stores.start(stores.add(three.at[turn], (send_h, keep_h)[turn]))
    stores.wait(*range(len(stores.made)))


def feed_back(mine, grad_pre, resid, cot, mixed, expand, out_weight, gain, tile=256, pieces=4):
    rows, width = resid.shape
    inner = expand.shape[1]
    steps = rows // tile
    S = jax.ShapeDtypeStruct
    B = pltpu.VMEM
    return launch(
        functools.partial(feed_back_kernel, tile, pieces), "feed_back", 12, (),
        [anywhere()] * 6 + [vmem()],
        [anywhere()] * 2 + [vmem()] + [anywhere()] * 2,
        [
            S((rows, width), f32), S((rows, width), bf16), S((4, width), f32),
            S((width // 2, width), bf16), S((width // 2, width), bf16),
        ],
        [
            B((rows, inner), bf16), B((rows, width), f32), B((rows, width), bf16), B((rows, width), bf16),
            B((width, inner), bf16), B((width, width), bf16), B((rows, width), bf16), B((rows, width), bf16),
            B((2, width // 2, width), bf16),
            pltpu.SemaphoreType.DMA((3 * steps + pieces + 2,)),
            pltpu.SemaphoreType.DMA((2 * steps + 2,)),
        ],
        44, (grad_pre, resid, cot, mixed, expand, out_weight, gain), (), (mine,),
    )


def finish_kernel(resid_ref, hidden_ref, reduce_ref, bias_ref, out_ref):
    out_ref[...] = (resid_ref[...] + nn(hidden_ref[...], reduce_ref[...]) + row(bias_ref)).astype(bf16)


def finish(resid, hidden, reduce, bias, after=(), tile=256):
    rows, width = resid.shape
    inner = reduce.shape[0]
    return launch(
        finish_kernel, "finish", 7, (rows // tile,),
        [tiled(tile, width), tiled(tile, inner), same(inner, width), same(width)],
        [tiled(tile, width)], [jax.ShapeDtypeStruct((rows, width), bf16)],
        [], 26, (resid, hidden, reduce, bias), after,
    )


def beside(refs):
    return jnp.concatenate([ref[...] for ref in refs], axis=1)


def join_kernel(
    steps, groups, tokens_ref, resid_ref, ds_ref, rim_ref, far_ref, picks_ref, gain_ref, shift_ref,
    joint_ref, score_weight_ref, sums_two_ref, expand_sums_ref, *refs,
):
    dq_refs, dk_refs, dv_refs = (refs[at * groups : (at + 1) * groups] for at in range(3))
    token_ref, small_ref = refs[3 * groups :]
    step = pl.program_id(0)
    tile, width = tokens_ref.shape
    heads = score_weight_ref.shape[0]
    unit, inverse = normalise(tokens_ref[...].astype(f32))
    gain = row(gain_ref)
    normed = (unit * gain + row(shift_ref)).astype(bf16)
    picks = spread_slots(picks_ref[...].astype(f32))
    row_of = lax.broadcasted_iota(jnp.int32, (picks.shape[0], tile), 1) + step * tile
    chosen = jnp.where(picks == row_of.astype(f32), 1.0, 0.0).astype(bf16)
    at_end = jnp.where(step == steps - 1, 1.0, 0.0)

    def whole(own, start):
        span = own.shape[1]
        total = own + tn(chosen, far_ref[:, start : start + span])
        rim = rim_ref[:, start : start + span].astype(f32) * at_end
        return jnp.concatenate([total[: tile - WIN], total[tile - WIN :] + rim], axis=0).astype(bf16)

    dq = beside(dq_refs)
    dk = whole(beside(dk_refs), 0)
    dv = whole(beside(dv_refs), width)
    ds = whole(ds_ref[...], 2 * width)
    grad_normed = (
        nt(dq, joint_ref[:, :width])
        + nt(dk, joint_ref[:, width : 2 * width])
        + nt(dv, joint_ref[:, 2 * width :])
        + nn(ds[:, :heads], score_weight_ref[...])
    )
    token_ref[...] = resid_ref[...] + normalise_back(grad_normed, unit, inverse, gain)
    sums = jnp.concatenate(
        [
            column_sums(grad_normed * unit),
            column_sums(grad_normed),
            column_sums(dq.astype(f32)),
            column_sums(dv.astype(f32)),
        ],
        axis=0,
    )
    score_grad = tn(ds, normed)[:heads]
    past = 8 + expand_sums_ref.shape[0]

    @pl.when(step == 0)
    def _():
        small_ref[0:4, :] = sums
        small_ref[4:8, :] = sums_two_ref[...]
        small_ref[8:past, :] = expand_sums_ref[...]
        small_ref[past : past + heads, :] = score_grad

    @pl.when(step > 0)
    def _():
        small_ref[0:4, :] += sums
        small_ref[past : past + heads, :] += score_grad


def join(
    tokens, resid, dqs, dks, dvs, ds, rim, far, picks, gain, shift, joint, score_weight, sums_two, expand_sums, after=(),
    tile=256,
):
    rows, width = tokens.shape
    heads = score_weight.shape[0]
    count = 8 + expand_sums.shape[0] + heads
    S = jax.ShapeDtypeStruct
    return launch(
        functools.partial(join_kernel, rows // tile, len(dqs)), "join", 14, (rows // tile,),
        [tiled(tile, width)] * 2 + [
            tiled(tile, LANES), same(*rim.shape), same(*far.shape), same(*picks.shape), same(width), same(width),
            same(*joint.shape), same(*score_weight.shape), same(*sums_two.shape), same(*expand_sums.shape),
        ] + [tiled(tile, part.shape[1]) for part in (*dqs, *dks, *dvs)],
        [tiled(tile, width), same(count, width)],
        [S((rows, width), f32), S((count, width), f32)],
        [], 28, (tokens, resid, ds, rim, far, picks, gain, shift, joint, score_weight, sums_two, expand_sums, *dqs, *dks, *dvs), after,
    )


def swap(value, axis, bit):
    count = lax.axis_size(axis)
    return lax.ppermute(value, axis, [(i, i ^ bit) for i in range(count)])


def side(axis, bit):
    return (lax.axis_index(axis) // bit) % 2


def axis_bits(axis):
    count, bits, bit = lax.axis_size(axis), [], 1
    while bit < count:
        bits.append((axis, bit))
        bit *= 2
    return bits


def woven(*lists):
    result = []
    for step in range(max(map(len, lists))):
        for items in lists:
            result += items[step : step + 1]
    return result


def orders():
    near, far = axis_bits("seq"), axis_bits("dp")
    first, rest = near[:1], near[1:]
    return (
        first + rest + far,
        first + woven(rest[::-1], far),
        first + woven(far, rest),
    )


def cut(value, pieces):
    return value.reshape(pieces, value.shape[0] // pieces, value.shape[1])


class Chain:
    def __init__(self, send, keep, order):
        self.order, self.level, self.down, self.held = order, 0, True, True
        half = 2 ** (len(order) - 1)
        self.send, self.keep = cut(send, half), cut(keep, half)
        self.mine = [side(*where).astype(jnp.int32) for where in order]

    def got(self):
        return swap(self.send, *self.order[self.level])


def added(one, two):
    return (one[...].astype(f32) + two[...].astype(f32)).astype(bf16)


class Total:
    def __init__(self, value, order):
        self.send, self.order, self.level = value, order, 0

    def got(self):
        return swap(self.send, *self.order[self.level])


def advance_kernel(plan, bits_ref, *refs):
    refs = list(refs)
    outs = refs[sum(4 if kind == "split" else 2 for kind in plan) :]
    for kind in plan:
        if kind == "split":
            for _ in range(2):
                outs.pop(0)[...] = added(refs.pop(0), refs.pop(0))
        elif kind == "sum":
            outs.pop(0)[...] = refs.pop(0)[...] + refs.pop(0)[...]
        elif kind == "close":
            outs.pop(0)[...] = added(refs.pop(0), refs.pop(0))
        else:
            out = outs.pop(0)
            for which in range(2):
                out[which] = refs.pop(0)[...]


def advance(chains, after=(), hold=False):
    held = []
    plan, operands, in_specs, out_specs, shapes, bits, free = [], [], [], [], [], [], []
    depth = len(chains[0].order)
    for chain in chains:
        if isinstance(chain, Total):
            plan.append("sum")
            continue
        last = chain.down and chain.level == depth - 1
        plan.append("close" if last else "split" if chain.down else "stack")
    sizes = [chain.send.shape[0] // (2 if kind == "split" else 1) for chain, kind in zip(chains, plan)]
    steps = min([4] + [size for size, kind in zip(sizes, plan) if kind != "sum"])
    S = jax.ShapeDtypeStruct

    def half_of(which, other, block, tail):
        def index(g, bits_ref):
            mine = bits_ref[which]
            return ((1 - mine if other else mine) * steps + g, 0, 0)

        return pl.BlockSpec((block,) + tail, index)

    for chain, kind, size in zip(chains, plan, sizes):
        got, tail = chain.got(), chain.send.shape[1:]
        block = size // steps
        if kind == "sum":
            free += [len(operands), len(operands) + 1]
            operands += [chain.send, got]
            in_specs += [same(*chain.send.shape)] * 2
            out_specs += [same(*chain.send.shape)]
            shapes += [S(chain.send.shape, f32)]
        elif kind == "split":
            which = len(bits)
            bits.append(chain.mine[chain.level + 1])
            places = len(operands)
            free += [places + 1, places + 3] if chain.held else range(places, places + 4)
            chain.held = hold
            held += [len(shapes) + 1] if hold else []
            for other in (True, False):
                operands += [chain.keep, got]
                in_specs += [half_of(which, other, block, tail)] * 2
            out_specs += [tiled(block, *tail)] * 2
            shapes += [S((size,) + tail, bf16)] * 2
        elif kind == "close":
            free += [len(operands) + 1] if chain.held else [len(operands), len(operands) + 1]
            operands += [chain.keep, got]
            in_specs += [tiled(block, *tail)] * 2
            out_specs += [tiled(block, *tail)]
            shapes += [S((size,) + tail, bf16)]
        else:
            free += [len(operands), len(operands) + 1]
            operands += [chain.send, got]
            in_specs += [tiled(block, *tail)] * 2
            out_specs += [pl.BlockSpec((2, block) + tail, lambda g, *_: (0, g, 0, 0))]
            shapes += [S((2, size) + tail, bf16)]
    bits = jnp.stack(bits) if bits else jnp.zeros((1,), jnp.int32)
    outs = launch(
        functools.partial(advance_kernel, plan), "advance", 2, (steps,), in_specs, out_specs, shapes, [], 20, operands,
        after, (bits,), free, None, held,
    )
    for chain, kind in zip(chains, plan):
        if kind == "split":
            chain.send, chain.keep = outs[:2]
            chain.level += 1
            outs = outs[2:]
        elif kind == "sum":
            chain.send = outs[0]
            chain.level += 1
            outs = outs[1:]
        else:
            chain.send = outs[0].reshape((-1,) + chain.send.shape[1:])
            outs = outs[1:]
            if kind == "close":
                chain.down = False
            else:
                chain.level -= 1
    return outs[0]


def finished(chain):
    if isinstance(chain, Total):
        return chain.level == len(chain.order)
    return not chain.down and chain.level == 0


def ends(chain):
    return chain.send, chain.got()


def own_place(order):
    place = 0
    for axis, bit in order:
        place = place * 2 + side(axis, bit)
    return place.astype(jnp.int32).reshape(1)


def widen_half(own, chain, half_of, into=(), after=()):
    value, other = half_of
    half, size, n = value.shape
    count, group = 2 * half, 4

    def side_of(own_ref):
        mine = own_ref[0] // half
        return 1 - mine if other else mine

    def kernel(own_ref, value_ref, *refs):
        out_ref = refs[-1]
        for i in range(group):
            out_ref[i] = value_ref[jnp.bitwise_xor(own_ref[0] % group, i)].astype(f32)

    out, token = launch(
        kernel, "widen", 4, (half // group,),
        [pl.BlockSpec((group, size, n), lambda s, own_ref: (jnp.bitwise_xor(own_ref[0] % half // group, s), 0, 0))]
        + [anywhere()] * len(into),
        [pl.BlockSpec((group, size, n), lambda s, own_ref: (side_of(own_ref) * (half // group) + s, 0, 0))],
        [jax.ShapeDtypeStruct((count, size, n), f32)],
        [], 24, (value, *into), after, (own,), (0,), {2: 0} if into else None,
    )
    return out, token


def widen_joint_half(owns, values, other, into=(), after=()):
    half, size, n = values[0].shape
    count, group, model, width = 2 * half, 4, n // 2, PACK * WIN

    def side_of(own_ref):
        mine = own_ref[0] // half
        return 1 - mine if other else mine

    def kernel(own_one_ref, own_two_ref, one_ref, two_ref, *refs):
        joint_ref, first_ref = refs[-2:]
        for i in range(group):
            one = one_ref[jnp.bitwise_xor(own_one_ref[0] % group, i)].astype(f32)
            two = two_ref[jnp.bitwise_xor(own_two_ref[0] % group, i)].astype(f32)
            first_ref[i] = two[:, :model]
            for piece, start, g in ((one, 0, 0), (one, 3 * width, 1), (two, model, 2)):
                for kind in range(3):
                    to = kind * model + g * width
                    joint_ref[i, :, to : to + width] = piece[:, start + kind * width : start + (kind + 1) * width]

    def read(which):
        def index(s, *own_refs):
            return (jnp.bitwise_xor(own_refs[which][0] % half // group, s), 0, 0)

        return pl.BlockSpec((group, size, n), index)

    def write(columns):
        return pl.BlockSpec((group, size, columns), lambda s, own_ref, _: (side_of(own_ref) * (half // group) + s, 0, 0))

    S = jax.ShapeDtypeStruct
    joint, first, token = launch(
        kernel, "widen_joint", 4, (half // group,),
        [read(0), read(1)] + [anywhere()] * len(into), [write(3 * model), write(model)],
        [S((count, size, 3 * model), f32), S((count, size, model), f32)],
        [], 24, (*values, *into), after, tuple(owns), (0, 1), {4: 0, 5: 1} if into else None,
    )
    return (joint, first), token


def per_device(
    tokens, cotangent, first_gain, first_shift, joint_weight, query_bias, value_bias, score_weight, out_weight, out_bias,
    second_gain, second_shift, expand_weight, expand_bias, reduce_weight, reduce_bias, picks, quota,
):
    rows, width = tokens.shape[1:]
    heads = score_weight.shape[1]
    inner = expand_weight.shape[1]
    blocks = lax.axis_size("seq")
    slots = blocks * PICK
    here = lax.axis_index("seq").astype(jnp.int32).reshape(1)
    first, second, _ = orders()
    mine = side(*first[0]).astype(jnp.int32).reshape(1)
    inputs, grad_out = tokens[0], cotangent[0]
    chosen, turned = picks[0, 0], score_weight.T
    normed, q, k, v, score, rim_sent, sent, _ = project(
        inputs, chosen, quota[0], first_gain, first_shift, joint_weight, query_bias, value_bias, turned
    )
    rim = passed_along(rim_sent, "seq", 1)
    far = lax.all_to_all(
        sent.reshape(blocks, PICK, -1), "seq", split_axis=0, concat_axis=0, tiled=True
    ).reshape(slots, -1)
    mixed, total, _ = attend(here, q, k, v, score, rim, far, heads)
    resid, hidden, grad_pre, expand_sums, *halves, _ = feed(
        mine, mixed, inputs, grad_out, out_weight, out_bias, second_gain, second_shift, expand_weight, expand_bias,
        reduce_weight,
    )
    reduced, expanded = Chain(*halves[:2], first), Chain(*halves[2:], second)
    grad_resid, grad_mixed, sums_two, *out_halves, stage = feed_back(
        mine, grad_pre, resid, grad_out, mixed, expand_weight, out_weight, second_gain
    )
    big = [reduced, expanded]
    back = functools.partial(attend_back, here, q, k, v, grad_mixed, total, score, rim, far, normed, heads)
    stage = advance(big, (stage,))
    grads_one, carried, joined, stage = back((0, 1), (), (), (stage,))
    one = Chain(*joined, first)
    stage = advance(big, (stage,), True)
    grads_two, carried, joined, stage = back((2,), carried, tuple(out_halves), (stage,))
    two = Chain(*joined, second)
    rim_grad, far_grad, _, _, ds = carried
    rim_back = passed_along(rim_grad, "seq", -1)
    far_back = lax.all_to_all(
        far_grad.reshape(blocks, PICK, -1), "seq", split_axis=0, concat_axis=0, tiled=True
    ).reshape(slots, -1)
    dqs, dks, dvs = zip(grads_one, grads_two)
    stage = advance(big + [one], (stage,), True)
    stage = advance(big + [two], (stage,), True)
    token_grad, small, stage = join(
        inputs, grad_resid, dqs, dks, dvs, ds, rim_back, far_back, chosen, first_gain, first_shift, joint_weight, turned,
        sums_two, expand_sums, (stage,),
    )
    small = Total(small, first)
    late = [one, two]
    stage = advance(big + late, (stage,))
    layer_out, stage = finish(resid, hidden, reduce_weight, reduce_bias, (stage,))
    for chains in (
        big + late + [small], big + late + [small], big + late + [small], late + [small], late + [small],
    ):
        stage = advance([chain for chain in chains if not finished(chain)], (stage,))
    while not finished(reduced):
        stage = advance([chain for chain in big + late if not finished(chain)], (stage,))
    own_first, own_second = own_place(first), own_place(second)
    halves_one, halves_two = ends(reduced), ends(expanded)
    reduce_weight_grad, stage = widen_half(own_first, reduced, (halves_one[0], False), (), (stage,))
    expand_weight_grad, stage = widen_half(own_second, expanded, (halves_two[0], False), (), (stage,))
    reduce_weight_grad, stage = widen_half(own_first, reduced, (halves_one[1], True), (reduce_weight_grad,), (stage,))
    expand_weight_grad, stage = widen_half(own_second, expanded, (halves_two[1], True), (expand_weight_grad,), (stage,))
    while not (finished(one) and finished(two)):
        stage = advance([chain for chain in late if not finished(chain)], (stage,))
    while not finished(small):
        stage = advance([small], (stage,))
    halves_one, halves_two = ends(one), ends(two)
    owns = (own_first, own_second)
    both, stage = widen_joint_half(owns, (halves_one[0], halves_two[0]), False, (), (stage,))
    both, stage = widen_joint_half(owns, (halves_one[1], halves_two[1]), True, both, (stage,))
    reduce_weight_grad = reduce_weight_grad.reshape(inner, width)
    expand_weight_grad = expand_weight_grad.reshape(width, inner)
    joint_weight_grad, out_weight_grad = both[0].reshape(width, 3 * width), both[1].reshape(width, width)
    small = small.send
    gain_one, shift_one, query_sum, value_sum, out_sum, gain_two, shift_two, reduce_sum = (small[i] for i in range(8))
    past = 8 + inner // width
    return (
        layer_out[None],
        token_grad[None],
        gain_one,
        shift_one,
        joint_weight_grad,
        query_sum,
        value_sum,
        small[past : past + heads].T,
        out_weight_grad,
        out_sum,
        gain_two,
        shift_two,
        expand_weight_grad,
        small[8:past].reshape(inner),
        reduce_weight_grad,
        reduce_sum,
    )


def solution(mesh):
    placed = (
        P("dp", "seq", None),
        P("dp", "seq", None),
        P(),
        P(),
        P(),
        P(),
        P(),
        P(),
        P(),
        P(),
        P(),
        P(),
        P(),
        P(),
        P(),
        P(),
        P("dp", "seq", None, None),
        P("dp", "seq", None),
    )
    return jax.shard_map(
        per_device,
        mesh=mesh,
        in_specs=placed,
        out_specs=(
            P("dp", "seq", None),
            P("dp", "seq", None),
            P(),
            P(),
            P(),
            P(),
            P(),
            P(),
            P(),
            P(),
            P(),
            P(),
            P(),
            P(),
            P(),
            P(),
        ),
        check_vma=False,
    )
```

```python
import functools
import math

import jax
import jax.numpy as jnp
from jax import lax
from jax.experimental import pallas as pl
from jax.experimental.pallas import tpu as pltpu
from jax.sharding import PartitionSpec as P

WIN = 64
PICK = 8
LANES = 128
PACK = 4
DIGIT = 32
TOKEN = (8, 128)
epsilon = 1e-05
very_low = -1e30
bf16 = jnp.bfloat16
f32 = jnp.float32


def nt(left, right):
    return lax.dot_general(left, right, (((1,), (1,)), ((), ())), preferred_element_type=f32)


def tn(left, right):
    return lax.dot_general(left, right, (((0,), (0,)), ((), ())), preferred_element_type=f32)


def nn(left, right):
    return jnp.dot(left, right, preferred_element_type=f32)


def three_parts(value):
    high = value.astype(bf16)
    rest = value - high.astype(f32)
    middle = rest.astype(bf16)
    low = (rest - middle.astype(f32)).astype(bf16)
    return high, middle, low


def head_spread(group, head_size, width):
    row = lax.broadcasted_iota(jnp.int32, (LANES, width), 0)
    lane = lax.broadcasted_iota(jnp.int32, (LANES, width), 1)
    return jnp.where(row == group * PACK + lane // WIN, 1.0, 0.0).astype(bf16)


def stack_heads(tile, head_size, factor):
    width = tile.shape[1]
    lane = lax.broadcasted_iota(jnp.int32, tile.shape, 1) // head_size
    scaled = tile * jnp.asarray(factor, tile.dtype)
    zero = jnp.zeros_like(scaled)
    return jnp.concatenate([jnp.where(lane == h, scaled, zero) for h in range(PACK)], axis=0)


def pick_heads(full, head_size):
    lane = lax.broadcasted_iota(jnp.int32, (WIN, full.shape[1]), 1) // head_size
    out = full[0:WIN]
    for h in range(1, PACK):
        out = jnp.where(lane == h, full[h * WIN : (h + 1) * WIN], out)
    return out


def gates_into(gate_ref, group, place, score_ref, rim_score_ref, far_score_ref, head_size, rows, slots):
    width = PACK * WIN
    spread = head_spread(group, head_size, width)

    def expand(score):
        gate = jax.nn.log_sigmoid(score.astype(f32))
        return sum(nn(part, spread) for part in three_parts(gate))

    gate_ref[0:WIN, :] = jnp.where(place == 0, very_low, expand(rim_score_ref[...]))
    gate_ref[WIN : WIN + rows, :] = expand(score_ref[...])
    gate_ref[WIN + rows :, :] = expand(far_score_ref[...])


def near_bias(width):
    key = lax.broadcasted_iota(jnp.int32, (2 * WIN, width), 0)
    query = lax.broadcasted_iota(jnp.int32, (2 * WIN, width), 1) % WIN
    return (key <= query + WIN) & (key > query)


def tile_logits(i, keys_cat, query_stack, gate_ref, far_pos, place, rows, near_ok):
    width = PACK * WIN
    raw = nt(keys_cat, query_stack)
    gate_near = gate_ref[pl.ds(pl.multiple_of(i * WIN, WIN), 2 * WIN), :]
    gate_far = gate_ref[WIN + rows :, :]
    slots = gate_far.shape[0]
    near = jnp.where(near_ok, raw[: 2 * WIN] + gate_near, very_low)
    lane = lax.broadcasted_iota(jnp.int32, (slots, LANES), 1) % WIN
    far_ok = far_pos <= lane + (place * rows + i * WIN - WIN)
    far_raw = raw[2 * WIN :] + gate_far
    far = jnp.concatenate(
        [
            jnp.where(far_ok, far_raw[:, c * LANES : (c + 1) * LANES], very_low)
            for c in range(width // LANES)
        ],
        axis=1,
    )
    return jnp.concatenate([near, far], axis=0)


def launch(kernel, name, work, grid, in_specs, out_specs, out_shape, scratch, limit, operands, after=(), prefetch=(),
           free=(), aliases=None, held=()):
    count, extra = len(operands), len(after)

    def body(*refs):
        lead = len(prefetch)
        rest = refs[lead + count + extra :]
        rest[len(shapes)][...] = jnp.zeros(TOKEN, f32)
        kernel(*refs[: lead + count], *rest[: len(shapes)], *rest[len(shapes) + 1 :])

    def place(at, value, spec):
        if spec.memory_space == pltpu.SMEM or at in free:
            return value
        return pltpu.with_memory_space_constraint(value, pltpu.HBM)

    operands = [place(at, value, spec) for at, (value, spec) in enumerate(zip(operands, in_specs))]
    after = [pltpu.with_memory_space_constraint(value, pltpu.HBM) for value in after]
    shapes, kept = out_shape, len(free) > 0 and name == "advance"
    out = pl.pallas_call(
        body,
        grid_spec=pltpu.PrefetchScalarGridSpec(
            num_scalar_prefetch=len(prefetch),
            grid=grid,
            in_specs=list(in_specs) + [pl.BlockSpec(memory_space=pl.ANY)] * extra,
            out_specs=list(out_specs) + [same(*TOKEN)],
            scratch_shapes=scratch,
        ),
        out_shape=[
            shape if kept and at not in held else pltpu.HBM(shape.shape, shape.dtype) for at, shape in enumerate(shapes)
        ] + [pltpu.HBM(TOKEN, f32)],
        compiler_params=pltpu.CompilerParams(vmem_limit_bytes=limit * 2**20),
        cost_estimate=pl.CostEstimate(flops=int(work * 5e9), bytes_accessed=2**20, transcendentals=0),
        input_output_aliases=aliases or {},
        name=name,
    )(*prefetch, *operands, *after)
    return list(out)


def passed_along(value, axis, steps):
    count = lax.axis_size(axis)
    leading, last = (max(0, -steps), min(count, count - steps))
    return lax.ppermute(value, axis, [(source, source + steps) for source in range(leading, last)])


def normalise(values):
    average = jnp.mean(values, axis=-1, keepdims=True)
    centred = values - average
    variance = jnp.mean(centred * centred, axis=-1, keepdims=True)
    inverse = lax.rsqrt(variance + epsilon)
    return (centred * inverse, inverse)


def normalise_back(grad_out, unit, inverse, gain):
    grad_unit = grad_out * gain
    mean_grad = jnp.mean(grad_unit, axis=-1, keepdims=True)
    mean_cross = jnp.mean(grad_unit * unit, axis=-1, keepdims=True)
    return (grad_unit - mean_grad - unit * mean_cross) * inverse


def row(ref):
    return ref[...].reshape(1, -1)


def column_sums(values):
    return jnp.sum(values, axis=0, keepdims=True)


def accumulate(ref, update):
    step = pl.program_id(0)

    @pl.when(step == 0)
    def _():
        ref[...] = update

    @pl.when(step > 0)
    def _():
        ref[...] += update


def same(*shape):
    return pl.BlockSpec(shape, lambda *_: (0,) * len(shape))


class Moves:
    def __init__(self, sems):
        self.sems, self.made = sems, []

    def add(self, source, target):
        self.made.append((source, target, self.sems.at[len(self.made)]))
        return len(self.made) - 1

    def start(self, *which):
        for at in which:
            pltpu.make_async_copy(*self.made[at]).start()

    def wait(self, *which):
        for at in which:
            pltpu.make_async_copy(*self.made[at]).wait()


def rows_at(index, size):
    return pl.ds(pl.multiple_of(index * size, size), size)


def vmem():
    return pl.BlockSpec(memory_space=pltpu.VMEM)


def anywhere():
    return pl.BlockSpec(memory_space=pl.ANY)


def spread_slots(grid):
    blocks = grid.shape[0]
    slots = blocks * PICK
    wide = jnp.concatenate([jnp.broadcast_to(grid[s : s + 1, :], (PICK, grid.shape[1])) for s in range(blocks)], axis=0)
    lane = lax.broadcasted_iota(jnp.int32, wide.shape, 1)
    turn = lax.broadcasted_iota(jnp.int32, wide.shape, 0) % PICK
    return jnp.sum(jnp.where(lane == turn, wide, 0.0), axis=1, keepdims=True)


def project_kernel(
    steps, tokens_ref, picks_ref, quota_ref, gain_ref, shift_ref, joint_ref, query_bias_ref, value_bias_ref,
    score_weight_ref, normed_ref, q_ref, k_ref, v_ref, score_ref, rim_ref, sent_ref, gathered,
):
    step = pl.program_id(0)
    tile, width = tokens_ref.shape
    unit, _ = normalise(tokens_ref[...].astype(f32))
    normed = (unit * row(gain_ref) + row(shift_ref)).astype(bf16)
    normed_ref[...] = normed
    q_ref[...] = (nn(normed, joint_ref[:, :width]) + row(query_bias_ref)).astype(bf16)
    keys = nn(normed, joint_ref[:, width : 2 * width]).astype(bf16)
    values = (nn(normed, joint_ref[:, 2 * width :]) + row(value_bias_ref)).astype(bf16)
    score = nt(normed, score_weight_ref[...]).astype(bf16)
    heads = score.shape[1]
    k_ref[...] = keys
    v_ref[...] = values
    score_ref[...] = jnp.zeros_like(score_ref)
    score_ref[:, :heads] = score
    picks = spread_slots(picks_ref[...].astype(f32))
    slots = picks.shape[0]
    row_of = lax.broadcasted_iota(jnp.int32, (slots, tile), 1) + step * tile
    chosen = jnp.where(picks == row_of.astype(f32), 1.0, 0.0).astype(bf16)
    parts = ((0, keys), (width, values), (2 * width, normed), (3 * width, score_ref[...]))

    @pl.when(step == 0)
    def _():
        gathered[...] = jnp.zeros_like(gathered)

    for start, part in parts:
        gathered[:, start : start + part.shape[1]] += nn(chosen, part)

    @pl.when(step == steps - 1)
    def _():
        for start, part in parts:
            rim_ref[:, start : start + part.shape[1]] = part[tile - WIN :]
        sent_ref[...] = gathered[...].astype(bf16)
        lane = lax.broadcasted_iota(jnp.int32, (slots, LANES), 1)
        blocks = slots // PICK
        quota = jnp.broadcast_to(quota_ref[...].astype(f32), (slots, blocks))
        block_of = lax.broadcasted_iota(jnp.int32, (slots, blocks), 0) // PICK
        taken = jnp.where(lax.broadcasted_iota(jnp.int32, (slots, blocks), 1) == block_of, quota, 0.0)
        taken = jnp.sum(taken, axis=1, keepdims=True)
        turn = (lax.broadcasted_iota(jnp.int32, (slots, 1), 0) % PICK).astype(f32)
        live = jnp.where(turn < taken, 1.0, 0.0)
        high = jnp.floor(picks * (1.0 / DIGIT))
        coded = jnp.where(lane == heads, high, jnp.where(lane == heads + 1, picks - high * DIGIT, live))
        sent_ref[:, 3 * width :] = jnp.where(
            (lane >= heads) & (lane < heads + 3), coded, gathered[:, 3 * width :]
        ).astype(bf16)


def tiled(*shape):
    return pl.BlockSpec(shape, lambda r, *_: (r,) + (0,) * (len(shape) - 1))


def project(tokens, picks, quota, gain, shift, joint, query_bias, value_bias, score_weight, tile=256):
    rows, width = tokens.shape
    slots = picks.shape[0] * picks.shape[1]
    channels = 3 * width + LANES
    steps = rows // tile
    S = jax.ShapeDtypeStruct
    return launch(
        functools.partial(project_kernel, steps),
        "project", 10, (steps,),
        [
            tiled(tile, width), same(*picks.shape), same(*quota.shape), same(width), same(width), same(*joint.shape),
            same(width), same(width), same(*score_weight.shape),
        ],
        [tiled(tile, width)] * 4 + [tiled(tile, LANES), same(WIN, channels), same(slots, channels)],
        [S((rows, width), bf16)] * 4 + [S((rows, LANES), bf16), S((WIN, channels), bf16), S((slots, channels), bf16)],
        [pltpu.VMEM((slots, channels), f32)], 24,
        (tokens, picks, quota, gain, shift, joint, query_bias, value_bias, score_weight),
    )


def far_positions(far_score, heads, place_rows, blocks):
    wide = far_score.astype(f32)
    slot = lax.broadcasted_iota(jnp.int32, (far_score.shape[0], 1), 0)
    at = (wide[:, heads : heads + 1] * DIGIT + wide[:, heads + 1 : heads + 2]).astype(jnp.int32)
    return jnp.where(
        wide[:, heads + 2 : heads + 3] > 0.5, (slot // PICK) * place_rows + at, 2 * place_rows * blocks
    )


def load_block(group, place_ref, k_ref, v_ref, score_ref, rim_refs, far_refs, keys, values, gate_ref, head_size):
    rows, width = k_ref.shape
    rim_k_ref, rim_v_ref, rim_score_ref = rim_refs
    far_score_ref = far_refs[2]
    slots = far_score_ref.shape[0]
    keys[0:WIN, :] = rim_k_ref[...]
    keys[WIN:, :] = k_ref[...]
    values[0:WIN, :] = rim_v_ref[...]
    values[WIN:, :] = v_ref[...]
    gates_into(gate_ref, group, place_ref[0], score_ref, rim_score_ref, far_score_ref, head_size, rows, slots)


def attend_kernel(
    heads, head_size, unroll, place_ref, q_ref, k_ref, v_ref, score_ref,
    rim_k_ref, rim_v_ref, rim_score_ref, far_k_ref, far_v_ref, far_score_ref,
    mixed_ref, total_ref, keys, values, gate_ref,
):
    group = pl.program_id(0)
    place = place_ref[0]
    rows, width = q_ref.shape
    slots = far_k_ref.shape[0]
    load_block(
        group, place_ref, k_ref, v_ref, score_ref, (rim_k_ref, rim_v_ref, rim_score_ref),
        (far_k_ref, far_v_ref, far_score_ref), keys, values, gate_ref, head_size,
    )
    near_ok = near_bias(width)
    far_pos = jnp.broadcast_to(far_positions(far_score_ref[...], heads, rows, slots // PICK), (slots, LANES))

    @pl.loop(0, rows // WIN, unroll=unroll)
    def _(i):
        at = pl.ds(pl.multiple_of(i * WIN, WIN), WIN)
        span = pl.ds(pl.multiple_of(i * WIN, WIN), 2 * WIN)
        keys_cat = jnp.concatenate([keys[span, :], far_k_ref[...]], axis=0)
        values_cat = jnp.concatenate([values[span, :], far_v_ref[...]], axis=0)
        stack = stack_heads(q_ref[at, :], head_size, 1.0 / math.sqrt(head_size))
        logit = tile_logits(i, keys_cat, stack, gate_ref, far_pos, place, rows, near_ok)
        top = jnp.max(logit, axis=0, keepdims=True)
        power = jnp.exp(logit - top)
        total = jnp.sum(power, axis=0, keepdims=True)
        prob = (power * (1.0 / total)).astype(bf16)
        total_ref[0, pl.ds(i, 1), :] = top + jnp.log(total)
        mixed_ref[at, :] = pick_heads(tn(prob, values_cat), head_size).astype(bf16)


def far_specs(slots, width, groups):
    return [
        pl.BlockSpec((slots, width), lambda g: (0, g)),
        pl.BlockSpec((slots, width), lambda g: (0, groups + g)),
        pl.BlockSpec((slots, LANES), lambda g: (0, 3 * groups * width // LANES)),
    ]


def attend(place, q, k, v, score, rim, far, heads, unroll=8):
    rows, model = q.shape
    slots = far.shape[0]
    width = PACK * WIN
    groups = model // width
    cols = pl.BlockSpec((rows, width), lambda g: (0, g))
    return launch(
        functools.partial(attend_kernel, heads, WIN, unroll),
        "attend", 12, (groups,),
        [pl.BlockSpec(memory_space=pltpu.SMEM), cols, cols, cols, pl.BlockSpec((rows, LANES), lambda g: (0, 0))]
        + far_specs(WIN, width, groups) + far_specs(slots, width, groups),
        [cols, pl.BlockSpec((1, rows // WIN, width), lambda g: (g, 0, 0))],
        [
            jax.ShapeDtypeStruct((rows, model), bf16),
            jax.ShapeDtypeStruct((groups, rows // WIN, width), f32),
        ],
        [
            pltpu.VMEM((WIN + rows, width), bf16),
            pltpu.VMEM((WIN + rows, width), bf16),
            pltpu.VMEM((WIN + rows + slots, width), f32),
        ],
        32, (place, q, k, v, score, rim, rim, rim, far, far, far),
    )


class Block:
    def __init__(self, groups, loaded, k_h, v_h, score_h, rim_h, far_h, score_ref, keys, values, model, rows):
        self.loads = loads = Moves(loaded)
        slots, width = far_h.shape[0], keys.shape[2]
        self.near, self.own, self.far = pl.ds(0, WIN), pl.ds(WIN, rows), pl.ds(WIN + rows, slots)
        scores = pl.ds(3 * model, LANES)
        self.first = [
            loads.add(source, target)
            for source, target in (
                (score_h, score_ref.at[self.own, :]), (rim_h.at[:, scores], score_ref.at[self.near, :]),
                (far_h.at[:, scores], score_ref.at[self.far, :]),
            )
        ]
        self.second = []
        for at, group in enumerate(groups):
            cols, value_cols = pl.ds(group * width, width), pl.ds(model + group * width, width)
            self.second.append(
                [
                    loads.add(source, target)
                    for source, target in (
                        (k_h.at[:, cols], keys.at[at, self.own, :]), (rim_h.at[:, cols], keys.at[at, self.near, :]),
                        (far_h.at[:, cols], keys.at[at, self.far, :]), (v_h.at[:, cols], values.at[at, self.own, :]),
                        (rim_h.at[:, value_cols], values.at[at, self.near, :]),
                        (far_h.at[:, value_cols], values.at[at, self.far, :]),
                    )
                ]
            )

    def add(self, at, source, target):
        self.second[at].append(self.loads.add(source, target))


def gates_of(gate, spread, place, gate_ref):
    gate_ref[...] = sum(nn(part, spread) for part in three_parts(gate))
    gate_ref[0:WIN, :] = jnp.where(place == 0, very_low, gate_ref[0:WIN, :])


def attend_back_kernel(
    heads, head_size, unroll, groups, last, place_ref, q_h, k_h, v_h, grad_h, total_ref, score_h, rim_h, far_h, normed_h,
    *refs,
):
    refs = list(refs)
    earlier = [refs.pop(0) for _ in range(5)] if groups[0] else []
    beside_refs = [refs.pop(0) for _ in range(2)] if groups[0] else []
    dq_h, dk_h, dv_h, ds_ref, rim_out, far_out, rim_ds, far_ds, send, keep = refs[:10]
    q_ref, grad_ref, score_ref, dq_ref, keys, values, gate_refs, all_dkeys, all_dvalues, all_dscore, normed = refs[10:21]
    loaded, stored = refs[21:]
    model = normed.shape[1]
    place = place_ref[0]
    _, rows, width = q_ref.shape
    slots = far_h.shape[0]
    block = Block(groups, loaded, k_h, v_h, score_h, rim_h, far_h, score_ref, keys, values, model, rows)
    near, own, far, loads = block.near, block.own, block.far, block.loads
    for g, group in enumerate(groups):
        cols = pl.ds(group * width, width)
        block.add(g, q_h.at[:, cols], q_ref.at[g])
        block.add(g, grad_h.at[:, cols], grad_ref.at[g])
    normed_cols = pl.ds(2 * model, model)
    third = [
        loads.add(source, target)
        for source, target in (
            (normed_h, normed.at[own, :]), (rim_h.at[:, normed_cols], normed.at[near, :]),
            (far_h.at[:, normed_cols], normed.at[far, :]),
        )
    ]
    loads.start(*range(len(loads.made)))
    for ref in (all_dkeys, all_dvalues, all_dscore):
        ref[...] = jnp.zeros_like(ref)
    loads.wait(*block.first)
    gate = jax.nn.log_sigmoid(score_ref[...].astype(f32))
    near_ok = near_bias(width)
    far_pos = jnp.broadcast_to(far_positions(score_ref[far, :], heads, rows, slots // PICK), (slots, LANES))
    stores = Moves(stored)
    mine = place % 2
    half = model // 2
    start = 0
    if beside_refs:
        start = beside_refs[0].shape[1]
        send[:, :start] = beside_refs[0][...]
        keep[:, :start] = beside_refs[1][...]
        for out, old in zip((rim_out, far_out), earlier[:2]):
            out[...] = old[...]
    for g, group in enumerate(groups):
        gate_ref, dkeys, dvalues, dscore = (ref.at[g] for ref in (gate_refs, all_dkeys, all_dvalues, all_dscore))
        gather = head_spread(group, head_size, width)
        gates_of(gate, gather, place, gate_ref)
        loads.wait(*block.second[g])

        @pl.loop(0, rows // WIN, unroll=unroll)
        def _(i):
            at = pl.ds(pl.multiple_of(i * WIN, WIN), WIN)
            after = pl.ds(pl.multiple_of(i * WIN + WIN, WIN), WIN)
            span = pl.ds(pl.multiple_of(i * WIN, WIN), 2 * WIN)
            keys_cat = jnp.concatenate([keys[g, span, :], keys[g, far, :]], axis=0)
            values_cat = jnp.concatenate([values[g, span, :], values[g, far, :]], axis=0)
            stack = stack_heads(q_ref[g, at, :], head_size, 1.0 / math.sqrt(head_size))
            grad_stack = stack_heads(grad_ref[g, at, :], head_size, 1.0)
            logit = tile_logits(i, keys_cat, stack, gate_ref, far_pos, place, rows, near_ok)
            prob = jnp.exp(logit - total_ref[group, pl.ds(i, 1), :])
            grad_prob = nt(values_cat, grad_stack)
            delta = jnp.sum(prob * grad_prob, axis=0, keepdims=True)
            grad_logit = prob * (grad_prob - delta)
            low = grad_logit.astype(bf16)
            dq = pick_heads(tn(low, keys_cat), head_size) * (1.0 / math.sqrt(head_size))
            dq_ref[g, at, :] = dq.astype(bf16)
            for ref, update in (
                (dkeys, nn(low, stack)),
                (dvalues, nn(prob.astype(bf16), grad_stack)),
                (dscore, grad_logit),
            ):
                ref[at, :] += update[:WIN]
                ref[after, :] = update[WIN : 2 * WIN]
                ref[far, :] += update[2 * WIN :]

        to = pl.ds(g * width, width)
        for source, target in ((dq_ref.at[g], dq_h), (dkeys.at[own, :], dk_h), (dvalues.at[own, :], dv_h)):
            stores.start(stores.add(source, target.at[:, to]))
        if g == 0:
            loads.wait(*third)
        joint = jnp.concatenate(
            [tn(normed[own, :], dq_ref[g])]
            + [tn(normed[...], ref[...].astype(bf16)) for ref in (dkeys, dvalues)],
            axis=1,
        ).astype(bf16)
        top, low = joint[:half], joint[half:]
        span = slice(start + 3 * width * g, start + 3 * width * (g + 1))
        send[:, span] = jnp.where(mine == 0, low, top)
        keep[:, span] = jnp.where(mine == 0, top, low)
        for out, part in ((rim_out, near), (far_out, far)):
            for base, ref in ((0, dkeys), (model, dvalues)):
                out[:, base + group * width : base + (group + 1) * width] = ref[part, :].astype(bf16)
        for number, (out_ref, part) in enumerate(((rim_ds, near), (far_ds, far), (ds_ref, own))):
            sums = dscore[part, :]
            high = sums.astype(bf16)
            rest = (sums - high.astype(f32)).astype(bf16)
            update = (nt(high, gather) + nt(rest, gather)) * jax.nn.sigmoid(-score_ref[part, :].astype(f32))
            if g:
                out_ref[...] += update
            else:
                out_ref[...] = update + earlier[2 + number][...] if earlier else update
    if last:
        rim_out[:, 2 * model :] = rim_ds[...].astype(bf16)
        far_out[:, 2 * model :] = far_ds[...].astype(bf16)
    stores.wait(*range(len(stores.made)))


def attend_back(place, q, k, v, grad, total, score, rim, far, normed, heads, groups, earlier, joined, after=(), unroll=8):
    rows, model = q.shape
    slots = far.shape[0]
    width = PACK * WIN
    count = len(groups)
    channels = 2 * model + LANES
    S = jax.ShapeDtypeStruct
    half = (model // 2, 3 * width * count + (joined[0].shape[1] if joined else 0))
    ext = WIN + rows + slots
    V = pltpu.VMEM
    out = launch(
        functools.partial(attend_back_kernel, heads, WIN, unroll, groups, groups[-1] == model // width - 1),
        "attend_back", 13 * count, (),
        [pl.BlockSpec(memory_space=pltpu.SMEM)] + [anywhere()] * 4 + [vmem()] + [anywhere()] * 4
        + [vmem()] * (len(earlier) + len(joined)),
        [anywhere()] * 3 + [vmem()] * 7,
        [
            S((rows, count * width), bf16), S((rows, count * width), f32), S((rows, count * width), f32),
            S((rows, LANES), f32), S((WIN, channels), bf16), S((slots, channels), bf16), S((WIN, LANES), f32),
            S((slots, LANES), f32),
        ] + [S(half, bf16)] * 2,
        [
            V((count, rows, width), bf16), V((count, rows, width), bf16), V((ext, LANES), bf16),
            V((count, rows, width), bf16), V((count, ext, width), bf16), V((count, ext, width), bf16),
        ] + [V((count, ext, width), f32)] * 4
        + [
            V((ext, model), bf16), pltpu.SemaphoreType.DMA((6 + 8 * count,)), pltpu.SemaphoreType.DMA((3 * count,)),
        ],
        32 if count == 1 else 44,
        (place, q, k, v, grad, total, score, rim, far, normed, *earlier, *joined), after,
    )
    dq, dk, dv, ds, rim_out, far_out, rim_ds, far_ds, send, keep, token = out
    return (dq, dk, dv), (rim_out, far_out, rim_ds, far_ds, ds), (send, keep), token


cubic = 0.044715
root = 0.7978845608028654


def feed_kernel(
    tile, pieces, block, mine_ref, mixed_h, tokens_h, cot_h, out_weight_h, expand_h, reduce_h, out_bias_ref, gain_ref,
    shift_ref, expand_bias_ref,
    resid_h, hidden_h, grad_pre_h, sums_ref, send_one, keep_one, send_two, keep_two,
    mixed, tokens, cot, out_weight, expand, reduce, resids, normed, hidden, grad_pre, one, two, loaded, stored,
):
    rows, width = cot.shape
    inner = expand.shape[1]
    span = inner // pieces
    steps = rows // tile
    mine = mine_ref[0]
    loads = Moves(loaded)
    first = [loads.add(*pair) for pair in ((mixed_h, mixed), (out_weight_h, out_weight), (tokens_h, tokens))]
    second = loads.add(cot_h, cot)
    parts = []
    for piece in range(pieces):
        at = pl.ds(piece * span, span)
        parts.append(
            (loads.add(expand_h.at[:, at], expand.at[:, at]), loads.add(reduce_h.at[at, :], reduce.at[at, :]))
        )
    loads.start(*range(len(loads.made)))

    def store(number, source, target):
        return pltpu.make_async_copy(source, target, stored.at[number])

    def tile_stores(step):
        here = rows_at(step, tile)
        return [
            store(3 * step + at, source.at[here, :], target.at[here, :])
            for at, (source, target) in enumerate(((resids, resid_h), (hidden, hidden_h), (grad_pre, grad_pre_h)))
        ]

    def feed_tile(step, leading):
        here = rows_at(step, tile)
        if leading:
            loads.wait(*first)
        resid = tokens[here, :].astype(f32) + nn(mixed[here, :], out_weight[...]) + row(out_bias_ref)
        resids[here, :] = resid
        unit, _ = normalise(resid)
        low = (unit * row(gain_ref) + row(shift_ref)).astype(bf16)
        normed[here, :] = low
        if leading:
            loads.wait(second)
        sums = []
        for piece in range(pieces):
            at = slice(piece * span, (piece + 1) * span)
            if leading:
                loads.wait(*parts[piece])
            pre = nn(low, expand[:, at]) + row(expand_bias_ref)[:, at]
            back = nt(cot[here, :], reduce[at, :])
            squared = pre * pre
            half = 0.5 + 0.5 * jnp.tanh(pre * (root + root * cubic * squared))
            active = pre * half
            slope = half + (active - active * half) * (2.0 * root + 6.0 * root * cubic * squared)
            hidden[here, at] = active.astype(bf16)
            grad = (back * slope).astype(bf16)
            grad_pre[here, at] = grad
            sums.append(column_sums(grad.astype(f32)))
        total = jnp.concatenate(sums, axis=0)
        if leading:
            sums_ref[...] = total
        else:
            sums_ref[...] += total
        for copy in tile_stores(step):
            copy.start()

    feed_tile(0, True)

    @pl.loop(1, steps)
    def _(step):
        feed_tile(step, False)

    base = 3 * steps
    count = inner // 2 // block
    half = width // 2

    def one_store(turn, j):
        here = rows_at(j, block)
        target = (send_one, keep_one)[turn]
        return store(base + turn * count + j, one.at[turn, here, :], target.at[here, :])

    def two_store(turn):
        return store(base + 2 * count + turn, two.at[turn], (send_two, keep_two)[turn])

    for turn in range(2):
        side_of = (1 - mine) if turn == 0 else mine

        @pl.loop(0, count)
        def _(j):
            one[turn, rows_at(j, block), :] = tn(hidden[:, rows_at(side_of * count + j, block)], cot[...]).astype(bf16)
            one_store(turn, j).start()

    for turn in range(2):
        side_of = (1 - mine) if turn == 0 else mine
        two[turn] = tn(normed[:, rows_at(side_of, half)], grad_pre[...]).astype(bf16)
        two_store(turn).start()

    @pl.loop(0, steps)
    def _(step):
        for copy in tile_stores(step):
            copy.wait()

    for turn in range(2):
        @pl.loop(0, count)
        def _(j):
            one_store(turn, j).wait()

        two_store(turn).wait()


def feed(
    mine, mixed, tokens, cot, out_weight, out_bias, gain, shift, expand, expand_bias, reduce, tile=1024, block=768,
):
    rows, width = tokens.shape
    inner = expand.shape[1]
    steps, pieces = rows // tile, inner // width
    S = jax.ShapeDtypeStruct
    B = pltpu.VMEM
    return launch(
        functools.partial(feed_kernel, tile, pieces, block),
        "feed", 33, (),
        [anywhere()] * 6 + [vmem()] * 4,
        [anywhere()] * 3 + [vmem()] + [anywhere()] * 4,
        [
            S((rows, width), f32), S((rows, inner), bf16), S((rows, inner), bf16), S((pieces, inner // pieces), f32),
            S((inner // 2, width), bf16), S((inner // 2, width), bf16),
            S((width // 2, inner), bf16), S((width // 2, inner), bf16),
        ],
        [
            B((rows, width), bf16), B((rows, width), bf16), B((rows, width), bf16), B((width, width), bf16),
            B((width, inner), bf16), B((inner, width), bf16), B((rows, width), f32), B((rows, width), bf16),
            B((rows, inner), bf16), B((rows, inner), bf16), B((2, inner // 2, width), bf16), B((2, width // 2, inner), bf16),
            pltpu.SemaphoreType.DMA((4 + 2 * pieces,)),
            pltpu.SemaphoreType.DMA((3 * steps + inner // block + 2,)),
        ],
        60, (mixed, tokens, cot, out_weight, expand, reduce, out_bias, gain, shift, expand_bias), (), (mine,),
    )


def feed_back_kernel(
    tile, pieces, mine_ref, grad_pre_h, resid_h, cot_h, mixed_h, expand_h, out_weight_h, gain_ref,
    grad_resid_h, grad_mixed_h, sums_ref, send_h, keep_h,
    grad_pre, resid, cot, mixed, expand, out_weight, grad_attn, grad_mixed, three, loaded, stored,
):
    rows, width = cot.shape
    inner = expand.shape[1]
    span = inner // pieces
    steps = rows // tile
    half = width // 2
    mine = mine_ref[0]
    loads = Moves(loaded)

    def tile_load(step):
        return [
            loads.add(source.at[rows_at(step, tile), :], target.at[rows_at(step, tile), :])
            for source, target in ((grad_pre_h, grad_pre), (resid_h, resid), (cot_h, cot))
        ]

    tiles = [tile_load(0)]
    weights = [
        loads.add(expand_h.at[:, pl.ds(piece * span, span)], expand.at[:, pl.ds(piece * span, span)])
        for piece in range(pieces)
    ]
    late = loads.add(out_weight_h, out_weight)
    tiles += [tile_load(step) for step in range(1, steps)]
    last = loads.add(mixed_h, mixed)
    loads.start(*range(len(loads.made)))
    stores = Moves(stored)
    sums = []

    def first_part(step):
        here = rows_at(step, tile)
        grad_normed = jnp.zeros((tile, width), f32)
        for piece in range(pieces):
            at = slice(piece * span, (piece + 1) * span)
            if step == 0:
                loads.wait(weights[piece])
            grad_normed = grad_normed + nt(grad_pre[here, at], expand[:, at])
        return grad_normed

    def second_part(step, grad_normed):
        here = rows_at(step, tile)
        wide = cot[here, :].astype(f32)
        unit, inverse = normalise(resid[here, :])
        grad_resid = wide + normalise_back(grad_normed, unit, inverse, row(gain_ref))
        resid[here, :] = grad_resid
        low = grad_resid.astype(bf16)
        grad_attn[here, :] = low
        grad_mixed[here, :] = nt(low, out_weight[...]).astype(bf16)
        sums.append(
            jnp.concatenate(
                [
                    column_sums(low.astype(f32)),
                    column_sums(grad_normed * unit),
                    column_sums(grad_normed),
                    column_sums(wide),
                ],
                axis=0,
            )
        )

    loads.wait(*tiles[0])
    before = first_part(0)
    loads.wait(late, *tiles[1])
    ahead = first_part(1)
    second_part(0, before)
    loads.wait(last, *[at for tile_loads in tiles[2:] for at in tile_loads])
    for step in range(2, steps + 1):
        before, ahead = ahead, first_part(step) if step < steps else None
        second_part(step - 1, before)
    sums_ref[...] = sum(sums)
    for step in range(steps):
        here = rows_at(step, tile)
        stores.start(
            stores.add(resid.at[here, :], grad_resid_h.at[here, :]),
            stores.add(grad_mixed.at[here, :], grad_mixed_h.at[here, :]),
        )
    for turn in range(2):
        side_of = (1 - mine) if turn == 0 else mine
        three[turn] = tn(mixed[:, rows_at(side_of, half)], grad_attn[...]).astype(bf16)
        stores.start(stores.add(three.at[turn], (send_h, keep_h)[turn]))
    stores.wait(*range(len(stores.made)))


def feed_back(mine, grad_pre, resid, cot, mixed, expand, out_weight, gain, tile=256, pieces=4):
    rows, width = resid.shape
    inner = expand.shape[1]
    steps = rows // tile
    S = jax.ShapeDtypeStruct
    B = pltpu.VMEM
    return launch(
        functools.partial(feed_back_kernel, tile, pieces), "feed_back", 12, (),
        [anywhere()] * 6 + [vmem()],
        [anywhere()] * 2 + [vmem()] + [anywhere()] * 2,
        [
            S((rows, width), f32), S((rows, width), bf16), S((4, width), f32),
            S((width // 2, width), bf16), S((width // 2, width), bf16),
        ],
        [
            B((rows, inner), bf16), B((rows, width), f32), B((rows, width), bf16), B((rows, width), bf16),
            B((width, inner), bf16), B((width, width), bf16), B((rows, width), bf16), B((rows, width), bf16),
            B((2, width // 2, width), bf16),
            pltpu.SemaphoreType.DMA((3 * steps + pieces + 2,)),
            pltpu.SemaphoreType.DMA((2 * steps + 2,)),
        ],
        44, (grad_pre, resid, cot, mixed, expand, out_weight, gain), (), (mine,),
    )


def finish_kernel(resid_ref, hidden_ref, reduce_ref, bias_ref, out_ref):
    out_ref[...] = (resid_ref[...] + nn(hidden_ref[...], reduce_ref[...]) + row(bias_ref)).astype(bf16)


def finish(resid, hidden, reduce, bias, after=(), tile=256):
    rows, width = resid.shape
    inner = reduce.shape[0]
    return launch(
        finish_kernel, "finish", 7, (rows // tile,),
        [tiled(tile, width), tiled(tile, inner), same(inner, width), same(width)],
        [tiled(tile, width)], [jax.ShapeDtypeStruct((rows, width), bf16)],
        [], 26, (resid, hidden, reduce, bias), after,
    )


def beside(refs):
    return jnp.concatenate([ref[...] for ref in refs], axis=1)


def join_kernel(
    steps, groups, tokens_ref, resid_ref, ds_ref, rim_ref, far_ref, picks_ref, gain_ref, shift_ref,
    joint_ref, score_weight_ref, sums_two_ref, expand_sums_ref, *refs,
):
    dq_refs, dk_refs, dv_refs = (refs[at * groups : (at + 1) * groups] for at in range(3))
    token_ref, small_ref = refs[3 * groups :]
    step = pl.program_id(0)
    tile, width = tokens_ref.shape
    heads = score_weight_ref.shape[0]
    unit, inverse = normalise(tokens_ref[...].astype(f32))
    gain = row(gain_ref)
    normed = (unit * gain + row(shift_ref)).astype(bf16)
    picks = spread_slots(picks_ref[...].astype(f32))
    row_of = lax.broadcasted_iota(jnp.int32, (picks.shape[0], tile), 1) + step * tile
    chosen = jnp.where(picks == row_of.astype(f32), 1.0, 0.0).astype(bf16)
    at_end = jnp.where(step == steps - 1, 1.0, 0.0)

    def whole(own, start):
        span = own.shape[1]
        total = own + tn(chosen, far_ref[:, start : start + span])
        rim = rim_ref[:, start : start + span].astype(f32) * at_end
        return jnp.concatenate([total[: tile - WIN], total[tile - WIN :] + rim], axis=0).astype(bf16)

    dq = beside(dq_refs)
    dk = whole(beside(dk_refs), 0)
    dv = whole(beside(dv_refs), width)
    ds = whole(ds_ref[...], 2 * width)
    grad_normed = (
        nt(dq, joint_ref[:, :width])
        + nt(dk, joint_ref[:, width : 2 * width])
        + nt(dv, joint_ref[:, 2 * width :])
        + nn(ds[:, :heads], score_weight_ref[...])
    )
    token_ref[...] = resid_ref[...] + normalise_back(grad_normed, unit, inverse, gain)
    sums = jnp.concatenate(
        [
            column_sums(grad_normed * unit),
            column_sums(grad_normed),
            column_sums(dq.astype(f32)),
            column_sums(dv.astype(f32)),
        ],
        axis=0,
    )
    score_grad = tn(ds, normed)[:heads]
    past = 8 + expand_sums_ref.shape[0]

    @pl.when(step == 0)
    def _():
        small_ref[0:4, :] = sums
        small_ref[4:8, :] = sums_two_ref[...]
        small_ref[8:past, :] = expand_sums_ref[...]
        small_ref[past : past + heads, :] = score_grad

    @pl.when(step > 0)
    def _():
        small_ref[0:4, :] += sums
        small_ref[past : past + heads, :] += score_grad


def join(
    tokens, resid, dqs, dks, dvs, ds, rim, far, picks, gain, shift, joint, score_weight, sums_two, expand_sums, after=(),
    tile=256,
):
    rows, width = tokens.shape
    heads = score_weight.shape[0]
    count = 8 + expand_sums.shape[0] + heads
    S = jax.ShapeDtypeStruct
    return launch(
        functools.partial(join_kernel, rows // tile, len(dqs)), "join", 14, (rows // tile,),
        [tiled(tile, width)] * 2 + [
            tiled(tile, LANES), same(*rim.shape), same(*far.shape), same(*picks.shape), same(width), same(width),
            same(*joint.shape), same(*score_weight.shape), same(*sums_two.shape), same(*expand_sums.shape),
        ] + [tiled(tile, part.shape[1]) for part in (*dqs, *dks, *dvs)],
        [tiled(tile, width), same(count, width)],
        [S((rows, width), f32), S((count, width), f32)],
        [], 28, (tokens, resid, ds, rim, far, picks, gain, shift, joint, score_weight, sums_two, expand_sums, *dqs, *dks, *dvs), after,
    )


def swap(value, axis, bit):
    count = lax.axis_size(axis)
    return lax.ppermute(value, axis, [(i, i ^ bit) for i in range(count)])


def side(axis, bit):
    return (lax.axis_index(axis) // bit) % 2


def axis_bits(axis):
    count, bits, bit = lax.axis_size(axis), [], 1
    while bit < count:
        bits.append((axis, bit))
        bit *= 2
    return bits


def woven(*lists):
    result = []
    for step in range(max(map(len, lists))):
        for items in lists:
            result += items[step : step + 1]
    return result


def orders():
    near, far = axis_bits("seq"), axis_bits("dp")
    first, rest = near[:1], near[1:]
    return (
        first + rest + far,
        first + woven(rest[::-1], far),
        first + woven(far, rest),
    )


def cut(value, pieces):
    return value.reshape(pieces, value.shape[0] // pieces, value.shape[1])


class Chain:
    def __init__(self, send, keep, order):
        self.order, self.level, self.down, self.held = order, 0, True, True
        half = 2 ** (len(order) - 1)
        self.send, self.keep = cut(send, half), cut(keep, half)
        self.mine = [side(*where).astype(jnp.int32) for where in order]

    def got(self):
        return swap(self.send, *self.order[self.level])


def added(one, two):
    return (one[...].astype(f32) + two[...].astype(f32)).astype(bf16)


class Total:
    def __init__(self, value, order):
        self.send, self.order, self.level = value, order, 0

    def got(self):
        return swap(self.send, *self.order[self.level])


def advance_kernel(plan, bits_ref, *refs):
    refs = list(refs)
    outs = refs[sum(4 if kind == "split" else 2 for kind in plan) :]
    for kind in plan:
        if kind == "split":
            for _ in range(2):
                outs.pop(0)[...] = added(refs.pop(0), refs.pop(0))
        elif kind == "sum":
            outs.pop(0)[...] = refs.pop(0)[...] + refs.pop(0)[...]
        elif kind == "close":
            outs.pop(0)[...] = added(refs.pop(0), refs.pop(0))
        else:
            out = outs.pop(0)
            for which in range(2):
                out[which] = refs.pop(0)[...]


def advance(chains, after=(), hold=False):
    held = []
    plan, operands, in_specs, out_specs, shapes, bits, free = [], [], [], [], [], [], []
    depth = len(chains[0].order)
    for chain in chains:
        if isinstance(chain, Total):
            plan.append("sum")
            continue
        last = chain.down and chain.level == depth - 1
        plan.append("close" if last else "split" if chain.down else "stack")
    sizes = [chain.send.shape[0] // (2 if kind == "split" else 1) for chain, kind in zip(chains, plan)]
    steps = min([4] + [size for size, kind in zip(sizes, plan) if kind != "sum"])
    S = jax.ShapeDtypeStruct

    def half_of(which, other, block, tail):
        def index(g, bits_ref):
            mine = bits_ref[which]
            return ((1 - mine if other else mine) * steps + g, 0, 0)

        return pl.BlockSpec((block,) + tail, index)

    for chain, kind, size in zip(chains, plan, sizes):
        got, tail = chain.got(), chain.send.shape[1:]
        block = size // steps
        if kind == "sum":
            free += [len(operands), len(operands) + 1]
            operands += [chain.send, got]
            in_specs += [same(*chain.send.shape)] * 2
            out_specs += [same(*chain.send.shape)]
            shapes += [S(chain.send.shape, f32)]
        elif kind == "split":
            which = len(bits)
            bits.append(chain.mine[chain.level + 1])
            places = len(operands)
            free += [places + 1, places + 3] if chain.held else range(places, places + 4)
            chain.held = hold
            held += [len(shapes) + 1] if hold else []
            for other in (True, False):
                operands += [chain.keep, got]
                in_specs += [half_of(which, other, block, tail)] * 2
            out_specs += [tiled(block, *tail)] * 2
            shapes += [S((size,) + tail, bf16)] * 2
        elif kind == "close":
            free += [len(operands) + 1] if chain.held else [len(operands), len(operands) + 1]
            operands += [chain.keep, got]
            in_specs += [tiled(block, *tail)] * 2
            out_specs += [tiled(block, *tail)]
            shapes += [S((size,) + tail, bf16)]
        else:
            free += [len(operands), len(operands) + 1]
            operands += [chain.send, got]
            in_specs += [tiled(block, *tail)] * 2
            out_specs += [pl.BlockSpec((2, block) + tail, lambda g, *_: (0, g, 0, 0))]
            shapes += [S((2, size) + tail, bf16)]
    bits = jnp.stack(bits) if bits else jnp.zeros((1,), jnp.int32)
    outs = launch(
        functools.partial(advance_kernel, plan), "advance", 2, (steps,), in_specs, out_specs, shapes, [], 20, operands,
        after, (bits,), free, None, held,
    )
    for chain, kind in zip(chains, plan):
        if kind == "split":
            chain.send, chain.keep = outs[:2]
            chain.level += 1
            outs = outs[2:]
        elif kind == "sum":
            chain.send = outs[0]
            chain.level += 1
            outs = outs[1:]
        else:
            chain.send = outs[0].reshape((-1,) + chain.send.shape[1:])
            outs = outs[1:]
            if kind == "close":
                chain.down = False
            else:
                chain.level -= 1
    return outs[0]


def finished(chain):
    if isinstance(chain, Total):
        return chain.level == len(chain.order)
    return not chain.down and chain.level == 0


def ends(chain):
    return chain.send, chain.got()


def own_place(order):
    place = 0
    for axis, bit in order:
        place = place * 2 + side(axis, bit)
    return place.astype(jnp.int32).reshape(1)


def widen_half(own, chain, half_of, into=(), after=()):
    value, other = half_of
    half, size, n = value.shape
    count, group = 2 * half, 4

    def side_of(own_ref):
        mine = own_ref[0] // half
        return 1 - mine if other else mine

    def kernel(own_ref, value_ref, *refs):
        out_ref = refs[-1]
        for i in range(group):
            out_ref[i] = value_ref[jnp.bitwise_xor(own_ref[0] % group, i)].astype(f32)

    out, token = launch(
        kernel, "widen", 4, (half // group,),
        [pl.BlockSpec((group, size, n), lambda s, own_ref: (jnp.bitwise_xor(own_ref[0] % half // group, s), 0, 0))]
        + [anywhere()] * len(into),
        [pl.BlockSpec((group, size, n), lambda s, own_ref: (side_of(own_ref) * (half // group) + s, 0, 0))],
        [jax.ShapeDtypeStruct((count, size, n), f32)],
        [], 24, (value, *into), after, (own,), (0,), {2: 0} if into else None,
    )
    return out, token


def widen_joint_half(owns, values, other, into=(), after=()):
    half, size, n = values[0].shape
    count, group, model, width = 2 * half, 4, n // 2, PACK * WIN

    def side_of(own_ref):
        mine = own_ref[0] // half
        return 1 - mine if other else mine

    def kernel(own_one_ref, own_two_ref, one_ref, two_ref, *refs):
        joint_ref, first_ref = refs[-2:]
        for i in range(group):
            one = one_ref[jnp.bitwise_xor(own_one_ref[0] % group, i)].astype(f32)
            two = two_ref[jnp.bitwise_xor(own_two_ref[0] % group, i)].astype(f32)
            first_ref[i] = two[:, :model]
            for piece, start, g in ((one, 0, 0), (one, 3 * width, 1), (two, model, 2)):
                for kind in range(3):
                    to = kind * model + g * width
                    joint_ref[i, :, to : to + width] = piece[:, start + kind * width : start + (kind + 1) * width]

    def read(which):
        def index(s, *own_refs):
            return (jnp.bitwise_xor(own_refs[which][0] % half // group, s), 0, 0)

        return pl.BlockSpec((group, size, n), index)

    def write(columns):
        return pl.BlockSpec((group, size, columns), lambda s, own_ref, _: (side_of(own_ref) * (half // group) + s, 0, 0))

    S = jax.ShapeDtypeStruct
    joint, first, token = launch(
        kernel, "widen_joint", 4, (half // group,),
        [read(0), read(1)] + [anywhere()] * len(into), [write(3 * model), write(model)],
        [S((count, size, 3 * model), f32), S((count, size, model), f32)],
        [], 24, (*values, *into), after, tuple(owns), (0, 1), {4: 0, 5: 1} if into else None,
    )
    return (joint, first), token


def per_device(
    tokens, cotangent, first_gain, first_shift, joint_weight, query_bias, value_bias, score_weight, out_weight, out_bias,
    second_gain, second_shift, expand_weight, expand_bias, reduce_weight, reduce_bias, picks, quota,
):
    rows, width = tokens.shape[1:]
    heads = score_weight.shape[1]
    inner = expand_weight.shape[1]
    blocks = lax.axis_size("seq")
    slots = blocks * PICK
    here = lax.axis_index("seq").astype(jnp.int32).reshape(1)
    first, second, _ = orders()
    mine = side(*first[0]).astype(jnp.int32).reshape(1)
    inputs, grad_out = tokens[0], cotangent[0]
    chosen, turned = picks[0, 0], score_weight.T
    normed, q, k, v, score, rim_sent, sent, _ = project(
        inputs, chosen, quota[0], first_gain, first_shift, joint_weight, query_bias, value_bias, turned
    )
    rim = passed_along(rim_sent, "seq", 1)
    far = lax.all_to_all(
        sent.reshape(blocks, PICK, -1), "seq", split_axis=0, concat_axis=0, tiled=True
    ).reshape(slots, -1)
    mixed, total, _ = attend(here, q, k, v, score, rim, far, heads)
    resid, hidden, grad_pre, expand_sums, *halves, _ = feed(
        mine, mixed, inputs, grad_out, out_weight, out_bias, second_gain, second_shift, expand_weight, expand_bias,
        reduce_weight,
    )
    reduced, expanded = Chain(*halves[:2], first), Chain(*halves[2:], second)
    grad_resid, grad_mixed, sums_two, *out_halves, stage = feed_back(
        mine, grad_pre, resid, grad_out, mixed, expand_weight, out_weight, second_gain
    )
    big = [reduced, expanded]
    back = functools.partial(attend_back, here, q, k, v, grad_mixed, total, score, rim, far, normed, heads)
    stage = advance(big, (stage,))
    grads_one, carried, joined, stage = back((0, 1), (), (), (stage,))
    one = Chain(*joined, first)
    stage = advance(big, (stage,), True)
    grads_two, carried, joined, stage = back((2,), carried, tuple(out_halves), (stage,))
    two = Chain(*joined, second)
    rim_grad, far_grad, _, _, ds = carried
    rim_back = passed_along(rim_grad, "seq", -1)
    far_back = lax.all_to_all(
        far_grad.reshape(blocks, PICK, -1), "seq", split_axis=0, concat_axis=0, tiled=True
    ).reshape(slots, -1)
    dqs, dks, dvs = zip(grads_one, grads_two)
    stage = advance(big + [one], (stage,), True)
    stage = advance(big + [two], (stage,), True)
    token_grad, small, stage = join(
        inputs, grad_resid, dqs, dks, dvs, ds, rim_back, far_back, chosen, first_gain, first_shift, joint_weight, turned,
        sums_two, expand_sums, (stage,),
    )
    small = Total(small, first)
    late = [one, two]
    stage = advance(big + late, (stage,))
    layer_out, stage = finish(resid, hidden, reduce_weight, reduce_bias, (stage,))
    for chains in (
        big + late + [small], big + late + [small], big + late + [small], late + [small], late + [small],
    ):
        stage = advance([chain for chain in chains if not finished(chain)], (stage,))
    while not finished(reduced):
        stage = advance([chain for chain in big + late if not finished(chain)], (stage,))
    own_first, own_second = own_place(first), own_place(second)
    halves_one, halves_two = ends(reduced), ends(expanded)
    reduce_weight_grad, stage = widen_half(own_first, reduced, (halves_one[0], False), (), (stage,))
    expand_weight_grad, stage = widen_half(own_second, expanded, (halves_two[0], False), (), (stage,))
    reduce_weight_grad, stage = widen_half(own_first, reduced, (halves_one[1], True), (reduce_weight_grad,), (stage,))
    expand_weight_grad, stage = widen_half(own_second, expanded, (halves_two[1], True), (expand_weight_grad,), (stage,))
    while not (finished(one) and finished(two)):
        stage = advance([chain for chain in late if not finished(chain)], (stage,))
    while not finished(small):
        stage = advance([small], (stage,))
    halves_one, halves_two = ends(one), ends(two)
    owns = (own_first, own_second)
    both, stage = widen_joint_half(owns, (halves_one[0], halves_two[0]), False, (), (stage,))
    both, stage = widen_joint_half(owns, (halves_one[1], halves_two[1]), True, both, (stage,))
    reduce_weight_grad = reduce_weight_grad.reshape(inner, width)
    expand_weight_grad = expand_weight_grad.reshape(width, inner)
    joint_weight_grad, out_weight_grad = both[0].reshape(width, 3 * width), both[1].reshape(width, width)
    small = small.send
    gain_one, shift_one, query_sum, value_sum, out_sum, gain_two, shift_two, reduce_sum = (small[i] for i in range(8))
    past = 8 + inner // width
    return (
        layer_out[None],
        token_grad[None],
        gain_one,
        shift_one,
        joint_weight_grad,
        query_sum,
        value_sum,
        small[past : past + heads].T,
        out_weight_grad,
        out_sum,
        gain_two,
        shift_two,
        expand_weight_grad,
        small[8:past].reshape(inner),
        reduce_weight_grad,
        reduce_sum,
    )


def solution(mesh):
    placed = (
        P("dp", "seq", None),
        P("dp", "seq", None),
        P(),
        P(),
        P(),
        P(),
        P(),
        P(),
        P(),
        P(),
        P(),
        P(),
        P(),
        P(),
        P(),
        P(),
        P("dp", "seq", None, None),
        P("dp", "seq", None),
    )
    return jax.shard_map(
        per_device,
        mesh=mesh,
        in_specs=placed,
        out_specs=(
            P("dp", "seq", None),
            P("dp", "seq", None),
            P(),
            P(),
            P(),
            P(),
            P(),
            P(),
            P(),
            P(),
            P(),
            P(),
            P(),
            P(),
            P(),
            P(),
        ),
        check_vma=False,
    )
```

```python
import functools
import math

import jax
import jax.numpy as jnp
from jax import lax
from jax.experimental import pallas as pl
from jax.experimental.pallas import tpu as pltpu
from jax.sharding import PartitionSpec as P

WIN = 64
PICK = 8
LANES = 128
PACK = 4
DIGIT = 32
TOKEN = (8, 128)
epsilon = 1e-05
very_low = -1e30
bf16 = jnp.bfloat16
f32 = jnp.float32


def nt(left, right):
    return lax.dot_general(left, right, (((1,), (1,)), ((), ())), preferred_element_type=f32)


def tn(left, right):
    return lax.dot_general(left, right, (((0,), (0,)), ((), ())), preferred_element_type=f32)


def nn(left, right):
    return jnp.dot(left, right, preferred_element_type=f32)


def three_parts(value):
    high = value.astype(bf16)
    rest = value - high.astype(f32)
    middle = rest.astype(bf16)
    low = (rest - middle.astype(f32)).astype(bf16)
    return high, middle, low


def head_spread(group, head_size, width):
    row = lax.broadcasted_iota(jnp.int32, (LANES, width), 0)
    lane = lax.broadcasted_iota(jnp.int32, (LANES, width), 1)
    return jnp.where(row == group * PACK + lane // WIN, 1.0, 0.0).astype(bf16)


def stack_heads(tile, head_size, factor):
    width = tile.shape[1]
    lane = lax.broadcasted_iota(jnp.int32, tile.shape, 1) // head_size
    scaled = tile * jnp.asarray(factor, tile.dtype)
    zero = jnp.zeros_like(scaled)
    return jnp.concatenate([jnp.where(lane == h, scaled, zero) for h in range(PACK)], axis=0)


def pick_heads(full, head_size):
    lane = lax.broadcasted_iota(jnp.int32, (WIN, full.shape[1]), 1) // head_size
    out = full[0:WIN]
    for h in range(1, PACK):
        out = jnp.where(lane == h, full[h * WIN : (h + 1) * WIN], out)
    return out


def gates_into(gate_ref, group, place, score_ref, rim_score_ref, far_score_ref, head_size, rows, slots):
    width = PACK * WIN
    spread = head_spread(group, head_size, width)

    def expand(score):
        gate = jax.nn.log_sigmoid(score.astype(f32))
        return sum(nn(part, spread) for part in three_parts(gate))

    gate_ref[0:WIN, :] = jnp.where(place == 0, very_low, expand(rim_score_ref[...]))
    gate_ref[WIN : WIN + rows, :] = expand(score_ref[...])
    gate_ref[WIN + rows :, :] = expand(far_score_ref[...])


def near_bias(width):
    key = lax.broadcasted_iota(jnp.int32, (2 * WIN, width), 0)
    query = lax.broadcasted_iota(jnp.int32, (2 * WIN, width), 1) % WIN
    return (key <= query + WIN) & (key > query)


def tile_logits(i, keys_cat, query_stack, gate_ref, far_pos, place, rows, near_ok):
    width = PACK * WIN
    raw = nt(keys_cat, query_stack)
    gate_near = gate_ref[pl.ds(pl.multiple_of(i * WIN, WIN), 2 * WIN), :]
    gate_far = gate_ref[WIN + rows :, :]
    slots = gate_far.shape[0]
    near = jnp.where(near_ok, raw[: 2 * WIN] + gate_near, very_low)
    lane = lax.broadcasted_iota(jnp.int32, (slots, LANES), 1) % WIN
    far_ok = far_pos <= lane + (place * rows + i * WIN - WIN)
    far_raw = raw[2 * WIN :] + gate_far
    far = jnp.concatenate(
        [
            jnp.where(far_ok, far_raw[:, c * LANES : (c + 1) * LANES], very_low)
            for c in range(width // LANES)
        ],
        axis=1,
    )
    return jnp.concatenate([near, far], axis=0)


def launch(kernel, name, work, grid, in_specs, out_specs, out_shape, scratch, limit, operands, after=(), prefetch=(),
           free=(), aliases=None, held=()):
    count, extra = len(operands), len(after)

    def body(*refs):
        lead = len(prefetch)
        rest = refs[lead + count + extra :]
        rest[len(shapes)][...] = jnp.zeros(TOKEN, f32)
        kernel(*refs[: lead + count], *rest[: len(shapes)], *rest[len(shapes) + 1 :])

    def place(at, value, spec):
        if spec.memory_space == pltpu.SMEM or at in free:
            return value
        return pltpu.with_memory_space_constraint(value, pltpu.HBM)

    operands = [place(at, value, spec) for at, (value, spec) in enumerate(zip(operands, in_specs))]
    after = [pltpu.with_memory_space_constraint(value, pltpu.HBM) for value in after]
    shapes, kept = out_shape, len(free) > 0 and name == "advance"
    out = pl.pallas_call(
        body,
        grid_spec=pltpu.PrefetchScalarGridSpec(
            num_scalar_prefetch=len(prefetch),
            grid=grid,
            in_specs=list(in_specs) + [pl.BlockSpec(memory_space=pl.ANY)] * extra,
            out_specs=list(out_specs) + [same(*TOKEN)],
            scratch_shapes=scratch,
        ),
        out_shape=[
            shape if kept and at not in held else pltpu.HBM(shape.shape, shape.dtype) for at, shape in enumerate(shapes)
        ] + [pltpu.HBM(TOKEN, f32)],
        compiler_params=pltpu.CompilerParams(vmem_limit_bytes=limit * 2**20),
        cost_estimate=pl.CostEstimate(flops=int(work * 5e9), bytes_accessed=2**20, transcendentals=0),
        input_output_aliases=aliases or {},
        name=name,
    )(*prefetch, *operands, *after)
    return list(out)


def passed_along(value, axis, steps):
    count = lax.axis_size(axis)
    leading, last = (max(0, -steps), min(count, count - steps))
    return lax.ppermute(value, axis, [(source, source + steps) for source in range(leading, last)])


def normalise(values):
    average = jnp.mean(values, axis=-1, keepdims=True)
    centred = values - average
    variance = jnp.mean(centred * centred, axis=-1, keepdims=True)
    inverse = lax.rsqrt(variance + epsilon)
    return (centred * inverse, inverse)


def normalise_back(grad_out, unit, inverse, gain):
    grad_unit = grad_out * gain
    mean_grad = jnp.mean(grad_unit, axis=-1, keepdims=True)
    mean_cross = jnp.mean(grad_unit * unit, axis=-1, keepdims=True)
    return (grad_unit - mean_grad - unit * mean_cross) * inverse


def row(ref):
    return ref[...].reshape(1, -1)


def column_sums(values):
    return jnp.sum(values, axis=0, keepdims=True)


def accumulate(ref, update):
    step = pl.program_id(0)

    @pl.when(step == 0)
    def _():
        ref[...] = update

    @pl.when(step > 0)
    def _():
        ref[...] += update


def same(*shape):
    return pl.BlockSpec(shape, lambda *_: (0,) * len(shape))


class Moves:
    def __init__(self, sems):
        self.sems, self.made = sems, []

    def add(self, source, target):
        self.made.append((source, target, self.sems.at[len(self.made)]))
        return len(self.made) - 1

    def start(self, *which):
        for at in which:
            pltpu.make_async_copy(*self.made[at]).start()

    def wait(self, *which):
        for at in which:
            pltpu.make_async_copy(*self.made[at]).wait()


def rows_at(index, size):
    return pl.ds(pl.multiple_of(index * size, size), size)


def vmem():
    return pl.BlockSpec(memory_space=pltpu.VMEM)


def anywhere():
    return pl.BlockSpec(memory_space=pl.ANY)


def spread_slots(grid):
    blocks = grid.shape[0]
    slots = blocks * PICK
    wide = jnp.concatenate([jnp.broadcast_to(grid[s : s + 1, :], (PICK, grid.shape[1])) for s in range(blocks)], axis=0)
    lane = lax.broadcasted_iota(jnp.int32, wide.shape, 1)
    turn = lax.broadcasted_iota(jnp.int32, wide.shape, 0) % PICK
    return jnp.sum(jnp.where(lane == turn, wide, 0.0), axis=1, keepdims=True)


def project_kernel(
    steps, tokens_ref, picks_ref, quota_ref, gain_ref, shift_ref, joint_ref, query_bias_ref, value_bias_ref,
    score_weight_ref, normed_ref, q_ref, k_ref, v_ref, score_ref, rim_ref, sent_ref, gathered,
):
    step = pl.program_id(0)
    tile, width = tokens_ref.shape
    unit, _ = normalise(tokens_ref[...].astype(f32))
    normed = (unit * row(gain_ref) + row(shift_ref)).astype(bf16)
    normed_ref[...] = normed
    q_ref[...] = (nn(normed, joint_ref[:, :width]) + row(query_bias_ref)).astype(bf16)
    keys = nn(normed, joint_ref[:, width : 2 * width]).astype(bf16)
    values = (nn(normed, joint_ref[:, 2 * width :]) + row(value_bias_ref)).astype(bf16)
    score = nt(normed, score_weight_ref[...]).astype(bf16)
    heads = score.shape[1]
    k_ref[...] = keys
    v_ref[...] = values
    score_ref[...] = jnp.zeros_like(score_ref)
    score_ref[:, :heads] = score
    picks = spread_slots(picks_ref[...].astype(f32))
    slots = picks.shape[0]
    row_of = lax.broadcasted_iota(jnp.int32, (slots, tile), 1) + step * tile
    chosen = jnp.where(picks == row_of.astype(f32), 1.0, 0.0).astype(bf16)
    parts = ((0, keys), (width, values), (2 * width, normed), (3 * width, score_ref[...]))

    @pl.when(step == 0)
    def _():
        gathered[...] = jnp.zeros_like(gathered)

    for start, part in parts:
        gathered[:, start : start + part.shape[1]] += nn(chosen, part)

    @pl.when(step == steps - 1)
    def _():
        for start, part in parts:
            rim_ref[:, start : start + part.shape[1]] = part[tile - WIN :]
        sent_ref[...] = gathered[...].astype(bf16)
        lane = lax.broadcasted_iota(jnp.int32, (slots, LANES), 1)
        blocks = slots // PICK
        quota = jnp.broadcast_to(quota_ref[...].astype(f32), (slots, blocks))
        block_of = lax.broadcasted_iota(jnp.int32, (slots, blocks), 0) // PICK
        taken = jnp.where(lax.broadcasted_iota(jnp.int32, (slots, blocks), 1) == block_of, quota, 0.0)
        taken = jnp.sum(taken, axis=1, keepdims=True)
        turn = (lax.broadcasted_iota(jnp.int32, (slots, 1), 0) % PICK).astype(f32)
        live = jnp.where(turn < taken, 1.0, 0.0)
        high = jnp.floor(picks * (1.0 / DIGIT))
        coded = jnp.where(lane == heads, high, jnp.where(lane == heads + 1, picks - high * DIGIT, live))
        sent_ref[:, 3 * width :] = jnp.where(
            (lane >= heads) & (lane < heads + 3), coded, gathered[:, 3 * width :]
        ).astype(bf16)


def tiled(*shape):
    return pl.BlockSpec(shape, lambda r, *_: (r,) + (0,) * (len(shape) - 1))


def project(tokens, picks, quota, gain, shift, joint, query_bias, value_bias, score_weight, tile=256):
    rows, width = tokens.shape
    slots = picks.shape[0] * picks.shape[1]
    channels = 3 * width + LANES
    steps = rows // tile
    S = jax.ShapeDtypeStruct
    return launch(
        functools.partial(project_kernel, steps),
        "project", 10, (steps,),
        [
            tiled(tile, width), same(*picks.shape), same(*quota.shape), same(width), same(width), same(*joint.shape),
            same(width), same(width), same(*score_weight.shape),
        ],
        [tiled(tile, width)] * 4 + [tiled(tile, LANES), same(WIN, channels), same(slots, channels)],
        [S((rows, width), bf16)] * 4 + [S((rows, LANES), bf16), S((WIN, channels), bf16), S((slots, channels), bf16)],
        [pltpu.VMEM((slots, channels), f32)], 24,
        (tokens, picks, quota, gain, shift, joint, query_bias, value_bias, score_weight),
    )


def far_positions(far_score, heads, place_rows, blocks):
    wide = far_score.astype(f32)
    slot = lax.broadcasted_iota(jnp.int32, (far_score.shape[0], 1), 0)
    at = (wide[:, heads : heads + 1] * DIGIT + wide[:, heads + 1 : heads + 2]).astype(jnp.int32)
    return jnp.where(
        wide[:, heads + 2 : heads + 3] > 0.5, (slot // PICK) * place_rows + at, 2 * place_rows * blocks
    )


def load_block(group, place_ref, k_ref, v_ref, score_ref, rim_refs, far_refs, keys, values, gate_ref, head_size):
    rows, width = k_ref.shape
    rim_k_ref, rim_v_ref, rim_score_ref = rim_refs
    far_score_ref = far_refs[2]
    slots = far_score_ref.shape[0]
    keys[0:WIN, :] = rim_k_ref[...]
    keys[WIN:, :] = k_ref[...]
    values[0:WIN, :] = rim_v_ref[...]
    values[WIN:, :] = v_ref[...]
    gates_into(gate_ref, group, place_ref[0], score_ref, rim_score_ref, far_score_ref, head_size, rows, slots)


def attend_kernel(
    heads, head_size, unroll, place_ref, q_ref, k_ref, v_ref, score_ref,
    rim_k_ref, rim_v_ref, rim_score_ref, far_k_ref, far_v_ref, far_score_ref,
    mixed_ref, total_ref, keys, values, gate_ref,
):
    group = pl.program_id(0)
    place = place_ref[0]
    rows, width = q_ref.shape
    slots = far_k_ref.shape[0]
    load_block(
        group, place_ref, k_ref, v_ref, score_ref, (rim_k_ref, rim_v_ref, rim_score_ref),
        (far_k_ref, far_v_ref, far_score_ref), keys, values, gate_ref, head_size,
    )
    near_ok = near_bias(width)
    far_pos = jnp.broadcast_to(far_positions(far_score_ref[...], heads, rows, slots // PICK), (slots, LANES))

    @pl.loop(0, rows // WIN, unroll=unroll)
    def _(i):
        at = pl.ds(pl.multiple_of(i * WIN, WIN), WIN)
        span = pl.ds(pl.multiple_of(i * WIN, WIN), 2 * WIN)
        keys_cat = jnp.concatenate([keys[span, :], far_k_ref[...]], axis=0)
        values_cat = jnp.concatenate([values[span, :], far_v_ref[...]], axis=0)
        stack = stack_heads(q_ref[at, :], head_size, 1.0 / math.sqrt(head_size))
        logit = tile_logits(i, keys_cat, stack, gate_ref, far_pos, place, rows, near_ok)
        top = jnp.max(logit, axis=0, keepdims=True)
        power = jnp.exp(logit - top)
        total = jnp.sum(power, axis=0, keepdims=True)
        prob = (power * (1.0 / total)).astype(bf16)
        total_ref[0, pl.ds(i, 1), :] = top + jnp.log(total)
        mixed_ref[at, :] = pick_heads(tn(prob, values_cat), head_size).astype(bf16)


def far_specs(slots, width, groups):
    return [
        pl.BlockSpec((slots, width), lambda g: (0, g)),
        pl.BlockSpec((slots, width), lambda g: (0, groups + g)),
        pl.BlockSpec((slots, LANES), lambda g: (0, 3 * groups * width // LANES)),
    ]


def attend(place, q, k, v, score, rim, far, heads, unroll=8):
    rows, model = q.shape
    slots = far.shape[0]
    width = PACK * WIN
    groups = model // width
    cols = pl.BlockSpec((rows, width), lambda g: (0, g))
    return launch(
        functools.partial(attend_kernel, heads, WIN, unroll),
        "attend", 12, (groups,),
        [pl.BlockSpec(memory_space=pltpu.SMEM), cols, cols, cols, pl.BlockSpec((rows, LANES), lambda g: (0, 0))]
        + far_specs(WIN, width, groups) + far_specs(slots, width, groups),
        [cols, pl.BlockSpec((1, rows // WIN, width), lambda g: (g, 0, 0))],
        [
            jax.ShapeDtypeStruct((rows, model), bf16),
            jax.ShapeDtypeStruct((groups, rows // WIN, width), f32),
        ],
        [
            pltpu.VMEM((WIN + rows, width), bf16),
            pltpu.VMEM((WIN + rows, width), bf16),
            pltpu.VMEM((WIN + rows + slots, width), f32),
        ],
        32, (place, q, k, v, score, rim, rim, rim, far, far, far),
    )


class Block:
    def __init__(self, groups, loaded, k_h, v_h, score_h, rim_h, far_h, score_ref, keys, values, model, rows):
        self.loads = loads = Moves(loaded)
        slots, width = far_h.shape[0], keys.shape[2]
        self.near, self.own, self.far = pl.ds(0, WIN), pl.ds(WIN, rows), pl.ds(WIN + rows, slots)
        scores = pl.ds(3 * model, LANES)
        self.first = [
            loads.add(source, target)
            for source, target in (
                (score_h, score_ref.at[self.own, :]), (rim_h.at[:, scores], score_ref.at[self.near, :]),
                (far_h.at[:, scores], score_ref.at[self.far, :]),
            )
        ]
        self.second = []
        for at, group in enumerate(groups):
            cols, value_cols = pl.ds(group * width, width), pl.ds(model + group * width, width)
            self.second.append(
                [
                    loads.add(source, target)
                    for source, target in (
                        (k_h.at[:, cols], keys.at[at, self.own, :]), (rim_h.at[:, cols], keys.at[at, self.near, :]),
                        (far_h.at[:, cols], keys.at[at, self.far, :]), (v_h.at[:, cols], values.at[at, self.own, :]),
                        (rim_h.at[:, value_cols], values.at[at, self.near, :]),
                        (far_h.at[:, value_cols], values.at[at, self.far, :]),
                    )
                ]
            )

    def add(self, at, source, target):
        self.second[at].append(self.loads.add(source, target))


def gates_of(gate, spread, place, gate_ref):
    gate_ref[...] = sum(nn(part, spread) for part in three_parts(gate))
    gate_ref[0:WIN, :] = jnp.where(place == 0, very_low, gate_ref[0:WIN, :])


def attend_back_kernel(
    heads, head_size, unroll, groups, last, place_ref, q_h, k_h, v_h, grad_h, total_ref, score_h, rim_h, far_h, normed_h,
    *refs,
):
    refs = list(refs)
    earlier = [refs.pop(0) for _ in range(5)] if groups[0] else []
    beside_refs = [refs.pop(0) for _ in range(2)] if groups[0] else []
    dq_h, dk_h, dv_h, ds_ref, rim_out, far_out, rim_ds, far_ds, send, keep = refs[:10]
    q_ref, grad_ref, score_ref, dq_ref, keys, values, gate_refs, all_dkeys, all_dvalues, all_dscore, normed = refs[10:21]
    loaded, stored = refs[21:]
    model = normed.shape[1]
    place = place_ref[0]
    _, rows, width = q_ref.shape
    slots = far_h.shape[0]
    block = Block(groups, loaded, k_h, v_h, score_h, rim_h, far_h, score_ref, keys, values, model, rows)
    near, own, far, loads = block.near, block.own, block.far, block.loads
    for g, group in enumerate(groups):
        cols = pl.ds(group * width, width)
        block.add(g, q_h.at[:, cols], q_ref.at[g])
        block.add(g, grad_h.at[:, cols], grad_ref.at[g])
    normed_cols = pl.ds(2 * model, model)
    third = [
        loads.add(source, target)
        for source, target in (
            (normed_h, normed.at[own, :]), (rim_h.at[:, normed_cols], normed.at[near, :]),
            (far_h.at[:, normed_cols], normed.at[far, :]),
        )
    ]
    loads.start(*range(len(loads.made)))
    for ref in (all_dkeys, all_dvalues, all_dscore):
        ref[...] = jnp.zeros_like(ref)
    loads.wait(*block.first)
    gate = jax.nn.log_sigmoid(score_ref[...].astype(f32))
    near_ok = near_bias(width)
    far_pos = jnp.broadcast_to(far_positions(score_ref[far, :], heads, rows, slots // PICK), (slots, LANES))
    stores = Moves(stored)
    mine = place % 2
    half = model // 2
    start = 0
    if beside_refs:
        start = beside_refs[0].shape[1]
        send[:, :start] = beside_refs[0][...]
        keep[:, :start] = beside_refs[1][...]
        for out, old in zip((rim_out, far_out), earlier[:2]):
            out[...] = old[...]
    for g, group in enumerate(groups):
        gate_ref, dkeys, dvalues, dscore = (ref.at[g] for ref in (gate_refs, all_dkeys, all_dvalues, all_dscore))
        gather = head_spread(group, head_size, width)
        gates_of(gate, gather, place, gate_ref)
        loads.wait(*block.second[g])

        @pl.loop(0, rows // WIN, unroll=unroll)
        def _(i):
            at = pl.ds(pl.multiple_of(i * WIN, WIN), WIN)
            after = pl.ds(pl.multiple_of(i * WIN + WIN, WIN), WIN)
            span = pl.ds(pl.multiple_of(i * WIN, WIN), 2 * WIN)
            keys_cat = jnp.concatenate([keys[g, span, :], keys[g, far, :]], axis=0)
            values_cat = jnp.concatenate([values[g, span, :], values[g, far, :]], axis=0)
            stack = stack_heads(q_ref[g, at, :], head_size, 1.0 / math.sqrt(head_size))
            grad_stack = stack_heads(grad_ref[g, at, :], head_size, 1.0)
            logit = tile_logits(i, keys_cat, stack, gate_ref, far_pos, place, rows, near_ok)
            prob = jnp.exp(logit - total_ref[group, pl.ds(i, 1), :])
            grad_prob = nt(values_cat, grad_stack)
            delta = jnp.sum(prob * grad_prob, axis=0, keepdims=True)
            grad_logit = prob * (grad_prob - delta)
            low = grad_logit.astype(bf16)
            dq = pick_heads(tn(low, keys_cat), head_size) * (1.0 / math.sqrt(head_size))
            dq_ref[g, at, :] = dq.astype(bf16)
            for ref, update in (
                (dkeys, nn(low, stack)),
                (dvalues, nn(prob.astype(bf16), grad_stack)),
                (dscore, grad_logit),
            ):
                ref[at, :] += update[:WIN]
                ref[after, :] = update[WIN : 2 * WIN]
                ref[far, :] += update[2 * WIN :]

        to = pl.ds(g * width, width)
        for source, target in ((dq_ref.at[g], dq_h), (dkeys.at[own, :], dk_h), (dvalues.at[own, :], dv_h)):
            stores.start(stores.add(source, target.at[:, to]))
        if g == 0:
            loads.wait(*third)
        joint = jnp.concatenate(
            [tn(normed[own, :], dq_ref[g])]
            + [tn(normed[...], ref[...].astype(bf16)) for ref in (dkeys, dvalues)],
            axis=1,
        ).astype(bf16)
        top, low = joint[:half], joint[half:]
        span = slice(start + 3 * width * g, start + 3 * width * (g + 1))
        send[:, span] = jnp.where(mine == 0, low, top)
        keep[:, span] = jnp.where(mine == 0, top, low)
        for out, part in ((rim_out, near), (far_out, far)):
            for base, ref in ((0, dkeys), (model, dvalues)):
                out[:, base + group * width : base + (group + 1) * width] = ref[part, :].astype(bf16)
        for number, (out_ref, part) in enumerate(((rim_ds, near), (far_ds, far), (ds_ref, own))):
            sums = dscore[part, :]
            high = sums.astype(bf16)
            rest = (sums - high.astype(f32)).astype(bf16)
            update = (nt(high, gather) + nt(rest, gather)) * jax.nn.sigmoid(-score_ref[part, :].astype(f32))
            if g:
                out_ref[...] += update
            else:
                out_ref[...] = update + earlier[2 + number][...] if earlier else update
    if last:
        rim_out[:, 2 * model :] = rim_ds[...].astype(bf16)
        far_out[:, 2 * model :] = far_ds[...].astype(bf16)
    stores.wait(*range(len(stores.made)))


def attend_back(place, q, k, v, grad, total, score, rim, far, normed, heads, groups, earlier, joined, after=(), unroll=8):
    rows, model = q.shape
    slots = far.shape[0]
    width = PACK * WIN
    count = len(groups)
    channels = 2 * model + LANES
    S = jax.ShapeDtypeStruct
    half = (model // 2, 3 * width * count + (joined[0].shape[1] if joined else 0))
    ext = WIN + rows + slots
    V = pltpu.VMEM
    out = launch(
        functools.partial(attend_back_kernel, heads, WIN, unroll, groups, groups[-1] == model // width - 1),
        "attend_back", 13 * count, (),
        [pl.BlockSpec(memory_space=pltpu.SMEM)] + [anywhere()] * 4 + [vmem()] + [anywhere()] * 4
        + [vmem()] * (len(earlier) + len(joined)),
        [anywhere()] * 3 + [vmem()] * 7,
        [
            S((rows, count * width), bf16), S((rows, count * width), f32), S((rows, count * width), f32),
            S((rows, LANES), f32), S((WIN, channels), bf16), S((slots, channels), bf16), S((WIN, LANES), f32),
            S((slots, LANES), f32),
        ] + [S(half, bf16)] * 2,
        [
            V((count, rows, width), bf16), V((count, rows, width), bf16), V((ext, LANES), bf16),
            V((count, rows, width), bf16), V((count, ext, width), bf16), V((count, ext, width), bf16),
        ] + [V((count, ext, width), f32)] * 4
        + [
            V((ext, model), bf16), pltpu.SemaphoreType.DMA((6 + 8 * count,)), pltpu.SemaphoreType.DMA((3 * count,)),
        ],
        32 if count == 1 else 44,
        (place, q, k, v, grad, total, score, rim, far, normed, *earlier, *joined), after,
    )
    dq, dk, dv, ds, rim_out, far_out, rim_ds, far_ds, send, keep, token = out
    return (dq, dk, dv), (rim_out, far_out, rim_ds, far_ds, ds), (send, keep), token


cubic = 0.044715
root = 0.7978845608028654


def feed_kernel(
    tile, pieces, block, mine_ref, mixed_h, tokens_h, cot_h, out_weight_h, expand_h, reduce_h, out_bias_ref, gain_ref,
    shift_ref, expand_bias_ref,
    resid_h, hidden_h, grad_pre_h, sums_ref, send_one, keep_one, send_two, keep_two,
    mixed, tokens, cot, out_weight, expand, reduce, resids, normed, hidden, grad_pre, one, two, loaded, stored,
):
    rows, width = cot.shape
    inner = expand.shape[1]
    span = inner // pieces
    steps = rows // tile
    mine = mine_ref[0]
    loads = Moves(loaded)
    first = [loads.add(*pair) for pair in ((mixed_h, mixed), (out_weight_h, out_weight), (tokens_h, tokens))]
    second = loads.add(cot_h, cot)
    parts = []
    for piece in range(pieces):
        at = pl.ds(piece * span, span)
        parts.append(
            (loads.add(expand_h.at[:, at], expand.at[:, at]), loads.add(reduce_h.at[at, :], reduce.at[at, :]))
        )
    loads.start(*range(len(loads.made)))

    def store(number, source, target):
        return pltpu.make_async_copy(source, target, stored.at[number])

    def tile_stores(step):
        here = rows_at(step, tile)
        return [
            store(3 * step + at, source.at[here, :], target.at[here, :])
            for at, (source, target) in enumerate(((resids, resid_h), (hidden, hidden_h), (grad_pre, grad_pre_h)))
        ]

    def feed_tile(step, leading):
        here = rows_at(step, tile)
        if leading:
            loads.wait(*first)
        resid = tokens[here, :].astype(f32) + nn(mixed[here, :], out_weight[...]) + row(out_bias_ref)
        resids[here, :] = resid
        unit, _ = normalise(resid)
        low = (unit * row(gain_ref) + row(shift_ref)).astype(bf16)
        normed[here, :] = low
        if leading:
            loads.wait(second)
        sums = []
        for piece in range(pieces):
            at = slice(piece * span, (piece + 1) * span)
            if leading:
                loads.wait(*parts[piece])
            pre = nn(low, expand[:, at]) + row(expand_bias_ref)[:, at]
            back = nt(cot[here, :], reduce[at, :])
            squared = pre * pre
            half = 0.5 + 0.5 * jnp.tanh(pre * (root + root * cubic * squared))
            active = pre * half
            slope = half + (active - active * half) * (2.0 * root + 6.0 * root * cubic * squared)
            hidden[here, at] = active.astype(bf16)
            grad = (back * slope).astype(bf16)
            grad_pre[here, at] = grad
            sums.append(column_sums(grad.astype(f32)))
        total = jnp.concatenate(sums, axis=0)
        if leading:
            sums_ref[...] = total
        else:
            sums_ref[...] += total
        for copy in tile_stores(step):
            copy.start()

    feed_tile(0, True)

    @pl.loop(1, steps)
    def _(step):
        feed_tile(step, False)

    base = 3 * steps
    count = inner // 2 // block
    half = width // 2

    def one_store(turn, j):
        here = rows_at(j, block)
        target = (send_one, keep_one)[turn]
        return store(base + turn * count + j, one.at[turn, here, :], target.at[here, :])

    def two_store(turn):
        return store(base + 2 * count + turn, two.at[turn], (send_two, keep_two)[turn])

    for turn in range(2):
        side_of = (1 - mine) if turn == 0 else mine

        @pl.loop(0, count)
        def _(j):
            one[turn, rows_at(j, block), :] = tn(hidden[:, rows_at(side_of * count + j, block)], cot[...]).astype(bf16)
            one_store(turn, j).start()

    for turn in range(2):
        side_of = (1 - mine) if turn == 0 else mine
        two[turn] = tn(normed[:, rows_at(side_of, half)], grad_pre[...]).astype(bf16)
        two_store(turn).start()

    @pl.loop(0, steps)
    def _(step):
        for copy in tile_stores(step):
            copy.wait()

    for turn in range(2):
        @pl.loop(0, count)
        def _(j):
            one_store(turn, j).wait()

        two_store(turn).wait()


def feed(
    mine, mixed, tokens, cot, out_weight, out_bias, gain, shift, expand, expand_bias, reduce, tile=1024, block=768,
):
    rows, width = tokens.shape
    inner = expand.shape[1]
    steps, pieces = rows // tile, inner // width
    S = jax.ShapeDtypeStruct
    B = pltpu.VMEM
    return launch(
        functools.partial(feed_kernel, tile, pieces, block),
        "feed", 33, (),
        [anywhere()] * 6 + [vmem()] * 4,
        [anywhere()] * 3 + [vmem()] + [anywhere()] * 4,
        [
            S((rows, width), f32), S((rows, inner), bf16), S((rows, inner), bf16), S((pieces, inner // pieces), f32),
            S((inner // 2, width), bf16), S((inner // 2, width), bf16),
            S((width // 2, inner), bf16), S((width // 2, inner), bf16),
        ],
        [
            B((rows, width), bf16), B((rows, width), bf16), B((rows, width), bf16), B((width, width), bf16),
            B((width, inner), bf16), B((inner, width), bf16), B((rows, width), f32), B((rows, width), bf16),
            B((rows, inner), bf16), B((rows, inner), bf16), B((2, inner // 2, width), bf16), B((2, width // 2, inner), bf16),
            pltpu.SemaphoreType.DMA((4 + 2 * pieces,)),
            pltpu.SemaphoreType.DMA((3 * steps + inner // block + 2,)),
        ],
        60, (mixed, tokens, cot, out_weight, expand, reduce, out_bias, gain, shift, expand_bias), (), (mine,),
    )


def feed_back_kernel(
    tile, pieces, mine_ref, grad_pre_h, resid_h, cot_h, mixed_h, expand_h, out_weight_h, gain_ref,
    grad_resid_h, grad_mixed_h, sums_ref, send_h, keep_h,
    grad_pre, resid, cot, mixed, expand, out_weight, grad_attn, grad_mixed, three, loaded, stored,
):
    rows, width = cot.shape
    inner = expand.shape[1]
    span = inner // pieces
    steps = rows // tile
    half = width // 2
    mine = mine_ref[0]
    loads = Moves(loaded)

    def tile_load(step):
        return [
            loads.add(source.at[rows_at(step, tile), :], target.at[rows_at(step, tile), :])
            for source, target in ((grad_pre_h, grad_pre), (resid_h, resid), (cot_h, cot))
        ]

    tiles = [tile_load(0)]
    weights = [
        loads.add(expand_h.at[:, pl.ds(piece * span, span)], expand.at[:, pl.ds(piece * span, span)])
        for piece in range(pieces)
    ]
    late = loads.add(out_weight_h, out_weight)
    tiles += [tile_load(step) for step in range(1, steps)]
    last = loads.add(mixed_h, mixed)
    loads.start(*range(len(loads.made)))
    stores = Moves(stored)
    sums = []

    def first_part(step):
        here = rows_at(step, tile)
        grad_normed = jnp.zeros((tile, width), f32)
        for piece in range(pieces):
            at = slice(piece * span, (piece + 1) * span)
            if step == 0:
                loads.wait(weights[piece])
            grad_normed = grad_normed + nt(grad_pre[here, at], expand[:, at])
        return grad_normed

    def second_part(step, grad_normed):
        here = rows_at(step, tile)
        wide = cot[here, :].astype(f32)
        unit, inverse = normalise(resid[here, :])
        grad_resid = wide + normalise_back(grad_normed, unit, inverse, row(gain_ref))
        resid[here, :] = grad_resid
        low = grad_resid.astype(bf16)
        grad_attn[here, :] = low
        grad_mixed[here, :] = nt(low, out_weight[...]).astype(bf16)
        sums.append(
            jnp.concatenate(
                [
                    column_sums(low.astype(f32)),
                    column_sums(grad_normed * unit),
                    column_sums(grad_normed),
                    column_sums(wide),
                ],
                axis=0,
            )
        )

    loads.wait(*tiles[0])
    before = first_part(0)
    loads.wait(late, *tiles[1])
    ahead = first_part(1)
    second_part(0, before)
    loads.wait(last, *[at for tile_loads in tiles[2:] for at in tile_loads])
    for step in range(2, steps + 1):
        before, ahead = ahead, first_part(step) if step < steps else None
        second_part(step - 1, before)
    sums_ref[...] = sum(sums)
    for step in range(steps):
        here = rows_at(step, tile)
        stores.start(
            stores.add(resid.at[here, :], grad_resid_h.at[here, :]),
            stores.add(grad_mixed.at[here, :], grad_mixed_h.at[here, :]),
        )
    for turn in range(2):
        side_of = (1 - mine) if turn == 0 else mine
        three[turn] = tn(mixed[:, rows_at(side_of, half)], grad_attn[...]).astype(bf16)
        stores.start(stores.add(three.at[turn], (send_h, keep_h)[turn]))
    stores.wait(*range(len(stores.made)))


def feed_back(mine, grad_pre, resid, cot, mixed, expand, out_weight, gain, tile=256, pieces=4):
    rows, width = resid.shape
    inner = expand.shape[1]
    steps = rows // tile
    S = jax.ShapeDtypeStruct
    B = pltpu.VMEM
    return launch(
        functools.partial(feed_back_kernel, tile, pieces), "feed_back", 12, (),
        [anywhere()] * 6 + [vmem()],
        [anywhere()] * 2 + [vmem()] + [anywhere()] * 2,
        [
            S((rows, width), f32), S((rows, width), bf16), S((4, width), f32),
            S((width // 2, width), bf16), S((width // 2, width), bf16),
        ],
        [
            B((rows, inner), bf16), B((rows, width), f32), B((rows, width), bf16), B((rows, width), bf16),
            B((width, inner), bf16), B((width, width), bf16), B((rows, width), bf16), B((rows, width), bf16),
            B((2, width // 2, width), bf16),
            pltpu.SemaphoreType.DMA((3 * steps + pieces + 2,)),
            pltpu.SemaphoreType.DMA((2 * steps + 2,)),
        ],
        44, (grad_pre, resid, cot, mixed, expand, out_weight, gain), (), (mine,),
    )


def finish_kernel(resid_ref, hidden_ref, reduce_ref, bias_ref, out_ref):
    out_ref[...] = (resid_ref[...] + nn(hidden_ref[...], reduce_ref[...]) + row(bias_ref)).astype(bf16)


def finish(resid, hidden, reduce, bias, after=(), tile=256):
    rows, width = resid.shape
    inner = reduce.shape[0]
    return launch(
        finish_kernel, "finish", 7, (rows // tile,),
        [tiled(tile, width), tiled(tile, inner), same(inner, width), same(width)],
        [tiled(tile, width)], [jax.ShapeDtypeStruct((rows, width), bf16)],
        [], 26, (resid, hidden, reduce, bias), after,
    )


def beside(refs):
    return jnp.concatenate([ref[...] for ref in refs], axis=1)


def join_kernel(
    steps, groups, tokens_ref, resid_ref, ds_ref, rim_ref, far_ref, picks_ref, gain_ref, shift_ref,
    joint_ref, score_weight_ref, sums_two_ref, expand_sums_ref, *refs,
):
    dq_refs, dk_refs, dv_refs = (refs[at * groups : (at + 1) * groups] for at in range(3))
    token_ref, small_ref = refs[3 * groups :]
    step = pl.program_id(0)
    tile, width = tokens_ref.shape
    heads = score_weight_ref.shape[0]
    unit, inverse = normalise(tokens_ref[...].astype(f32))
    gain = row(gain_ref)
    normed = (unit * gain + row(shift_ref)).astype(bf16)
    picks = spread_slots(picks_ref[...].astype(f32))
    row_of = lax.broadcasted_iota(jnp.int32, (picks.shape[0], tile), 1) + step * tile
    chosen = jnp.where(picks == row_of.astype(f32), 1.0, 0.0).astype(bf16)
    at_end = jnp.where(step == steps - 1, 1.0, 0.0)

    def whole(own, start):
        span = own.shape[1]
        total = own + tn(chosen, far_ref[:, start : start + span])
        rim = rim_ref[:, start : start + span].astype(f32) * at_end
        return jnp.concatenate([total[: tile - WIN], total[tile - WIN :] + rim], axis=0).astype(bf16)

    dq = beside(dq_refs)
    dk = whole(beside(dk_refs), 0)
    dv = whole(beside(dv_refs), width)
    ds = whole(ds_ref[...], 2 * width)
    grad_normed = (
        nt(dq, joint_ref[:, :width])
        + nt(dk, joint_ref[:, width : 2 * width])
        + nt(dv, joint_ref[:, 2 * width :])
        + nn(ds[:, :heads], score_weight_ref[...])
    )
    token_ref[...] = resid_ref[...] + normalise_back(grad_normed, unit, inverse, gain)
    sums = jnp.concatenate(
        [
            column_sums(grad_normed * unit),
            column_sums(grad_normed),
            column_sums(dq.astype(f32)),
            column_sums(dv.astype(f32)),
        ],
        axis=0,
    )
    score_grad = tn(ds, normed)[:heads]
    past = 8 + expand_sums_ref.shape[0]

    @pl.when(step == 0)
    def _():
        small_ref[0:4, :] = sums
        small_ref[4:8, :] = sums_two_ref[...]
        small_ref[8:past, :] = expand_sums_ref[...]
        small_ref[past : past + heads, :] = score_grad

    @pl.when(step > 0)
    def _():
        small_ref[0:4, :] += sums
        small_ref[past : past + heads, :] += score_grad


def join(
    tokens, resid, dqs, dks, dvs, ds, rim, far, picks, gain, shift, joint, score_weight, sums_two, expand_sums, after=(),
    tile=256,
):
    rows, width = tokens.shape
    heads = score_weight.shape[0]
    count = 8 + expand_sums.shape[0] + heads
    S = jax.ShapeDtypeStruct
    return launch(
        functools.partial(join_kernel, rows // tile, len(dqs)), "join", 14, (rows // tile,),
        [tiled(tile, width)] * 2 + [
            tiled(tile, LANES), same(*rim.shape), same(*far.shape), same(*picks.shape), same(width), same(width),
            same(*joint.shape), same(*score_weight.shape), same(*sums_two.shape), same(*expand_sums.shape),
        ] + [tiled(tile, part.shape[1]) for part in (*dqs, *dks, *dvs)],
        [tiled(tile, width), same(count, width)],
        [S((rows, width), f32), S((count, width), f32)],
        [], 28, (tokens, resid, ds, rim, far, picks, gain, shift, joint, score_weight, sums_two, expand_sums, *dqs, *dks, *dvs), after,
    )


def swap(value, axis, bit):
    count = lax.axis_size(axis)
    return lax.ppermute(value, axis, [(i, i ^ bit) for i in range(count)])


def side(axis, bit):
    return (lax.axis_index(axis) // bit) % 2


def axis_bits(axis):
    count, bits, bit = lax.axis_size(axis), [], 1
    while bit < count:
        bits.append((axis, bit))
        bit *= 2
    return bits


def woven(*lists):
    result = []
    for step in range(max(map(len, lists))):
        for items in lists:
            result += items[step : step + 1]
    return result


def orders():
    near, far = axis_bits("seq"), axis_bits("dp")
    first, rest = near[:1], near[1:]
    return (
        first + rest + far,
        first + woven(rest[::-1], far),
        first + woven(far, rest),
    )


def cut(value, pieces):
    return value.reshape(pieces, value.shape[0] // pieces, value.shape[1])


class Chain:
    def __init__(self, send, keep, order):
        self.order, self.level, self.down, self.held = order, 0, True, True
        half = 2 ** (len(order) - 1)
        self.send, self.keep = cut(send, half), cut(keep, half)
        self.mine = [side(*where).astype(jnp.int32) for where in order]

    def got(self):
        return swap(self.send, *self.order[self.level])


def added(one, two):
    return (one[...].astype(f32) + two[...].astype(f32)).astype(bf16)


class Total:
    def __init__(self, value, order):
        self.send, self.order, self.level = value, order, 0

    def got(self):
        return swap(self.send, *self.order[self.level])


def advance_kernel(plan, bits_ref, *refs):
    refs = list(refs)
    outs = refs[sum(4 if kind == "split" else 2 for kind in plan) :]
    for kind in plan:
        if kind == "split":
            for _ in range(2):
                outs.pop(0)[...] = added(refs.pop(0), refs.pop(0))
        elif kind == "sum":
            outs.pop(0)[...] = refs.pop(0)[...] + refs.pop(0)[...]
        elif kind == "close":
            outs.pop(0)[...] = added(refs.pop(0), refs.pop(0))
        else:
            out = outs.pop(0)
            for which in range(2):
                out[which] = refs.pop(0)[...]


def advance(chains, after=(), hold=False):
    held = []
    plan, operands, in_specs, out_specs, shapes, bits, free = [], [], [], [], [], [], []
    depth = len(chains[0].order)
    for chain in chains:
        if isinstance(chain, Total):
            plan.append("sum")
            continue
        last = chain.down and chain.level == depth - 1
        plan.append("close" if last else "split" if chain.down else "stack")
    sizes = [chain.send.shape[0] // (2 if kind == "split" else 1) for chain, kind in zip(chains, plan)]
    steps = min([4] + [size for size, kind in zip(sizes, plan) if kind != "sum"])
    S = jax.ShapeDtypeStruct

    def half_of(which, other, block, tail):
        def index(g, bits_ref):
            mine = bits_ref[which]
            return ((1 - mine if other else mine) * steps + g, 0, 0)

        return pl.BlockSpec((block,) + tail, index)

    for chain, kind, size in zip(chains, plan, sizes):
        got, tail = chain.got(), chain.send.shape[1:]
        block = size // steps
        if kind == "sum":
            free += [len(operands), len(operands) + 1]
            operands += [chain.send, got]
            in_specs += [same(*chain.send.shape)] * 2
            out_specs += [same(*chain.send.shape)]
            shapes += [S(chain.send.shape, f32)]
        elif kind == "split":
            which = len(bits)
            bits.append(chain.mine[chain.level + 1])
            places = len(operands)
            free += [places + 1, places + 3] if chain.held else range(places, places + 4)
            chain.held = hold
            held += [len(shapes) + 1] if hold else []
            for other in (True, False):
                operands += [chain.keep, got]
                in_specs += [half_of(which, other, block, tail)] * 2
            out_specs += [tiled(block, *tail)] * 2
            shapes += [S((size,) + tail, bf16)] * 2
        elif kind == "close":
            free += [len(operands) + 1] if chain.held else [len(operands), len(operands) + 1]
            operands += [chain.keep, got]
            in_specs += [tiled(block, *tail)] * 2
            out_specs += [tiled(block, *tail)]
            shapes += [S((size,) + tail, bf16)]
        else:
            free += [len(operands), len(operands) + 1]
            operands += [chain.send, got]
            in_specs += [tiled(block, *tail)] * 2
            out_specs += [pl.BlockSpec((2, block) + tail, lambda g, *_: (0, g, 0, 0))]
            shapes += [S((2, size) + tail, bf16)]
    bits = jnp.stack(bits) if bits else jnp.zeros((1,), jnp.int32)
    outs = launch(
        functools.partial(advance_kernel, plan), "advance", 2, (steps,), in_specs, out_specs, shapes, [], 20, operands,
        after, (bits,), free, None, held,
    )
    for chain, kind in zip(chains, plan):
        if kind == "split":
            chain.send, chain.keep = outs[:2]
            chain.level += 1
            outs = outs[2:]
        elif kind == "sum":
            chain.send = outs[0]
            chain.level += 1
            outs = outs[1:]
        else:
            chain.send = outs[0].reshape((-1,) + chain.send.shape[1:])
            outs = outs[1:]
            if kind == "close":
                chain.down = False
            else:
                chain.level -= 1
    return outs[0]


def finished(chain):
    if isinstance(chain, Total):
        return chain.level == len(chain.order)
    return not chain.down and chain.level == 0


def ends(chain):
    return chain.send, chain.got()


def own_place(order):
    place = 0
    for axis, bit in order:
        place = place * 2 + side(axis, bit)
    return place.astype(jnp.int32).reshape(1)


def widen_half(own, chain, half_of, into=(), after=()):
    value, other = half_of
    half, size, n = value.shape
    count, group = 2 * half, 4

    def side_of(own_ref):
        mine = own_ref[0] // half
        return 1 - mine if other else mine

    def kernel(own_ref, value_ref, *refs):
        out_ref = refs[-1]
        for i in range(group):
            out_ref[i] = value_ref[jnp.bitwise_xor(own_ref[0] % group, i)].astype(f32)

    out, token = launch(
        kernel, "widen", 4, (half // group,),
        [pl.BlockSpec((group, size, n), lambda s, own_ref: (jnp.bitwise_xor(own_ref[0] % half // group, s), 0, 0))]
        + [anywhere()] * len(into),
        [pl.BlockSpec((group, size, n), lambda s, own_ref: (side_of(own_ref) * (half // group) + s, 0, 0))],
        [jax.ShapeDtypeStruct((count, size, n), f32)],
        [], 24, (value, *into), after, (own,), (0,), {2: 0} if into else None,
    )
    return out, token


def widen_joint_half(owns, values, other, into=(), after=()):
    half, size, n = values[0].shape
    count, group, model, width = 2 * half, 4, n // 2, PACK * WIN

    def side_of(own_ref):
        mine = own_ref[0] // half
        return 1 - mine if other else mine

    def kernel(own_one_ref, own_two_ref, one_ref, two_ref, *refs):
        joint_ref, first_ref = refs[-2:]
        for i in range(group):
            one = one_ref[jnp.bitwise_xor(own_one_ref[0] % group, i)].astype(f32)
            two = two_ref[jnp.bitwise_xor(own_two_ref[0] % group, i)].astype(f32)
            first_ref[i] = two[:, :model]
            for piece, start, g in ((one, 0, 0), (one, 3 * width, 1), (two, model, 2)):
                for kind in range(3):
                    to = kind * model + g * width
                    joint_ref[i, :, to : to + width] = piece[:, start + kind * width : start + (kind + 1) * width]

    def read(which):
        def index(s, *own_refs):
            return (jnp.bitwise_xor(own_refs[which][0] % half // group, s), 0, 0)

        return pl.BlockSpec((group, size, n), index)

    def write(columns):
        return pl.BlockSpec((group, size, columns), lambda s, own_ref, _: (side_of(own_ref) * (half // group) + s, 0, 0))

    S = jax.ShapeDtypeStruct
    joint, first, token = launch(
        kernel, "widen_joint", 4, (half // group,),
        [read(0), read(1)] + [anywhere()] * len(into), [write(3 * model), write(model)],
        [S((count, size, 3 * model), f32), S((count, size, model), f32)],
        [], 24, (*values, *into), after, tuple(owns), (0, 1), {4: 0, 5: 1} if into else None,
    )
    return (joint, first), token


def per_device(
    tokens, cotangent, first_gain, first_shift, joint_weight, query_bias, value_bias, score_weight, out_weight, out_bias,
    second_gain, second_shift, expand_weight, expand_bias, reduce_weight, reduce_bias, picks, quota,
):
    rows, width = tokens.shape[1:]
    heads = score_weight.shape[1]
    inner = expand_weight.shape[1]
    blocks = lax.axis_size("seq")
    slots = blocks * PICK
    here = lax.axis_index("seq").astype(jnp.int32).reshape(1)
    first, second, _ = orders()
    mine = side(*first[0]).astype(jnp.int32).reshape(1)
    inputs, grad_out = tokens[0], cotangent[0]
    chosen, turned = picks[0, 0], score_weight.T
    normed, q, k, v, score, rim_sent, sent, _ = project(
        inputs, chosen, quota[0], first_gain, first_shift, joint_weight, query_bias, value_bias, turned
    )
    rim = passed_along(rim_sent, "seq", 1)
    far = lax.all_to_all(
        sent.reshape(blocks, PICK, -1), "seq", split_axis=0, concat_axis=0, tiled=True
    ).reshape(slots, -1)
    mixed, total, _ = attend(here, q, k, v, score, rim, far, heads)
    resid, hidden, grad_pre, expand_sums, *halves, _ = feed(
        mine, mixed, inputs, grad_out, out_weight, out_bias, second_gain, second_shift, expand_weight, expand_bias,
        reduce_weight,
    )
    reduced, expanded = Chain(*halves[:2], first), Chain(*halves[2:], second)
    grad_resid, grad_mixed, sums_two, *out_halves, stage = feed_back(
        mine, grad_pre, resid, grad_out, mixed, expand_weight, out_weight, second_gain
    )
    big = [reduced, expanded]
    back = functools.partial(attend_back, here, q, k, v, grad_mixed, total, score, rim, far, normed, heads)
    stage = advance(big, (stage,))
    grads_one, carried, joined, stage = back((0, 1), (), (), (stage,))
    one = Chain(*joined, first)
    stage = advance(big, (stage,), True)
    grads_two, carried, joined, stage = back((2,), carried, tuple(out_halves), (stage,))
    two = Chain(*joined, second)
    rim_grad, far_grad, _, _, ds = carried
    rim_back = passed_along(rim_grad, "seq", -1)
    far_back = lax.all_to_all(
        far_grad.reshape(blocks, PICK, -1), "seq", split_axis=0, concat_axis=0, tiled=True
    ).reshape(slots, -1)
    dqs, dks, dvs = zip(grads_one, grads_two)
    stage = advance(big + [one], (stage,), True)
    stage = advance(big + [two], (stage,), True)
    token_grad, small, stage = join(
        inputs, grad_resid, dqs, dks, dvs, ds, rim_back, far_back, chosen, first_gain, first_shift, joint_weight, turned,
        sums_two, expand_sums, (stage,),
    )
    small = Total(small, first)
    late = [one, two]
    stage = advance(big + late, (stage,))
    layer_out, stage = finish(resid, hidden, reduce_weight, reduce_bias, (stage,))
    for chains in (big + late, big + late, big + late + [small], late + [small], late + [small]):
        stage = advance([chain for chain in chains if not finished(chain)], (stage,))
    while not finished(reduced):
        stage = advance([chain for chain in big + late + [small] if not finished(chain)], (stage,))
    own_first, own_second = own_place(first), own_place(second)
    halves_one, halves_two = ends(reduced), ends(expanded)
    reduce_weight_grad, stage = widen_half(own_first, reduced, (halves_one[0], False), (), (stage,))
    expand_weight_grad, stage = widen_half(own_second, expanded, (halves_two[0], False), (), (stage,))
    reduce_weight_grad, stage = widen_half(own_first, reduced, (halves_one[1], True), (reduce_weight_grad,), (stage,))
    expand_weight_grad, stage = widen_half(own_second, expanded, (halves_two[1], True), (expand_weight_grad,), (stage,))
    while not (finished(one) and finished(two)):
        stage = advance([chain for chain in late + [small] if not finished(chain)], (stage,))
    while not finished(small):
        stage = advance([small], (stage,))
    halves_one, halves_two = ends(one), ends(two)
    owns = (own_first, own_second)
    both, stage = widen_joint_half(owns, (halves_one[0], halves_two[0]), False, (), (stage,))
    both, stage = widen_joint_half(owns, (halves_one[1], halves_two[1]), True, both, (stage,))
    reduce_weight_grad = reduce_weight_grad.reshape(inner, width)
    expand_weight_grad = expand_weight_grad.reshape(width, inner)
    joint_weight_grad, out_weight_grad = both[0].reshape(width, 3 * width), both[1].reshape(width, width)
    small = small.send
    gain_one, shift_one, query_sum, value_sum, out_sum, gain_two, shift_two, reduce_sum = (small[i] for i in range(8))
    past = 8 + inner // width
    return (
        layer_out[None],
        token_grad[None],
        gain_one,
        shift_one,
        joint_weight_grad,
        query_sum,
        value_sum,
        small[past : past + heads].T,
        out_weight_grad,
        out_sum,
        gain_two,
        shift_two,
        expand_weight_grad,
        small[8:past].reshape(inner),
        reduce_weight_grad,
        reduce_sum,
    )


def solution(mesh):
    placed = (
        P("dp", "seq", None),
        P("dp", "seq", None),
        P(),
        P(),
        P(),
        P(),
        P(),
        P(),
        P(),
        P(),
        P(),
        P(),
        P(),
        P(),
        P(),
        P(),
        P("dp", "seq", None, None),
        P("dp", "seq", None),
    )
    return jax.shard_map(
        per_device,
        mesh=mesh,
        in_specs=placed,
        out_specs=(
            P("dp", "seq", None),
            P("dp", "seq", None),
            P(),
            P(),
            P(),
            P(),
            P(),
            P(),
            P(),
            P(),
            P(),
            P(),
            P(),
            P(),
            P(),
            P(),
        ),
        check_vma=False,
    )
```
